32 devices in a mesh: dp: 4 (over y, x), expert: 8 (over z, core).
Axes of the slice: x: 2, y: 2, z: 4, core: 2. Of those that a mesh axis runs over, the one named last changes fastest.
Arguments:
- grad_rows: bfloat16 [4, 8, 5120, 512], P('dp', None, 'expert'), may hold values from -80 to 80
- momentum_rows: bfloat16 [4, 8, 5120, 512], P('dp', None, 'expert'), may hold values from -1.796875 to 1.796875
- weight_rows: bfloat16 [4, 8, 5120, 512], P('dp', None, 'expert'), may hold values from -0.099609375 to 0.099609375
- row_counts: int32 [4, 8, 8], P('dp', None, 'expert'), may hold values from 1 to 640, 4096 in all within a row
- logit_peaks: bfloat16 [4, 8, 8, 64], P('dp', 'expert'), may hold values from 0 to 300, as said below
Outputs:
- update_rows: bfloat16 [4, 8, 5120, 512], P('dp', None, 'expert')
- weights_out: bfloat16 [4, 8, 5120, 512], P('dp', None, 'expert')
The draws below stay inside these ranges and needn't reach their ends.
Inputs may be any that keep to these rules, and one draw needn't show every extreme that they name: row_counts[d, m, :] sums to 4096, and its largest entry is 640. `logit_peaks`: positive.
All inputs are finite; a program needn't handle non-finite values. No bound on the sum of `row_counts` on one device may be relied on, other than what follows from the above.
Results may differ from the reference program's by a relative error of at most 0.012.
The reference program's roundings to bfloat16 on the way count: a program that leaves them out, or rounds other values in their place, can miss the bound.
Values may be sent and summed in bfloat16 or wider, within the bound.
No kernel may reach another device: no remote copies, remote signals or barrier semaphores. Data moves between devices by JAX's collectives and lax.ppermute only.
A program may use at most 128 MiB of HBM per device.

```python
import math
import jax
import jax.numpy as jnp
import numpy as np
from jax import lax

KV_RANK = 512
HEADS = 64
NOPE = 128
VDIM = 128
NS_ITERS = 5
KV_ROWS = 16384
MATS = 8
ROWS_DP = 4096
CAP = 640
N_DP = 4
N_EXPERT = 8


clip_limit = 100.0


def draw_grad_rows(key, part):
    key = jax.random.fold_in(key, 11)
    first, second, third, fourth = jax.random.split(key, 4)
    shape = (N_DP, MATS, N_EXPERT * CAP, KV_RANK)
    row_scale = jnp.exp(jax.random.uniform(second, (N_DP, MATS, N_EXPERT * CAP, 1), jnp.float32) * math.log(10.0))
    col_scale = jnp.exp(jax.random.uniform(third, (1, MATS, 1, KV_RANK), jnp.float32) * math.log(10.0))
    block_place = jnp.arange(N_DP, dtype=jnp.float32)[:, None, None, None] / max(N_DP - 1, 1)
    block_scale = jnp.exp(block_place * math.log(4.0))
    values = jnp.clip(jax.random.normal(first, shape, jnp.float32), -6.0, 6.0) * row_scale * col_scale * block_scale
    return (0.025 * values).astype(jnp.bfloat16)


def draw_logit_peaks(key, part):
    key = jax.random.fold_in(key, 23)
    first, second, third = jax.random.split(key, 3)
    shape = (N_DP, N_EXPERT, MATS, HEADS)
    spread = jnp.exp(jax.random.uniform(first, (MATS, HEADS), jnp.float32, math.log(0.3), math.log(3.0)))
    hottest = jax.random.randint(second, (MATS, HEADS), 0, N_DP * N_EXPERT)
    device = lax_device(shape)
    lower = jax.random.uniform(third, shape, jnp.float32, 0.2, 0.6)
    values = clip_limit * spread * jnp.where(device == hottest, 1.0, lower)
    return values.astype(jnp.bfloat16)


def lax_device(shape):
    first_axis = jnp.arange(shape[0], dtype=jnp.int32)[:, None, None, None]
    second_axis = jnp.arange(shape[1], dtype=jnp.int32)[None, :, None, None]
    return jnp.broadcast_to(first_axis * shape[1] + second_axis, shape)


def shard_levels(stream_key, shape, cuts, least, top_value):
    loudness, own = 1.0, jax.random.fold_in(stream_key, 6)
    for position, blocks in cuts:
        draws = jnp.exp(jax.random.uniform(jax.random.fold_in(own, position), (blocks,), jnp.float32, least / len(cuts), top_value / len(cuts)))
        loudness = loudness * jnp.repeat(draws, shape[position] // blocks).reshape([-1 if axis == position else 1 for axis in range(len(shape))])
    return loudness


def profile(number_of, total, bound, skew):
    loads = [(1 << 20) // math.isqrt(rank ** skew) + 1 for rank in range(2, number_of + 1)]
    rest, given = total - bound - (number_of - 1), [1] * (number_of - 1)
    while rest > 0:
        movable = [i for i in range(number_of - 1) if given[i] < bound]
        mass, left = sum([loads[i] for i in movable]), rest
        for i in movable:
            more = min(bound - given[i], max(1, left * loads[i] // mass), rest)
            given[i] = given[i] + more
            rest = rest - more
    return np.array([bound] + given)


def ragged(own_key, count, total, bound, slope):
    if count == 2:
        one = jax.random.randint(own_key, (), max(1, total - bound), min(bound, total - 1) + 1)
        return jnp.stack([one, total - one])
    tallies = jnp.asarray(profile(count, total, bound, slope), jnp.int32)
    pairs = (count - 1) // 2
    donor, receiver = tallies[1:1 + 2 * pairs:2], tallies[2:2 + 2 * pairs:2]
    slack = jnp.minimum(donor - 1, bound - receiver)
    shifted = jax.random.randint(jax.random.fold_in(own_key, 1), (pairs,), 0, 1 << 20) % (slack + 1)
    tallies = tallies.at[1:1 + 2 * pairs:2].set(donor - shifted).at[2:2 + 2 * pairs:2].set(receiver + shifted)
    return tallies[jax.random.permutation(jax.random.fold_in(own_key, 2), count)]


def noise(stream_key, extent, width, most, pieces=(), held_as=jnp.bfloat16):
    values = width * jax.random.normal(stream_key, extent, jnp.float32)
    if pieces:
        values = values * shard_levels(stream_key, extent, pieces, -0.22, 0.18)
    return jnp.clip(values, -most, most).astype(held_as)


def setup_inputs(seed: int = 0) -> dict:
    splits = jax.random.split(jax.random.key(seed), 6)
    return {
        "grad_rows": draw_grad_rows(jax.random.fold_in(splits[5], 71), 0),
        "momentum_rows": noise(splits[1], (N_DP, MATS, N_EXPERT * CAP, KV_RANK), 0.3, 1.796875, ((0, 4), (2, 8))),
        "weight_rows": noise(splits[2], (N_DP, MATS, N_EXPERT * CAP, KV_RANK), 0.02, 0.099609375, ((0, 4), (2, 8))),
        "row_counts": jax.vmap(lambda own: ragged(own, N_EXPERT, ROWS_DP, CAP, 2))(jax.random.split(splits[3], N_DP * MATS)).reshape((N_DP, MATS, N_EXPERT)).astype(jnp.int32),
        "logit_peaks": draw_logit_peaks(jax.random.fold_in(splits[5], 71), 0),
    }


momentum_coef = 0.95
learn_rate = 0.02
decay_rate = 0.1
clip_limit = 100.0
coef_first = 3.4445
coef_second = -4.775
coef_third = 2.0315

def orthogonal(matrix):
    squares = jnp.sum(jnp.square(matrix.astype(jnp.float32)))
    iterate = (matrix.astype(jnp.float32) / (jnp.sqrt(squares) + 1e-07)).astype(jnp.bfloat16)
    for repeat in range(NS_ITERS):
        gram_sum = lax.dot_general(iterate, iterate, (((0,), (0,)), ((), ())), preferred_element_type=jnp.float32)
        square = jnp.dot(gram_sum, gram_sum, precision=lax.Precision.HIGHEST)
        mixing = (coef_second * gram_sum + coef_third * square).astype(jnp.bfloat16)
        iterate = (coef_first * iterate.astype(jnp.float32) + jnp.dot(iterate, mixing, preferred_element_type=jnp.float32)).astype(jnp.bfloat16)
    return iterate

def reference(grad_rows, momentum_rows, weight_rows, row_counts, logit_peaks):
    dp_count, layers, slots_all, features = grad_rows.shape
    groups = row_counts.shape[2]
    capacity = slots_all // groups
    rows_dp = KV_ROWS // dp_count
    head_rows = NOPE + VDIM
    rms_scale = 0.2 * math.sqrt(max(KV_ROWS, KV_RANK))
    before = jnp.cumsum(row_counts, axis=2).astype(jnp.int32) - row_counts
    slot_iota = jnp.arange(capacity, dtype=jnp.int32)
    dp_iota = jnp.arange(dp_count, dtype=jnp.int32)
    row_index = (dp_iota[:, None, None, None] * rows_dp + before[..., None] + slot_iota).reshape(dp_count, layers, slots_all)
    slot_live = (slot_iota < row_counts[..., None]).reshape(dp_count, layers, slots_all)
    peaks = lax.optimization_barrier(jnp.max(logit_peaks.astype(jnp.float32), axis=(0, 1)))
    factor = jnp.sqrt(jnp.minimum(1.0, clip_limit / peaks))

    def per_layer(inputs):
        gradient, momentum, weight, row_layer, live_layer, factor_layer = inputs
        gradient = gradient.astype(jnp.float32)
        velocity = momentum_coef * momentum.astype(jnp.float32) + gradient
        nesterov = jnp.where(live_layer[..., None], gradient + momentum_coef * velocity, 0.0).astype(jnp.bfloat16)
        target = jnp.where(live_layer, row_layer, KV_ROWS).reshape(-1).astype(jnp.int32)
        assembled = jnp.zeros((KV_ROWS + 1, features), jnp.float32).at[target].add(nesterov.reshape(-1, features).astype(jnp.float32))
        result = orthogonal(assembled[:KV_ROWS].astype(jnp.bfloat16))
        picked = jnp.take(result, jnp.minimum(row_layer, KV_ROWS - 1).reshape(-1).astype(jnp.int32), axis=0).reshape(nesterov.shape)
        updated = rms_scale * picked.astype(jnp.float32)
        head_index = jnp.minimum(row_layer // head_rows, HEADS - 1).astype(jnp.int32)
        row_factor = jnp.where(row_layer % head_rows < NOPE, factor_layer[head_index], 1.0)
        retained = 1.0 - learn_rate * decay_rate
        new_weight = row_factor[..., None] * (weight.astype(jnp.float32) * retained - learn_rate * updated)
        update_out = jnp.where(live_layer[..., None], updated, 0.0).astype(jnp.bfloat16)
        weight_out = jnp.where(live_layer[..., None], new_weight, 0.0).astype(jnp.bfloat16)
        return (update_out, weight_out)
    update_layers, weight_layers = lax.map(per_layer, (jnp.moveaxis(grad_rows, 1, 0), jnp.moveaxis(momentum_rows, 1, 0), jnp.moveaxis(weight_rows, 1, 0), jnp.moveaxis(row_index, 1, 0), jnp.moveaxis(slot_live, 1, 0), factor))
    return (jnp.moveaxis(update_layers, 0, 1), jnp.moveaxis(weight_layers, 0, 1))
```

```python
import functools
import math

import jax
import jax.numpy as jnp
from jax import lax
from jax.experimental import pallas as pl
from jax.experimental.pallas import tpu as pltpu
from jax.sharding import PartitionSpec as P

KV_RANK = 512
NOPE = 128
VDIM = 128
NS_ITERS = 5
KV_ROWS = 16384

momentum_coef = 0.95
learn_rate = 0.02
decay_rate = 0.1
clip_limit = 100.0
coef_first = 3.4445
coef_second = -4.775
coef_third = 2.0315

f32 = jnp.float32
bf16 = jnp.bfloat16

LANES = 128
BLOCKS = KV_RANK // LANES
PAIRS = [(i, j) for i in range(BLOCKS) for j in range(i, BLOCKS)]
HALF = len(PAIRS) // 2
AUX = 8
HEAD_A = AUX + HALF * LANES
ROWS = AUX + len(PAIRS) * LANES
TAIL_B = ROWS - HEAD_A
AUX_P = 32
ROWS_P = AUX_P + len(PAIRS) * LANES
HALF_P = ROWS_P // 2


def params(**more):
    return pltpu.CompilerParams(vmem_limit_bytes=40 * 1024 * 1024, **more)


def whole(shape):
    return pl.BlockSpec(shape, lambda *_: (0,) * len(shape))


def gram_kernel(ids, counts, grad_ref, mom_ref, aux_ref, nes_ref, gram_ref):
    count = counts[ids[pl.program_id(0)]]
    gradient = grad_ref[0].astype(f32)
    velocity = momentum_coef * mom_ref[0].astype(f32) + gradient
    nesterov = gradient + momentum_coef * velocity
    slot = lax.broadcasted_iota(jnp.int32, nesterov.shape, 0)
    rows = jnp.where(slot < count, nesterov, 0.0).astype(bf16)
    nes_ref[0] = rows
    gram_ref[0, 0:AUX, :] = aux_ref[0]
    half = KV_RANK // 2
    dims = (((0,), (0,)), ((), ()))
    upper = lax.dot_general(rows[:, :half], rows, dims, preferred_element_type=f32)
    lower = lax.dot_general(rows[:, half:], rows[:, half:], dims, preferred_element_type=f32)
    for place, (i, j) in enumerate(PAIRS):
        at = AUX + place * LANES
        if i < 2:
            block = upper[i * LANES : (i + 1) * LANES, j * LANES : (j + 1) * LANES]
        else:
            block = lower[(i - 2) * LANES : (i - 1) * LANES, (j - 2) * LANES : (j - 1) * LANES]
        gram_ref[0, at : at + LANES, :] = block


def gram_parts(ids, counts, grad, mom, aux):
    number = ids.shape[0]
    capacity, features = grad.shape[1:]
    picked = lambda i, ids, counts: (ids[i], 0, 0)
    here = lambda i, ids, counts: (i, 0, 0)
    return pl.pallas_call(
        gram_kernel,
        grid_spec=pltpu.PrefetchScalarGridSpec(
            num_scalar_prefetch=2,
            grid=(number,),
            in_specs=[
                pl.BlockSpec((1, capacity, features), picked),
                pl.BlockSpec((1, capacity, features), picked),
                pl.BlockSpec((1, AUX, LANES), picked),
            ],
            out_specs=[
                pl.BlockSpec((1, capacity, features), here),
                pl.BlockSpec((1, ROWS, LANES), here),
            ],
        ),
        out_shape=[
            jax.ShapeDtypeStruct((number, capacity, features), bf16),
            jax.ShapeDtypeStruct((number, ROWS, LANES), f32),
        ],
        compiler_params=params(),
        cost_estimate=pl.CostEstimate(
            flops=number * capacity * features * features * 2,
            bytes_accessed=number * (capacity * features * 6 + ROWS * LANES * 4),
            transcendentals=0,
        ),
        name="gram_parts",
    )(ids, counts, grad, mom, aux)


def joined(first, second):
    row = lax.broadcasted_iota(jnp.int32, first.shape, 0)
    return jnp.where(row == 0, jnp.maximum(first, second), first + second)


def local_call(kernel, out_shapes, name, *args):
    size = sum(math.prod(x.shape) * x.dtype.itemsize for x in list(args) + list(out_shapes))
    return pl.pallas_call(
        kernel,
        in_specs=[pl.BlockSpec(memory_space=pltpu.VMEM)] * len(args),
        out_specs=[pl.BlockSpec(memory_space=pltpu.VMEM)] * len(out_shapes),
        out_shape=list(out_shapes),
        compiler_params=params(),
        cost_estimate=pl.CostEstimate(flops=size // 4, bytes_accessed=size, transcendentals=0),
        name=name,
    )(*args)


def split_kernel(kept, arrived, first_ref, second_ref):
    first_ref[...] = joined(kept[0, :HEAD_A], arrived[0, :HEAD_A])
    second_ref[...] = kept[0, HEAD_A:] + arrived[0, HEAD_A:]


def relay_kernel(kept, arrived, from_left, from_right, up_ref, down_ref, own_ref):
    up = kept[0, :HEAD_A], arrived[0, :HEAD_A]
    up_ref[:HEAD_A] = joined(joined(*up), from_left[...])
    up_ref[HEAD_A:] = kept[0, HEAD_A:] + arrived[0, HEAD_A:]
    down_ref[:HEAD_A] = joined(kept[1, :HEAD_A], arrived[1, :HEAD_A])
    down_ref[HEAD_A:] = kept[1, HEAD_A:] + arrived[1, HEAD_A:] + from_right[...]
    own_ref[...] = joined(kept[2], arrived[2])


def pass_kernel(kept_up, kept_down, from_left, from_right, up_ref, down_ref):
    up_ref[...] = joined(kept_up[...], from_left[...])
    down_ref[...] = joined(kept_down[...], from_right[...])


def own_kernel(own, from_left, from_right, first_ref, second_ref):
    first_ref[...] = joined(joined(own[:HEAD_A], from_left[:HEAD_A]), from_right[:HEAD_A])
    second_ref[...] = own[HEAD_A:] + from_left[HEAD_A:] + from_right[HEAD_A:]


def pair_kernel(first, first_other, second, second_other, first_ref, second_ref):
    first_ref[...] = joined(first[...], first_other[...])
    second_ref[...] = second[...] + second_other[...]


def mm(x, y):
    return jnp.dot(x, y, preferred_element_type=f32)


def parts_of(x):
    high = x.astype(bf16)
    return high, (x - high.astype(f32)).astype(bf16)


def iterate_kernel(first, first_other, second, second_other, out_ref, gram_ref):
    head = joined(first[...], first_other[...])
    tail = second[...] + second_other[...]
    row = lax.broadcasted_iota(jnp.int32, (LANES, LANES), 0)
    col = lax.broadcasted_iota(jnp.int32, (LANES, LANES), 1)
    eye_block = (row == col).astype(f32)
    squares = jnp.zeros((1, LANES), f32)
    for place, (i, j) in enumerate(PAIRS):
        if place < HALF:
            block = head[AUX + place * LANES : AUX + (place + 1) * LANES]
        else:
            block = tail[(place - HALF) * LANES : (place - HALF + 1) * LANES]
        gram_ref[i * LANES : (i + 1) * LANES, j * LANES : (j + 1) * LANES] = block
        if i != j:
            gram_ref[j * LANES : (j + 1) * LANES, i * LANES : (i + 1) * LANES] = block.T
        else:
            squares = squares + jnp.sum(block * eye_block, axis=0, keepdims=True)
    squares = jnp.sum(squares, axis=1, keepdims=True)
    inverse = 1.0 / (jnp.sqrt(squares) + 1e-07)
    gram = gram_ref[...] * inverse * inverse
    full_row = lax.broadcasted_iota(jnp.int32, (KV_RANK, KV_RANK), 0)
    full_col = lax.broadcasted_iota(jnp.int32, (KV_RANK, KV_RANK), 1)
    product = None
    for repeat in range(NS_ITERS):
        high, low = parts_of(gram)
        square = mm(high, high) + (mm(high, low) + mm(low, high))
        mixing = (coef_second * gram + coef_third * square).astype(bf16)
        if product is None:
            product = jnp.where(full_row == full_col, coef_first, 0.0) + mixing.astype(f32)
        else:
            product_high, product_low = parts_of(product)
            product = coef_first * product + (mm(product_high, mixing) + mm(product_low, mixing))
        if repeat < NS_ITERS - 1:
            half = coef_first * gram + (mm(high, mixing) + mm(low, mixing))
            half_high, half_low = parts_of(half)
            gram = coef_first * half + (mm(mixing, half_high) + mm(mixing, half_low))
    gram_ref[...] = product
    diagonals = []
    for place, (i, j) in enumerate(PAIRS):
        block = gram_ref[i * LANES : (i + 1) * LANES, j * LANES : (j + 1) * LANES]
        if i != j:
            other = gram_ref[j * LANES : (j + 1) * LANES, i * LANES : (i + 1) * LANES]
            block = 0.5 * (block + other.T)
        else:
            diagonals.append(jnp.sum(block * eye_block, axis=0, keepdims=True))
        at = AUX_P + place * LANES
        out_ref[at : at + LANES, :] = block.astype(bf16)

    def three(x):
        high = x.astype(bf16).astype(f32)
        middle = (x - high).astype(bf16).astype(f32)
        return high, middle, x - high - middle

    lines = [[], [], []]
    for diagonal in diagonals:
        for line, part in zip(lines, three(diagonal)):
            line.append(part)
    peaks = head[0:1]
    tallies = head[1:2]
    tally_high = tallies.astype(bf16).astype(f32)
    norm = three(jnp.broadcast_to(inverse, (1, LANES)))
    stacked = lines[0] + lines[1] + lines[2] + [peaks, tally_high, tallies - tally_high] + list(norm)
    place = lax.broadcasted_iota(jnp.int32, (AUX_P, LANES), 0)
    aux = jnp.zeros((AUX_P, LANES), f32)
    for number, line in enumerate(stacked):
        aux = jnp.where(place == number, line, aux)
    out_ref[0:AUX_P, :] = aux.astype(bf16)


def iterations(first, first_other, second, second_other):
    passes = 9 * NS_ITERS
    return pl.pallas_call(
        iterate_kernel,
        in_specs=[pl.BlockSpec(memory_space=pltpu.VMEM)] * 4,
        out_specs=pl.BlockSpec(memory_space=pltpu.VMEM),
        out_shape=jax.ShapeDtypeStruct((ROWS_P, LANES), bf16),
        scratch_shapes=[pltpu.VMEM((KV_RANK, KV_RANK), f32)],
        compiler_params=params(),
        cost_estimate=pl.CostEstimate(
            flops=passes * 2 * KV_RANK**3, bytes_accessed=4 * ROWS * LANES * 4, transcendentals=0
        ),
        name="iterations",
    )(first, first_other, second, second_other)


def apply_kernel(spread, seats, ids, counts, me, *refs):
    number = sum(1 for _ in {place for step in spread for place, _ in step})
    tables = refs[:number]
    nes_ref, weight_ref = refs[number : number + 2]
    update_ref, weight_out_ref, mat_ref, line_ref = refs[-4:]
    step_now = pl.program_id(0)
    row = lax.broadcasted_iota(jnp.int32, (LANES, LANES), 0)
    col = lax.broadcasted_iota(jnp.int32, (LANES, LANES), 1)

    def unpack(step):
        (place_a, start_a), (place_b, start_b) = spread[step]

        def rows_at(at, size):
            if at < HALF_P:
                piece = tables[place_a][start_a + at : start_a + min(at + size, HALF_P), :]
                if at + size > HALF_P:
                    piece = jnp.concatenate(
                        [piece, tables[place_b][start_b : start_b + at + size - HALF_P, :]], axis=0
                    )
                return piece.astype(f32)
            return tables[place_b][start_b + at - HALF_P : start_b + at + size - HALF_P, :].astype(f32)

        aux = rows_at(0, AUX_P)
        diagonal = [aux[i : i + 1] + aux[4 + i : 5 + i] + aux[8 + i : 9 + i] for i in range(BLOCKS)]
        inverse = [1.0 / line for line in diagonal]
        norm = aux[15:16] + aux[16:17] + aux[17:18]
        rms_scale = 0.2 * math.sqrt(max(KV_ROWS, KV_RANK))
        for i in range(BLOCKS):
            line_ref[0:1, i * LANES : (i + 1) * LANES] = diagonal[i] * (norm * rms_scale)
        peaks = aux[12:13]
        factor = jnp.sqrt(jnp.minimum(1.0, clip_limit / peaks))
        line_ref[1:2, 0:LANES] = factor
        line_ref[2:3, 0:LANES] = aux[13:14] + aux[14:15]
        for place, (i, j) in enumerate(PAIRS):
            block = rows_at(AUX_P + place * LANES, LANES)
            if i == j:
                scaled = jnp.where(row == col, 1.0, block * inverse[i])
                mat_ref[i * LANES : (i + 1) * LANES, i * LANES : (i + 1) * LANES] = scaled.astype(bf16)
            else:
                mat_ref[i * LANES : (i + 1) * LANES, j * LANES : (j + 1) * LANES] = (block * inverse[j]).astype(bf16)
                mat_ref[j * LANES : (j + 1) * LANES, i * LANES : (i + 1) * LANES] = (block.T * inverse[i]).astype(bf16)

    for step in range(len(spread)):
        pl.when(step_now == step)(functools.partial(unpack, step))

    capacity = nes_ref.shape[1]
    count = counts[ids[step_now]]
    groups, rows_block = seats
    lane = lax.broadcasted_iota(jnp.int32, (1, LANES), 1)
    lowest = me[0] * groups
    earlier = jnp.where((lane >= lowest) & (lane < lowest + me[1]), line_ref[2:3, 0:LANES], 0.0)
    before = jnp.sum(earlier, axis=1, keepdims=True).astype(jnp.int32)
    base = before + me[0] * rows_block
    head_rows = NOPE + VDIM
    first_head = base // head_rows
    factor = line_ref[1:2, 0:LANES]
    slot = lax.broadcasted_iota(jnp.int32, (capacity, LANES), 0)
    row_index = base + slot
    head_of = row_index // head_rows
    scale = jnp.ones((capacity, LANES), f32)
    for k in range((capacity - 1) // head_rows + 2):
        one = jnp.sum(jnp.where(lane == first_head + k, factor, 0.0), axis=1, keepdims=True)
        scale = jnp.where(head_of == first_head + k, one, scale)
    scale = jnp.where(row_index % head_rows < NOPE, scale, 1.0)
    scale = jnp.where(slot < count, scale, 0.0)
    kept = scale * (1.0 - learn_rate * decay_rate)
    moved = scale * learn_rate
    rows = nes_ref[0]
    half = KV_RANK // 2
    for side in range(2):
        product = mm(rows, mat_ref[:, side * half : (side + 1) * half])
        for part in range(half // LANES):
            at = side * half + part * LANES
            update = product[:, part * LANES : (part + 1) * LANES] * line_ref[0:1, at : at + LANES]
            update_ref[0, :, at : at + LANES] = update.astype(bf16)
            weight = weight_ref[0, :, at : at + LANES].astype(f32)
            weight_out_ref[0, :, at : at + LANES] = (weight * kept - update * moved).astype(bf16)


def apply_rows(spread, seats, ids, counts, me, tables, nes, order, weight, update, weight_out):
    number = len(spread)
    layers, capacity, features = weight.shape
    picked = lambda i, ids, counts, me: (ids[i], 0, 0)
    start = order[0]
    assert list(order) == list(range(start, start + number))
    in_specs = [whole(table.shape) for table in tables]
    in_specs += [
        pl.BlockSpec((1, capacity, features), lambda i, ids, counts, me: (i + start, 0, 0)),
        pl.BlockSpec((1, capacity, features), picked),
    ]
    args = list(tables) + [nes, weight]
    aliases = {}
    if update is not None:
        in_specs += [pl.BlockSpec(memory_space=pl.ANY)] * 2
        aliases = {3 + len(args): 0, 4 + len(args): 1}
        args += [update, weight_out]
    shape = jax.ShapeDtypeStruct((layers, capacity, features), bf16)
    return pl.pallas_call(
        functools.partial(apply_kernel, spread, seats),
        grid_spec=pltpu.PrefetchScalarGridSpec(
            num_scalar_prefetch=3,
            grid=(number,),
            in_specs=in_specs,
            out_specs=[pl.BlockSpec((1, capacity, features), picked)] * 2,
            scratch_shapes=[pltpu.VMEM((KV_RANK, KV_RANK), bf16), pltpu.VMEM((8, KV_RANK), f32)],
        ),
        out_shape=[shape, shape],
        input_output_aliases=aliases,
        compiler_params=params(),
        cost_estimate=pl.CostEstimate(
            flops=number * capacity * features * features * 2,
            bytes_accessed=number * capacity * features * 8,
            transcendentals=0,
        ),
        name="apply_rows",
    )(ids, counts, me, *args)


def local(dp_size, expert_size, grad_rows, momentum_rows, weight_rows, row_counts, logit_peaks):
    layers, capacity = grad_rows.shape[1:3]
    ring = expert_size // 2
    far = ring // 2
    assert layers == expert_size and ring >= 4 and ring % 2 == 0
    assert dp_size == 4 and dp_size * expert_size <= LANES
    dp = lax.axis_index("dp")
    expert = lax.axis_index("expert")
    seat, core = expert // 2, expert % 2
    counts = row_counts[0, :, 0]
    me = jnp.stack([dp, expert]).astype(jnp.int32)

    def layer(distance, own_core):
        return 2 * ((seat + distance) % ring) + (core if own_core else 1 - core)

    def across(x):
        return lax.ppermute(x, "expert", [(i, i ^ 1) for i in range(expert_size)])

    def along(x, by):
        return lax.ppermute(x, "expert", [(i, (i + 2 * by) % expert_size) for i in range(expert_size)])

    def over_dp(x, bit):
        return lax.ppermute(x, "dp", [(i, i ^ bit) for i in range(dp_size)])

    lane = lax.broadcasted_iota(jnp.int32, (layers, AUX, LANES), 2)
    line = lax.broadcasted_iota(jnp.int32, (layers, AUX, LANES), 1)
    peaks = jnp.pad(logit_peaks[0, 0].astype(f32), ((0, 0), (0, LANES - logit_peaks.shape[3])))
    mine = dp * expert_size + expert
    aux = jnp.where(line == 0, peaks[:, None, :], 0.0)
    aux = jnp.where((line == 1) & (lane == mine), counts[:, None, None].astype(f32), aux)

    def partials(distances, own_core):
        ids = jnp.stack([layer(distance, own_core) for distance in distances]).astype(jnp.int32)
        return gram_parts(ids, counts, grad_rows[0], momentum_rows[0], aux)

    near = [r for s in range(1, far) for r in (far - s, ring - far + s)] + [0]
    nes_far_other, far_other = partials([far], False)
    nes_far, far_own = partials([far], True)
    far_arrived = across(far_other)
    nes_near_other, near_other = partials(near, False)
    nes_near, near_own = partials(near, True)
    near_arrived = across(near_other)

    part = lambda rows: jax.ShapeDtypeStruct((rows, LANES), f32)
    first, second = local_call(split_kernel, [part(HEAD_A), part(TAIL_B)], "split", far_own, far_arrived)
    from_left, from_right = along(first, 1), along(second, -1)
    last = len(near) - 3
    if far == 2:
        up, down, own = local_call(
            relay_kernel, [part(ROWS)] * 3, "relay", near_own, near_arrived, from_left, from_right
        )
    else:
        rest = jnp.stack([joined(near_own[k], near_arrived[k]) for k in range(len(near))])
        pad_left = jnp.pad(from_left, ((0, TAIL_B), (0, 0)))
        pad_right = jnp.pad(from_right, ((HEAD_A, 0), (0, 0)))
        for k in range(0, last, 2):
            up, down = local_call(
                pass_kernel, [part(ROWS)] * 2, "pass", rest[k], rest[k + 1], pad_left, pad_right
            )
            pad_left, pad_right = along(up, 1), along(down, -1)
        up, down = local_call(
            pass_kernel, [part(ROWS)] * 2, "pass", rest[last], rest[last + 1], pad_left, pad_right
        )
        own = rest[last + 2]
    from_left, from_right = along(up, 1), along(down, -1)
    first, second = local_call(own_kernel, [part(HEAD_A), part(TAIL_B)], "own", own, from_left, from_right)
    first_other, second_other = over_dp(first, 1), over_dp(second, 2)
    first, second = local_call(
        pair_kernel, [part(HEAD_A), part(TAIL_B)], "pair", first, first_other, second, second_other
    )
    table = iterations(first, over_dp(first, 2), second, over_dp(second, 1))

    seats = (expert_size, KV_ROWS // dp_size)
    full = lambda place: ((place, 0), (place, HALF_P))
    weight = weight_rows[0]

    def ids_of(pairs):
        return jnp.stack([layer(distance, own_core) for distance, own_core in pairs]).astype(jnp.int32)

    left, right = along(table, 1), along(table, -1)
    own_tables = [table, across(table)]
    end = len(near) - 1
    update, weight_out = apply_rows(
        (full(0),), seats, ids_of([(0, True)]), counts, me, own_tables[:1], nes_near, [end], weight, None, None
    )
    update, weight_out = apply_rows(
        (full(0),), seats, ids_of([(0, False)]), counts, me, own_tables[1:], nes_near_other, [end], weight, update, weight_out
    )
    for hop in range(1, far):
        if hop == far - 1:
            next_left = along(left[:HALF_P], 1)
            next_right = along(right[HALF_P:], -1)
        else:
            next_left, next_right = along(left, 1), along(right, -1)
        place = near.index(hop)
        pair = [right, left]
        update, weight_out = apply_rows(
            (full(0), full(1)), seats, ids_of([(hop, True), (ring - hop, True)]), counts, me, pair, nes_near,
            [place, place + 1], weight, update, weight_out,
        )
        update, weight_out = apply_rows(
            (full(0), full(1)), seats, ids_of([(hop, False), (ring - hop, False)]), counts, me, [across(t) for t in pair],
            nes_near_other, [place, place + 1], weight, update, weight_out,
        )
        left, right = next_left, next_right
    halves = ((0, 0), (1, 0))
    update, weight_out = apply_rows(
        (halves,), seats, ids_of([(far, True)]), counts, me, [left, right], nes_far, [0], weight, update, weight_out
    )
    update, weight_out = apply_rows(
        (halves,), seats, ids_of([(far, False)]), counts, me, [across(left), across(right)], nes_far_other, [0],
        weight, update, weight_out,
    )
    return (update[None], weight_out[None])


def solution(mesh):
    return jax.shard_map(
        functools.partial(local, mesh.shape["dp"], mesh.shape["expert"]),
        mesh=mesh,
        in_specs=(
            P("dp", None, "expert", None),
            P("dp", None, "expert", None),
            P("dp", None, "expert", None),
            P("dp", None, "expert"),
            P("dp", "expert", None, None),
        ),
        out_specs=(P("dp", None, "expert", None), P("dp", None, "expert", None)),
        check_vma=False,
    )
```

```python
import functools
import math

import jax
import jax.numpy as jnp
from jax import lax
from jax.experimental import pallas as pl
from jax.experimental.pallas import tpu as pltpu
from jax.sharding import PartitionSpec as P

KV_RANK = 512
NOPE = 128
VDIM = 128
NS_ITERS = 5
KV_ROWS = 16384

momentum_coef = 0.95
learn_rate = 0.02
decay_rate = 0.1
clip_limit = 100.0
coef_first = 3.4445
coef_second = -4.775
coef_third = 2.0315

f32 = jnp.float32
bf16 = jnp.bfloat16
i16 = jnp.int16
i32 = jnp.int32

LANES = 128
BLOCKS = KV_RANK // LANES
HALVES = (
    ((0, 1, True), (0, 1, False), (0, 2, False), (1, 2, False)),
    ((2, 3, True), (0, 3, False), (1, 3, False), (2, 3, False)),
)
AUX = 8
HALF = AUX + 4 * LANES
AUX_CODE = 16
HALF_CODE = AUX_CODE + 4 * LANES
AUX_P = 32
HEAD_P = AUX_P + 4 * LANES
ROWS_P = AUX_P + 8 * LANES
UNIT = 32000.0


def params(mebibytes=40):
    return pltpu.CompilerParams(vmem_limit_bytes=mebibytes * 1024 * 1024)


def whole(shape):
    return pl.BlockSpec(shape, lambda *_: (0,) * len(shape))


def square_iotas():
    row = lax.broadcasted_iota(i32, (LANES, LANES), 0)
    col = lax.broadcasted_iota(i32, (LANES, LANES), 1)
    return row, col


def layer_of(me, relative, own_core):
    core = me[1] if own_core else 1 - me[1]
    return 2 * (me[0] ^ relative) + core


def gram_kernel(own_core, me, counts, grad_ref, mom_ref, peaks_ref, *refs):
    nes_ref, gram_ref = refs[-2:]
    layer = layer_of(me, pl.program_id(0), own_core)
    count = counts[layer]
    gradient = grad_ref[0].astype(f32)
    velocity = momentum_coef * mom_ref[0].astype(f32) + gradient
    nesterov = gradient + momentum_coef * velocity
    slot = lax.broadcasted_iota(i32, nesterov.shape, 0)
    rows = jnp.where(slot < count, nesterov, 0.0).astype(bf16)
    nes_ref[0] = rows
    half = KV_RANK // 2
    dims = (((0,), (0,)), ((), ()))
    upper = lax.dot_general(rows[:, :half], rows, dims, preferred_element_type=f32)
    lower = lax.dot_general(rows[:, half:], rows[:, half:], dims, preferred_element_type=f32)

    def block(i, j):
        if i < 2:
            return upper[i * LANES : (i + 1) * LANES, j * LANES : (j + 1) * LANES]
        return lower[(i - 2) * LANES : (i - 1) * LANES, (j - 2) * LANES : (j - 1) * LANES]

    row, col = square_iotas()
    line = lax.broadcasted_iota(i32, (AUX, LANES), 0)
    lane = lax.broadcasted_iota(i32, (AUX, LANES), 1)
    aux = jnp.where((line == 5) & (lane == me[2]), count.astype(f32), 0.0)
    peaks = peaks_ref[...].astype(f32)
    pick = lax.broadcasted_iota(i32, peaks.shape, 0) == layer
    peaks = jnp.sum(jnp.where(pick, peaks, 0.0), axis=0, keepdims=True)
    peaks = jnp.concatenate([peaks, jnp.zeros((1, LANES - peaks.shape[1]), f32)], axis=1)
    aux = jnp.where(line == 4, peaks, aux)
    for i in range(BLOCKS):
        diagonal = jnp.sum(jnp.where(row == col, block(i, i), 0.0), axis=0, keepdims=True)
        aux = jnp.where(line == i, diagonal, aux)
    for number, entries in enumerate(HALVES):
        base = number * HALF
        gram_ref[0, base : base + AUX, :] = aux
        for place, (i, j, triangle) in enumerate(entries):
            at = base + AUX + place * LANES
            value = jnp.where(row <= col, block(i, i), block(j, j)) if triangle else block(i, j)
            gram_ref[0, at : at + LANES, :] = value


def gram_parts(own_core, me, counts, grad, mom, peaks, nes):
    layers, capacity, features = grad.shape
    number = layers // 2
    picked = lambda i, me, counts: (layer_of(me, i, own_core), 0, 0)
    in_specs = [
        pl.BlockSpec((1, capacity, features), picked),
        pl.BlockSpec((1, capacity, features), picked),
        whole(peaks.shape),
    ]
    args = [grad, mom, peaks]
    aliases = {}
    if nes is not None:
        in_specs.append(pl.BlockSpec(memory_space=pl.ANY))
        args.append(nes)
        aliases = {5: 0}
    return pl.pallas_call(
        functools.partial(gram_kernel, own_core),
        grid_spec=pltpu.PrefetchScalarGridSpec(
            num_scalar_prefetch=2,
            grid=(number,),
            in_specs=in_specs,
            out_specs=[
                pl.BlockSpec((1, capacity, features), picked),
                pl.BlockSpec((1, 2 * HALF, LANES), lambda i, me, counts: (i, 0, 0)),
            ],
        ),
        out_shape=[
            jax.ShapeDtypeStruct((layers, capacity, features), bf16),
            jax.ShapeDtypeStruct((number, 2 * HALF, LANES), f32),
        ],
        input_output_aliases=aliases,
        compiler_params=params(60),
        cost_estimate=pl.CostEstimate(
            flops=number * capacity * features * features * 2,
            bytes_accessed=number * (capacity * features * 6 + 2 * HALF * LANES * 4),
            transcendentals=0,
        ),
        name="gram_parts",
    )(me, counts, *args)


def joined(first, second):
    line = lax.broadcasted_iota(i32, (AUX, LANES), 0)
    aux = jnp.where(line == 4, jnp.maximum(first[0], second[0]), first[0] + second[0])
    return [aux] + [x + y for x, y in zip(first[1:], second[1:])]


def load_half(ref, index, base=0):
    starts = [base + AUX + place * LANES for place in range(4)]
    return [ref[index, base : base + AUX, :]] + [ref[index, at : at + LANES, :] for at in starts]


def store_half(ref, index, half):
    ref[index, 0:AUX, :] = half[0]
    for place in range(4):
        at = AUX + place * LANES
        ref[index, at : at + LANES, :] = half[1 + place]


def outer_scales(which, scale):
    row, col = square_iotas()
    across = [scale[g : g + 1] for g in range(BLOCKS)]
    down = {}

    def outer(i, j):
        if i not in down:
            down[i] = jnp.broadcast_to(across[i], (LANES, LANES)).T
        return down[i] * across[j]

    return [
        jnp.where(row <= col, outer(i, i), outer(j, j)) if triangle else outer(i, j)
        for i, j, triangle in HALVES[which]
    ]


def decoded(which, ref, index):
    line = lax.broadcasted_iota(i32, (AUX, LANES), 0)
    codes = ref[index, 0:AUX_CODE, :].astype(i32).astype(f32)
    low, high = codes[0:AUX], codes[AUX:AUX_CODE]
    scale = jnp.where(line < 4, jnp.exp2(low) * jnp.sqrt(high * (1.0 / UNIT)), 0.0)
    aux = jnp.where(line < 4, scale * scale, jnp.where(line == 4, low * (1.0 / 64.0), low))
    half = [aux]
    for place, factor in enumerate(outer_scales(which, scale)):
        at = AUX_CODE + place * LANES
        half.append(ref[index, at : at + LANES, :].astype(i32).astype(f32) * (factor * (1.0 / UNIT)))
    return half


def encode(which, ref, index, half):
    line = lax.broadcasted_iota(i32, (AUX, LANES), 0)
    aux = half[0]
    diagonal = jnp.maximum(aux, 1e-30)
    power = jnp.ceil(0.5 * jnp.log2(diagonal))
    high = jnp.clip(jnp.floor(diagonal * jnp.exp2(-2.0 * power) * UNIT + 0.5), 1.0, 32767.0)
    low = jnp.where(line < 4, power, jnp.where(line == 4, jnp.floor(aux * 64.0 + 0.5), aux))
    high = jnp.where(line < 4, high, 0.0)
    ref[index, 0:AUX_CODE, :] = jnp.concatenate([low, high], axis=0).astype(i32).astype(i16)
    inverse = jnp.where(line < 4, jnp.exp2(-power) * lax.rsqrt(high * (1.0 / UNIT)), 0.0)
    for place, factor in enumerate(outer_scales(which, inverse)):
        at = AUX_CODE + place * LANES
        value = jnp.floor(half[1 + place] * (factor * UNIT) + 0.5)
        value = jnp.clip(value, -32767.0, 32767.0)
        ref[index, at : at + LANES, :] = value.astype(i32).astype(i16)


def local_call(kernel, out_shapes, name, *args):
    size = sum(math.prod(x.shape) * x.dtype.itemsize for x in list(args) + list(out_shapes))
    return pl.pallas_call(
        kernel,
        in_specs=[pl.BlockSpec(memory_space=pltpu.VMEM)] * len(args),
        out_specs=[pl.BlockSpec(memory_space=pltpu.VMEM)] * len(out_shapes),
        out_shape=list(out_shapes),
        compiler_params=params(),
        cost_estimate=pl.CostEstimate(flops=size * 4, bytes_accessed=size, transcendentals=0),
        name=name,
    )(*args)


def first_kernel(sends, keeps, kept, arrived, *refs):
    for which in range(2):
        message, stay = refs[2 * which : 2 * which + 2]
        for index in range(kept.shape[0]):
            base = which * HALF
            half = joined(load_half(kept, index, base), load_half(arrived, index, base))
            if index in sends[which]:
                encode(which, message, sends[which].index(index), half)
            else:
                store_half(stay, keeps[which].index(index), half)


def next_kernel(sends, keeps, *refs):
    for which in range(2):
        kept, arrived = refs[2 * which : 2 * which + 2]
        message, stay = refs[4 + 2 * which : 6 + 2 * which]
        for index in range(kept.shape[0]):
            half = joined(load_half(kept, index), decoded(which, arrived, index))
            if index in sends[which]:
                encode(which, message, sends[which].index(index), half)
            if index in keeps[which]:
                store_half(stay, keeps[which].index(index), half)


def mm(x, y):
    return jnp.dot(x, y, preferred_element_type=f32)


def parts_of(x):
    high = x.astype(bf16)
    return high, (x - high.astype(f32)).astype(bf16)


def unpack_symmetric(which, blocks, diagonal, store):
    row, col = square_iotas()
    for (i, j, triangle), block in zip(HALVES[which], blocks):
        other = block.T
        if triangle:
            first = jnp.where(row < col, block, other)
            second = jnp.where(row > col, block, other)
            store(i, i, jnp.where(row == col, diagonal(i), first))
            store(j, j, jnp.where(row == col, diagonal(j), second))
        else:
            store(i, j, block)
            store(j, i, other)


def iterate_kernel(kept_a, arrived_a, kept_b, arrived_b, out_ref, gram_ref):
    row, col = square_iotas()

    def store(i, j, block):
        gram_ref[i * LANES : (i + 1) * LANES, j * LANES : (j + 1) * LANES] = block

    aux = None
    for which, kept, arrived in ((0, kept_a, arrived_a), (1, kept_b, arrived_b)):
        half = joined(load_half(kept, 0), decoded(which, arrived, 0))
        if aux is None:
            aux = half[0]
        unpack_symmetric(which, half[1:], lambda g: aux[g : g + 1], store)
    line = lax.broadcasted_iota(i32, (AUX, LANES), 0)
    squares = jnp.sum(jnp.where(line < 4, aux, 0.0), axis=0, keepdims=True)
    squares = jnp.sum(squares, axis=1, keepdims=True)
    inverse = 1.0 / (jnp.sqrt(squares) + 1e-07)
    gram = gram_ref[...] * inverse * inverse
    full_row = lax.broadcasted_iota(i32, (KV_RANK, KV_RANK), 0)
    full_col = lax.broadcasted_iota(i32, (KV_RANK, KV_RANK), 1)
    product = None
    for repeat in range(NS_ITERS):
        high, low = parts_of(gram)
        square = mm(high, high) + (mm(high, low) + mm(low, high))
        mixing = (coef_second * gram + coef_third * square).astype(bf16)
        if product is None:
            product = jnp.where(full_row == full_col, coef_first, 0.0) + mixing.astype(f32)
        else:
            product_high, product_low = parts_of(product)
            product = coef_first * product + (mm(product_high, mixing) + mm(product_low, mixing))
        if repeat < NS_ITERS - 1:
            half = coef_first * gram + (mm(high, mixing) + mm(low, mixing))
            half_high, half_low = parts_of(half)
            gram = coef_first * half + (mm(mixing, half_high) + mm(mixing, half_low))
    gram_ref[...] = product
    at = AUX_P
    for entries in HALVES:
        for i, j, triangle in entries:
            load = lambda i, j: gram_ref[i * LANES : (i + 1) * LANES, j * LANES : (j + 1) * LANES]
            if triangle:
                block = jnp.where(row <= col, load(i, i), load(j, j))
            else:
                block = 0.5 * (load(i, j) + load(j, i).T)
            out_ref[at : at + LANES, :] = block.astype(bf16)
            at += LANES

    def three(x):
        high = x.astype(bf16).astype(f32)
        middle = (x - high).astype(bf16).astype(f32)
        return high, middle, x - high - middle

    lines = [[], [], []]
    for i in range(BLOCKS):
        block = gram_ref[i * LANES : (i + 1) * LANES, i * LANES : (i + 1) * LANES]
        diagonal = jnp.sum(jnp.where(row == col, block, 0.0), axis=0, keepdims=True)
        for lines_of, part in zip(lines, three(diagonal)):
            lines_of.append(part)
    peaks = aux[4:5]
    tallies = aux[5:6]
    tally_high = tallies.astype(bf16).astype(f32)
    norm = three(jnp.broadcast_to(inverse, (1, LANES)))
    stacked = lines[0] + lines[1] + lines[2] + [peaks, tally_high, tallies - tally_high] + list(norm)
    place = lax.broadcasted_iota(i32, (AUX_P, LANES), 0)
    table = jnp.zeros((AUX_P, LANES), f32)
    for number, one in enumerate(stacked):
        table = jnp.where(place == number, one, table)
    out_ref[0:AUX_P, :] = table.astype(bf16)


def iterations(*args):
    return pl.pallas_call(
        iterate_kernel,
        in_specs=[pl.BlockSpec(memory_space=pltpu.VMEM)] * 4,
        out_specs=pl.BlockSpec(memory_space=pltpu.VMEM),
        out_shape=jax.ShapeDtypeStruct((ROWS_P, LANES), bf16),
        scratch_shapes=[pltpu.VMEM((KV_RANK, KV_RANK), f32)],
        compiler_params=params(),
        cost_estimate=pl.CostEstimate(
            flops=9 * NS_ITERS * 2 * KV_RANK**3, bytes_accessed=12 * HALF * LANES, transcendentals=0
        ),
        name="iterations",
    )(*args)


def apply_kernel(steps, spread, seats, me, counts, *refs):
    number = 1 + max(place for step in spread for place, _ in step)
    tables = refs[:number]
    nes_ref, weight_ref = refs[number : number + 2]
    update_ref, weight_out_ref, mat_ref, line_ref = refs[-4:]
    step_now = pl.program_id(0)

    def unpack(step):
        (place_a, start_a), (place_b, start_b) = spread[step]
        aux = tables[place_a][start_a : start_a + AUX_P, :].astype(f32)
        diagonal = [aux[i : i + 1] + aux[4 + i : 5 + i] + aux[8 + i : 9 + i] for i in range(BLOCKS)]
        inverse = [1.0 / line for line in diagonal]
        norm = aux[15:16] + aux[16:17] + aux[17:18]
        rms_scale = 0.2 * math.sqrt(max(KV_ROWS, KV_RANK))
        for i in range(BLOCKS):
            line_ref[0:1, i * LANES : (i + 1) * LANES] = diagonal[i] * (norm * rms_scale)
        peaks = aux[12:13]
        line_ref[1:2, 0:LANES] = jnp.sqrt(jnp.minimum(1.0, clip_limit / peaks))
        line_ref[2:3, 0:LANES] = aux[13:14] + aux[14:15]

        def store(i, j, block):
            mat_ref[i * LANES : (i + 1) * LANES, j * LANES : (j + 1) * LANES] = (block * inverse[j]).astype(bf16)

        for which, (place, start) in enumerate(((place_a, start_a + AUX_P), (place_b, start_b))):
            blocks = [
                tables[place][start + k * LANES : start + (k + 1) * LANES, :].astype(f32) for k in range(4)
            ]
            unpack_symmetric(which, blocks, lambda g: diagonal[g], store)

    for step in range(len(spread)):
        pl.when(step_now == step)(functools.partial(unpack, step))

    capacity = nes_ref.shape[1]
    count = counts[chosen_layer(steps, step_now, me)]
    groups, rows_block = seats
    dp, expert = me[2] // groups, me[2] % groups
    lane = lax.broadcasted_iota(i32, (1, LANES), 1)
    lowest = dp * groups
    earlier = jnp.where((lane >= lowest) & (lane < lowest + expert), line_ref[2:3, 0:LANES], 0.0)
    before = jnp.sum(earlier, axis=1, keepdims=True).astype(i32)
    base = before + dp * rows_block
    head_rows = NOPE + VDIM
    first_head = base // head_rows
    factor = line_ref[1:2, 0:LANES]
    slot = lax.broadcasted_iota(i32, (capacity, LANES), 0)
    row_index = base + slot
    head_of = row_index // head_rows
    scale = jnp.ones((capacity, LANES), f32)
    for k in range((capacity - 1) // head_rows + 2):
        one = jnp.sum(jnp.where(lane == first_head + k, factor, 0.0), axis=1, keepdims=True)
        scale = jnp.where(head_of == first_head + k, one, scale)
    scale = jnp.where(row_index % head_rows < NOPE, scale, 1.0)
    scale = jnp.where(slot < count, scale, 0.0)
    kept = scale * (1.0 - learn_rate * decay_rate)
    moved = scale * learn_rate
    rows = nes_ref[0]
    half = KV_RANK // 2
    for side in range(2):
        product = mm(rows, mat_ref[:, side * half : (side + 1) * half])
        for part in range(half // LANES):
            at = side * half + part * LANES
            update = product[:, part * LANES : (part + 1) * LANES] * line_ref[0:1, at : at + LANES]
            update_ref[0, :, at : at + LANES] = update.astype(bf16)
            weight = weight_ref[0, :, at : at + LANES].astype(f32)
            weight_out_ref[0, :, at : at + LANES] = (weight * kept - update * moved).astype(bf16)


def chosen_layer(steps, i, me):
    layer = layer_of(me, *steps[0])
    for number in range(1, len(steps)):
        layer = jnp.where(i == number, layer_of(me, *steps[number]), layer)
    return layer


def apply_rows(steps, spread, seats, me, counts, tables, nes, weight, update, weight_out):
    number = len(steps)
    layers, capacity, features = weight.shape
    picked = lambda i, me, counts: (chosen_layer(steps, i, me), 0, 0)
    in_specs = [whole(table.shape) for table in tables]
    in_specs += [pl.BlockSpec((1, capacity, features), picked)] * 2
    args = list(tables) + [nes, weight]
    aliases = {}
    if update is not None:
        in_specs += [pl.BlockSpec(memory_space=pl.ANY)] * 2
        aliases = {2 + len(args): 0, 3 + len(args): 1}
        args += [update, weight_out]
    shape = jax.ShapeDtypeStruct((layers, capacity, features), bf16)
    return pl.pallas_call(
        functools.partial(apply_kernel, steps, spread, seats),
        grid_spec=pltpu.PrefetchScalarGridSpec(
            num_scalar_prefetch=2,
            grid=(number,),
            in_specs=in_specs,
            out_specs=[pl.BlockSpec((1, capacity, features), picked)] * 2,
            scratch_shapes=[pltpu.VMEM((KV_RANK, KV_RANK), bf16), pltpu.VMEM((8, KV_RANK), f32)],
        ),
        out_shape=[shape, shape],
        input_output_aliases=aliases,
        compiler_params=params(),
        cost_estimate=pl.CostEstimate(
            flops=number * capacity * features * features * 2,
            bytes_accessed=number * capacity * features * 8,
            transcendentals=0,
        ),
        name="apply_rows",
    )(me, counts, *args)


def local(dp_size, expert_size, grad_rows, momentum_rows, weight_rows, row_counts, logit_peaks):
    layers = grad_rows.shape[1]
    expert_bits = expert_size.bit_length() - 1
    bits = expert_bits - 1
    assert layers == expert_size == 1 << expert_bits and bits >= 2
    assert dp_size == 4 and dp_size * expert_size <= LANES
    dp = lax.axis_index("dp")
    expert = lax.axis_index("expert")
    counts = row_counts.reshape(layers)
    owner = ((dp >> 1) << (bits - 1)) | ((expert >> 1) & ((1 << (bits - 1)) - 1))
    me = jnp.stack([owner, expert & 1, dp * expert_size + expert]).astype(i32)
    owner_axes = [("expert", 1 << (p + 1)) for p in range(bits - 1)] + [("dp", 2)]
    copy_axes = [("dp", 1), ("expert", 1 << (expert_bits - 1))]
    sizes = {"dp": dp_size, "expert": expert_size}

    def over(x, axis_bit):
        axis, bit = axis_bit
        return lax.ppermute(x, axis, [(i, i ^ bit) for i in range(sizes[axis])])

    core_axis = ("expert", 1)
    grad, mom, peaks = grad_rows[0], momentum_rows[0], logit_peaks[0, 0]
    nes, other = gram_parts(False, me, counts, grad, mom, peaks, None)
    arrived = over(other, core_axis)
    nes, own = gram_parts(True, me, counts, grad, mom, peaks, nes)

    codes = lambda n: jax.ShapeDtypeStruct((n, HALF_CODE, LANES), i16)
    plain = lambda n: jax.ShapeDtypeStruct((n, HALF, LANES), f32)
    orders = (list(range(bits - 1, -1, -1)), list(range(bits)))
    current = [list(range(1 << bits)) for _ in range(2)]
    state = None
    for step in range(bits + 2):
        if step < bits:
            axes = [owner_axes[orders[which][step]] for which in range(2)]
            sends = [[k for k, r in enumerate(current[w]) if r >> orders[w][step] & 1] for w in range(2)]
            keeps = [[k for k in range(len(current[w])) if k not in sends[w]] for w in range(2)]
            current = [[current[w][k] for k in keeps[w]] for w in range(2)]
        else:
            axes = [copy_axes[step - bits], copy_axes[1 - (step - bits)]]
            sends = keeps = [[0], [0]]
        shapes = [s for w in range(2) for s in (codes(len(sends[w])), plain(len(keeps[w])))]
        if state is None:
            kernel, state = first_kernel, (own, arrived)
        else:
            kernel = next_kernel
        out = local_call(functools.partial(kernel, sends, keeps), shapes, "sum" + str(step), *state)
        state = (out[1], over(out[0], axes[0]), out[3], over(out[2], axes[1]))
    table = iterations(*state)

    seats = (expert_size, KV_ROWS // dp_size)
    weight = weight_rows[0]
    full = lambda place: ((place, 0), (place, HEAD_P))
    apply = lambda steps, spread, tables, *outs: apply_rows(
        steps, spread, seats, me, counts, tables, nes, weight, *outs
    )
    tables = {0: table}
    for position in range(bits - 1, -1, -1) if bits > 2 else ():
        for known in list(tables):
            tables[known | 1 << position] = over(tables[known], owner_axes[position])
    if bits == 2:
        tables[2], tables[1] = over(table, owner_axes[1]), over(table, owner_axes[0])
    pair = [table, over(table, core_axis)]
    update, weight_out = apply(((0, True), (0, False)), (full(0), full(1)), pair, None, None)
    if bits == 2:
        tables[1], tables[2], update = lax.optimization_barrier((tables[1], tables[2], update))
        tail = [over(tables[1][:HEAD_P], owner_axes[1]), over(tables[2][HEAD_P:], owner_axes[0])]
        near = [tables[1], tables[2]]
        near += [over(x, core_axis) for x in near]
        update, weight_out = apply(
            ((1, True), (2, True), (1, False), (2, False)), tuple(full(k) for k in range(4)), near, update, weight_out
        )
        tail += [over(x, core_axis) for x in tail]
        spread = (((0, 0), (1, 0)), ((2, 0), (3, 0)))
        update, weight_out = apply(((3, True), (3, False)), spread, tail, update, weight_out)
    else:
        for relative in range(1, 1 << bits):
            pair = [tables[relative], over(tables[relative], core_axis)]
            update, weight_out = apply(
                ((relative, True), (relative, False)), (full(0), full(1)), pair, update, weight_out
            )
    return (update[None], weight_out[None])


def solution(mesh):
    return jax.shard_map(
        functools.partial(local, mesh.shape["dp"], mesh.shape["expert"]),
        mesh=mesh,
        in_specs=(
            P("dp", None, "expert", None),
            P("dp", None, "expert", None),
            P("dp", None, "expert", None),
            P("dp", None, "expert"),
            P("dp", "expert", None, None),
        ),
        out_specs=(P("dp", None, "expert", None), P("dp", None, "expert", None)),
        check_vma=False,
    )
```

```python
import functools
import math

import jax
import jax.numpy as jnp
from jax import lax
from jax.experimental import pallas as pl
from jax.experimental.pallas import tpu as pltpu
from jax.sharding import PartitionSpec as P

KV_RANK = 512
NOPE = 128
VDIM = 128
NS_ITERS = 5
KV_ROWS = 16384

momentum_coef = 0.95
learn_rate = 0.02
decay_rate = 0.1
clip_limit = 100.0
coef_first = 3.4445
coef_second = -4.775
coef_third = 2.0315

f32 = jnp.float32
bf16 = jnp.bfloat16
i16 = jnp.int16
i32 = jnp.int32

LANES = 128
BLOCKS = KV_RANK // LANES
HALVES = (
    ((0, 1, True), (0, 1, False), (0, 2, False), (1, 2, False)),
    ((2, 3, True), (0, 3, False), (1, 3, False), (2, 3, False)),
)
AUX = 8
HALF = AUX + 4 * LANES
AUX_CODE = 16
HALF_CODE = AUX_CODE + 4 * LANES
AUX_P = 32
HEAD_P = AUX_P + 4 * LANES
ROWS_P = AUX_P + 8 * LANES
UNIT = 32000.0
CHUNKS = 2


def params(mebibytes=40):
    return pltpu.CompilerParams(vmem_limit_bytes=mebibytes * 1024 * 1024)


def pinned(x):
    return pltpu.with_memory_space_constraint(x, pltpu.HBM)


def square_iotas():
    row = lax.broadcasted_iota(i32, (LANES, LANES), 0)
    col = lax.broadcasted_iota(i32, (LANES, LANES), 1)
    return row, col


def layer_of(me, relative, own_core):
    core = me[1] if own_core else 1 - me[1]
    return 2 * (me[0] ^ relative) + core


def gram_kernel(picks, me, counts_ref, grad_ref, mom_ref, peaks_ref, nes_ref, *refs):
    number = len(picks)
    outs = refs[:-7]
    counts, counts_arrival, peaks_buf, peaks_arrival, grad_buf, mom_buf, arrivals = refs[-7:]
    layers = [layer_of(me, *pick) for pick in picks]
    copies = []
    for k, layer in enumerate(layers):
        copies.append(pltpu.make_async_copy(grad_ref.at[layer], grad_buf.at[k], arrivals.at[0, k]))
        copies.append(pltpu.make_async_copy(mom_ref.at[layer], mom_buf.at[k], arrivals.at[1, k]))
    small = [
        pltpu.make_async_copy(counts_ref, counts, counts_arrival),
        pltpu.make_async_copy(peaks_ref, peaks_buf, peaks_arrival),
    ]
    for copy in copies[:2] + small + copies[2:]:
        copy.start()
    for copy in small:
        copy.wait()
    row, col = square_iotas()
    line = lax.broadcasted_iota(i32, (AUX, LANES), 0)
    lane = lax.broadcasted_iota(i32, (AUX, LANES), 1)
    every_peak = peaks_buf[...].astype(f32)
    every_peak = jnp.concatenate(
        [every_peak, jnp.zeros((every_peak.shape[0], LANES - every_peak.shape[1]), f32)], axis=1
    )
    pick_row = lax.broadcasted_iota(i32, every_peak.shape, 0)
    width = KV_RANK // 2
    dims = (((0,), (0,)), ((), ()))
    slot = lax.broadcasted_iota(i32, (grad_buf.shape[1], LANES), 0)

    def form_rows(k):
        copies[2 * k].wait()
        copies[2 * k + 1].wait()
        live = slot < counts[layers[k]]
        for i in range(BLOCKS):
            span = slice(i * LANES, (i + 1) * LANES)
            gradient = grad_buf[k, :, span].astype(f32)
            velocity = momentum_coef * mom_buf[k, :, span].astype(f32) + gradient
            nesterov = gradient + momentum_coef * velocity
            nes_ref[k, :, span] = jnp.where(live, nesterov, 0.0).astype(bf16)

    form_rows(0)
    for k, layer in enumerate(layers):
        if k + 1 < number:
            form_rows(k + 1)
        rows = nes_ref[k]
        upper = lax.dot_general(rows[:, :width], rows, dims, preferred_element_type=f32)
        lower = lax.dot_general(rows[:, width:], rows[:, width:], dims, preferred_element_type=f32)

        def block(i, j):
            if i < 2:
                return upper[i * LANES : (i + 1) * LANES, j * LANES : (j + 1) * LANES]
            return lower[(i - 2) * LANES : (i - 1) * LANES, (j - 2) * LANES : (j - 1) * LANES]

        aux = jnp.where((line == 5) & (lane == me[2]), counts[layer].astype(f32), 0.0)
        peaks = jnp.sum(jnp.where(pick_row == layer, every_peak, 0.0), axis=0, keepdims=True)
        aux = jnp.where(line == 4, peaks, aux)
        for i in range(BLOCKS):
            diagonal = jnp.sum(jnp.where(row == col, block(i, i), 0.0), axis=0, keepdims=True)
            aux = jnp.where(line == i, diagonal, aux)
        for which, entries in enumerate(HALVES):
            half = [aux]
            for i, j, triangle in entries:
                half.append(jnp.where(row <= col, block(i, i), block(j, j)) if triangle else block(i, j))
            if len(outs) > 1:
                store_half(outs[2 * k + which], 0, half)
            else:
                store_half(outs[0], k, half, which * HALF)


def gram_parts(picks, out_shapes, me, counts, grad, mom, peaks):
    capacity, features = grad.shape[1:]
    number = len(picks)
    smem = pl.BlockSpec(memory_space=pltpu.SMEM)
    vmem = pl.BlockSpec(memory_space=pltpu.VMEM)
    hbm = pl.BlockSpec(memory_space=pltpu.HBM)
    out_shapes = [jax.ShapeDtypeStruct((number, capacity, features), bf16)] + list(out_shapes)
    return pl.pallas_call(
        functools.partial(gram_kernel, picks),
        in_specs=[smem, hbm, hbm, hbm, hbm],
        out_specs=[vmem] * len(out_shapes),
        out_shape=out_shapes,
        scratch_shapes=[
            pltpu.SMEM(counts.shape, i32),
            pltpu.SemaphoreType.DMA(()),
            pltpu.VMEM(peaks.shape, bf16),
            pltpu.SemaphoreType.DMA(()),
            pltpu.VMEM((number, capacity, features), bf16),
            pltpu.VMEM((number, capacity, features), bf16),
            pltpu.SemaphoreType.DMA((2, number)),
        ],
        compiler_params=params(),
        cost_estimate=pl.CostEstimate(
            flops=number * capacity * features * features * 2,
            bytes_accessed=number * (capacity * features * 6 + 2 * HALF * LANES * 4),
            transcendentals=0,
        ),
        name="gram_parts",
    )(me, pinned(counts), pinned(grad), pinned(mom), pinned(peaks))


def joined(first, second):
    line = lax.broadcasted_iota(i32, (AUX, LANES), 0)
    aux = jnp.where(line == 4, jnp.maximum(first[0], second[0]), first[0] + second[0])
    return [aux] + [x + y for x, y in zip(first[1:], second[1:])]


def load_half(ref, index, base=0):
    starts = [base + AUX + place * LANES for place in range(4)]
    return [ref[index, base : base + AUX, :]] + [ref[index, at : at + LANES, :] for at in starts]


def store_half(ref, index, half, base=0):
    ref[index, base : base + AUX, :] = half[0]
    for place in range(4):
        at = base + AUX + place * LANES
        ref[index, at : at + LANES, :] = half[1 + place]


def outer_scales(which, scale):
    row, col = square_iotas()
    across = [scale[g : g + 1] for g in range(BLOCKS)]
    down = {}

    def outer(i, j):
        if i not in down:
            down[i] = jnp.broadcast_to(across[i], (LANES, LANES)).T
        return down[i] * across[j]

    return [
        jnp.where(row <= col, outer(i, i), outer(j, j)) if triangle else outer(i, j)
        for i, j, triangle in HALVES[which]
    ]


def decoded(which, ref, index):
    line = lax.broadcasted_iota(i32, (AUX, LANES), 0)
    codes = ref[index, 0:AUX_CODE, :].astype(i32).astype(f32)
    low, high = codes[0:AUX], codes[AUX:AUX_CODE]
    scale = jnp.where(line < 4, jnp.exp2(low) * jnp.sqrt(high * (1.0 / UNIT)), 0.0)
    aux = jnp.where(line < 4, scale * scale, jnp.where(line == 4, low * (1.0 / 64.0), low))
    half = [aux]
    for place, factor in enumerate(outer_scales(which, scale)):
        at = AUX_CODE + place * LANES
        half.append(ref[index, at : at + LANES, :].astype(i32).astype(f32) * (factor * (1.0 / UNIT)))
    return half


def encode(which, ref, index, half):
    line = lax.broadcasted_iota(i32, (AUX, LANES), 0)
    aux = half[0]
    diagonal = jnp.maximum(aux, 1e-30)
    power = jnp.ceil(0.5 * jnp.log2(diagonal))
    high = jnp.clip(jnp.floor(diagonal * jnp.exp2(-2.0 * power) * UNIT + 0.5), 1.0, 32767.0)
    low = jnp.where(line < 4, power, jnp.where(line == 4, jnp.floor(aux * 64.0 + 0.5), aux))
    high = jnp.where(line < 4, high, 0.0)
    ref[index, 0:AUX_CODE, :] = jnp.concatenate([low, high], axis=0).astype(i32).astype(i16)
    inverse = jnp.where(line < 4, jnp.exp2(-power) * lax.rsqrt(high * (1.0 / UNIT)), 0.0)
    for place, factor in enumerate(outer_scales(which, inverse)):
        at = AUX_CODE + place * LANES
        value = jnp.floor(half[1 + place] * (factor * UNIT) + 0.5)
        value = jnp.clip(value, -32767.0, 32767.0)
        ref[index, at : at + LANES, :] = value.astype(i32).astype(i16)


def local_call(kernel, out_shapes, name, *args):
    size = sum(math.prod(x.shape) * x.dtype.itemsize for x in list(args) + list(out_shapes))
    return pl.pallas_call(
        kernel,
        in_specs=[pl.BlockSpec(memory_space=pltpu.VMEM)] * len(args),
        out_specs=[pl.BlockSpec(memory_space=pltpu.VMEM)] * len(out_shapes),
        out_shape=list(out_shapes),
        compiler_params=params(),
        cost_estimate=pl.CostEstimate(flops=size * 4, bytes_accessed=size, transcendentals=0),
        name=name,
    )(*args)


def first_kernel(message_of, kept, arrived, *refs):
    for which in range(2):
        message, stay = refs[2 * which : 2 * which + 2]
        for index, (send, place) in enumerate(message_of[which]):
            base = which * HALF
            half = joined(load_half(kept, index, base), load_half(arrived, index, base))
            if send:
                encode(which, message, place, half)
            else:
                store_half(stay, place, half)


def sum_kernel(sends, keeps, late, *refs):
    outs = refs[8 if late else 4 :]
    for which in range(2):
        kept, arrived = refs[2 * which : 2 * which + 2]
        message, stay = outs[2 * which : 2 * which + 2]
        for index in range(arrived.shape[0]):
            if late and index == 0:
                half = joined(load_half(refs[4 + which], 0), load_half(refs[6 + which], 0))
            else:
                half = load_half(kept, index - 1 if late else index)
            half = joined(half, decoded(which, arrived, index))
            if index in sends[which]:
                encode(which, message, sends[which].index(index), half)
            if index in keeps[which]:
                store_half(stay, keeps[which].index(index), half)


def mm(x, y):
    return jnp.dot(x, y, preferred_element_type=f32)


def wide(*parts):
    return jnp.concatenate(parts, axis=1)


def tall(*parts):
    return jnp.concatenate(parts, axis=0)


def parts_of(x):
    high = x.astype(bf16)
    return high, (x - high.astype(f32)).astype(bf16)


def unpack_symmetric(which, blocks, diagonal, store):
    row, col = square_iotas()
    for (i, j, triangle), block in zip(HALVES[which], blocks):
        other = block.T
        if triangle:
            first = jnp.where(row < col, block, other)
            second = jnp.where(row > col, block, other)
            store(i, i, jnp.where(row == col, diagonal(i), first))
            store(j, j, jnp.where(row == col, diagonal(j), second))
        else:
            store(i, j, block)
            store(j, i, other)


def iterate_kernel(kept_a, arrived_a, kept_b, arrived_b, out_ref, gram_ref):
    row, col = square_iotas()

    def store(i, j, block):
        gram_ref[i * LANES : (i + 1) * LANES, j * LANES : (j + 1) * LANES] = block

    aux = None
    for which, kept, arrived in ((0, kept_a, arrived_a), (1, kept_b, arrived_b)):
        half = joined(load_half(kept, 0), decoded(which, arrived, 0))
        if aux is None:
            aux = half[0]
        unpack_symmetric(which, half[1:], lambda g: aux[g : g + 1], store)
    line = lax.broadcasted_iota(i32, (AUX, LANES), 0)
    squares = jnp.sum(jnp.where(line < 4, aux, 0.0), axis=0, keepdims=True)
    squares = jnp.sum(squares, axis=1, keepdims=True)
    inverse = 1.0 / (jnp.sqrt(squares) + 1e-07)
    gram = gram_ref[...] * inverse * inverse
    full_row = lax.broadcasted_iota(i32, (KV_RANK, KV_RANK), 0)
    full_col = lax.broadcasted_iota(i32, (KV_RANK, KV_RANK), 1)
    product = None
    for repeat in range(NS_ITERS):
        high, low = parts_of(gram)
        if repeat >= 2:
            square = mm(wide(high, high, low), tall(high, low, high))
        else:
            square = mm(high, high)
        mixing = (coef_second * gram + coef_third * square).astype(bf16)
        if product is None:
            product = jnp.where(full_row == full_col, coef_first, 0.0) + mixing.astype(f32)
        else:
            product_high, product_low = parts_of(product)
            product = coef_first * product + mm(wide(product_high, product_low), tall(mixing, mixing))
        if repeat < NS_ITERS - 1:
            half = coef_first * gram + mm(wide(high, low), tall(mixing, mixing))
            half_high, half_low = parts_of(half)
            gram = coef_first * half + mm(wide(mixing, mixing), tall(half_high, half_low))
    gram_ref[...] = product
    at = AUX_P
    for entries in HALVES:
        for i, j, triangle in entries:
            load = lambda i, j: gram_ref[i * LANES : (i + 1) * LANES, j * LANES : (j + 1) * LANES]
            if triangle:
                block = jnp.where(row <= col, load(i, i), load(j, j))
                block = 0.5 * (block + jnp.where(row <= col, load(i, i).T, load(j, j).T))
            else:
                block = 0.5 * (load(i, j) + load(j, i).T)
            out_ref[at : at + LANES, :] = block.astype(bf16)
            at += LANES

    def three(x):
        high = x.astype(bf16).astype(f32)
        middle = (x - high).astype(bf16).astype(f32)
        return high, middle, x - high - middle

    lines = [[], [], []]
    for i in range(BLOCKS):
        block = gram_ref[i * LANES : (i + 1) * LANES, i * LANES : (i + 1) * LANES]
        diagonal = jnp.sum(jnp.where(row == col, block, 0.0), axis=0, keepdims=True)
        for lines_of, part in zip(lines, three(diagonal)):
            lines_of.append(part)
    peaks = aux[4:5]
    tallies = aux[5:6]
    tally_high = tallies.astype(bf16).astype(f32)
    norm = three(jnp.broadcast_to(inverse, (1, LANES)))
    stacked = lines[0] + lines[1] + lines[2] + [peaks, tally_high, tallies - tally_high] + list(norm)
    place = lax.broadcasted_iota(i32, (AUX_P, LANES), 0)
    table = jnp.zeros((AUX_P, LANES), f32)
    for number, one in enumerate(stacked):
        table = jnp.where(place == number, one, table)
    out_ref[0:AUX_P, :] = table.astype(bf16)


def iterations(*args):
    return pl.pallas_call(
        iterate_kernel,
        in_specs=[pl.BlockSpec(memory_space=pltpu.VMEM)] * 4,
        out_specs=pl.BlockSpec(memory_space=pltpu.VMEM),
        out_shape=jax.ShapeDtypeStruct((ROWS_P, LANES), bf16),
        scratch_shapes=[pltpu.VMEM((KV_RANK, KV_RANK), f32)],
        compiler_params=params(),
        cost_estimate=pl.CostEstimate(
            flops=9 * NS_ITERS * 2 * KV_RANK**3, bytes_accessed=12 * HALF * LANES, transcendentals=0
        ),
        name="iterations",
    )(*args)


def apply_kernel(steps, spread, places, seats, number_of, me, counts, *refs):
    tables = refs[: number_of[0]]
    rows_in = refs[number_of[0] : sum(number_of)]
    weight_ref = refs[sum(number_of)]
    update_out, weight_out, mat_ref, update_ref, new_ref, leaving = refs[-6:]
    groups, rows_block = seats
    dp, expert = me[2] // groups, me[2] % groups
    capacity = weight_ref.shape[1]
    head_rows = NOPE + VDIM
    rms_scale = 0.2 * math.sqrt(max(KV_ROWS, KV_RANK))
    lane = lax.broadcasted_iota(i32, (1, LANES), 1)
    head_shift = head_rows.bit_length() - 1
    assert head_rows == 1 << head_shift and capacity % (16 * CHUNKS) == 0
    rows_of_slots = -(-capacity // LANES)
    slot = lax.broadcasted_iota(i32, (rows_of_slots, LANES), 0) * LANES
    slot = slot + lax.broadcasted_iota(i32, (rows_of_slots, LANES), 1)
    copies = []
    for step, pick in enumerate(steps):
        layer = layer_of(me, *pick)
        (place_a, start_a), (place_b, start_b) = spread[step]
        aux = tables[place_a][start_a : start_a + AUX_P, :].astype(f32)
        diagonal = [aux[i : i + 1] + aux[4 + i : 5 + i] + aux[8 + i : 9 + i] for i in range(BLOCKS)]
        inverse = [1.0 / line for line in diagonal]
        norm = (aux[15:16] + aux[16:17] + aux[17:18]) * rms_scale
        factor = jnp.sqrt(jnp.minimum(1.0, clip_limit / aux[12:13]))
        tallies = aux[13:14] + aux[14:15]

        def store(i, j, block):
            block = (block * inverse[j]).astype(bf16)
            mat_ref[step, i * LANES : (i + 1) * LANES, j * LANES : (j + 1) * LANES] = block

        for which, (place, start) in enumerate(((place_a, start_a + AUX_P), (place_b, start_b))):
            blocks = [
                tables[place][start + k * LANES : start + (k + 1) * LANES, :].astype(f32) for k in range(4)
            ]
            unpack_symmetric(which, blocks, lambda g: diagonal[g], store)
        lowest = dp * groups
        earlier = jnp.where((lane >= lowest) & (lane < lowest + expert), tallies, 0.0)
        base = jnp.sum(earlier, axis=1, keepdims=True).astype(i32) + dp * rows_block
        first_head = base >> head_shift
        row_index = base + slot
        head_of = row_index >> head_shift
        scale = jnp.ones(slot.shape, f32)
        for k in range((capacity - 1) // head_rows + 2):
            one = jnp.sum(jnp.where(lane == first_head + k, factor, 0.0), axis=1, keepdims=True)
            scale = jnp.where(head_of == first_head + k, one, scale)
        scale = jnp.where((row_index & (head_rows - 1)) < NOPE, scale, 1.0)
        scale = jnp.where(slot < counts[layer], scale, 0.0)
        columns = [jnp.broadcast_to(scale[k : k + 1], (LANES, LANES)).T for k in range(slot.shape[0])]
        scale = jnp.concatenate(columns, axis=0)[:capacity]
        kept = scale * (1.0 - learn_rate * decay_rate)
        moved = scale * learn_rate
        source, index = places[step]
        for chunk in range(CHUNKS):
            size = capacity // CHUNKS
            among = slice(chunk * size, (chunk + 1) * size)
            product = mm(rows_in[source][index, among, :], mat_ref[step])
            for i in range(BLOCKS):
                span = slice(i * LANES, (i + 1) * LANES)
                update = product[:, span] * (diagonal[i] * norm)
                update_ref[step, among, span] = update.astype(bf16)
                weight = weight_ref[layer, among, span].astype(f32)
                new_ref[step, among, span] = (weight * kept[among] - update * moved[among]).astype(bf16)
            at = pl.ds(chunk * size, size)
            for number, (held, out) in enumerate(((update_ref, update_out), (new_ref, weight_out))):
                copy = pltpu.make_async_copy(
                    held.at[step, at], out.at[layer, at], leaving.at[number, step * CHUNKS + chunk]
                )
                copy.start()
                copies.append(copy)
    for copy in copies:
        copy.wait()


def apply_rows(steps, spread, places, seats, me, counts, tables, rows, weight, *outs):
    number = len(steps)
    layers, capacity, features = weight.shape
    smem = pl.BlockSpec(memory_space=pltpu.SMEM)
    vmem = pl.BlockSpec(memory_space=pltpu.VMEM)
    hbm = pl.BlockSpec(memory_space=pltpu.HBM)
    args = [me, counts] + list(tables) + list(rows) + [weight] + list(outs)
    shape = jax.ShapeDtypeStruct((layers, capacity, features), bf16)
    return pl.pallas_call(
        functools.partial(apply_kernel, steps, spread, places, seats, (len(tables), len(rows))),
        in_specs=[smem, smem] + [vmem] * (len(tables) + len(rows) + 1) + [hbm] * len(outs),
        out_specs=[hbm, hbm],
        out_shape=[shape, shape],
        scratch_shapes=[
            pltpu.VMEM((number, KV_RANK, KV_RANK), bf16),
            pltpu.VMEM((number, capacity, features), bf16),
            pltpu.VMEM((number, capacity, features), bf16),
            pltpu.SemaphoreType.DMA((2, number * CHUNKS)),
        ],
        input_output_aliases={len(args) - 2: 0, len(args) - 1: 1} if outs else {},
        compiler_params=params(),
        cost_estimate=pl.CostEstimate(
            flops=number * capacity * features * features * 2,
            bytes_accessed=number * capacity * features * 8,
            transcendentals=0,
        ),
        name="apply_rows",
    )(*args)


def local(dp_size, expert_size, grad_rows, momentum_rows, weight_rows, row_counts, logit_peaks):
    layers = grad_rows.shape[1]
    expert_bits = expert_size.bit_length() - 1
    bits = expert_bits - 1
    assert layers == expert_size == 1 << expert_bits and bits >= 2
    assert dp_size == 4 and dp_size * expert_size <= LANES
    dp = lax.axis_index("dp")
    expert = lax.axis_index("expert")
    counts = row_counts.reshape(layers)
    owner = ((dp >> 1) << (bits - 1)) | ((expert >> 1) & ((1 << (bits - 1)) - 1))
    me = jnp.stack([owner, expert & 1, dp * expert_size + expert]).astype(i32)
    owner_axes = [("expert", 1 << (p + 1)) for p in range(bits - 1)] + [("dp", 2)]
    copy_axes = [("dp", 1), ("expert", 1 << (expert_bits - 1))]
    sizes = {"dp": dp_size, "expert": expert_size}

    def over(x, axis_bit):
        axis, bit = axis_bit
        return lax.ppermute(x, axis, [(i, i ^ bit) for i in range(sizes[axis])])

    core_axis = ("expert", 1)
    grad, mom, peaks = grad_rows[0], momentum_rows[0], logit_peaks[0, 0]
    codes = lambda n: jax.ShapeDtypeStruct((n, HALF_CODE, LANES), i16)
    plain = lambda n: jax.ShapeDtypeStruct((n, HALF, LANES), f32)
    both = lambda n: jax.ShapeDtypeStruct((n, 2 * HALF, LANES), f32)
    every = list(range((1 << bits) - 1, 0, -1))
    orders = (list(range(bits - 1, -1, -1)), list(range(bits)))
    sent = [[r for r in range(1 << bits) if r >> orders[w][0] & 1] for w in range(2)]
    current = [[r for r in range(1 << bits) if r not in sent[w]] for w in range(2)]
    stays = [current[w][1:] for w in range(2)]
    message_of = [
        [(True, sent[w].index(r)) if r in sent[w] else (False, stays[w].index(r)) for r in every] for w in range(2)
    ]
    shapes = [shape for w in range(2) for shape in (codes(len(sent[w])), plain(len(stays[w])))]

    sources = (counts, grad, mom, peaks)
    rows_other, other = gram_parts([(r, False) for r in every], [both(len(every))], me, *sources)
    rows_own, own = gram_parts([(r, True) for r in every], [both(len(every))], me, *sources)
    out = list(
        local_call(functools.partial(first_kernel, message_of), shapes, "sum0", own, over(other, core_axis))
    )
    out[0], out[2], me_late = lax.optimization_barrier((out[0], out[2], me))
    rows_zero, *halves = gram_parts([(0, False), (0, True)], [plain(1)] * 4, me_late, *sources)
    late = halves[2:] + [over(x, core_axis) for x in halves[:2]]
    axes = [owner_axes[orders[w][0]] for w in range(2)]
    state = [out[1], over(out[0], axes[0]), out[3], over(out[2], axes[1])]
    for step in range(1, bits + 2):
        if step < bits:
            axes = [owner_axes[orders[w][step]] for w in range(2)]
            sends = [[k for k, r in enumerate(current[w]) if r >> orders[w][step] & 1] for w in range(2)]
            keeps = [[k for k in range(len(current[w])) if k not in sends[w]] for w in range(2)]
            current = [[current[w][k] for k in keeps[w]] for w in range(2)]
        else:
            axes = [copy_axes[step - bits], copy_axes[1 - (step - bits)]]
            sends = keeps = [[0], [0]]
        shapes = [s for w in range(2) for s in (codes(len(sends[w])), plain(len(keeps[w])))]
        kernel = functools.partial(sum_kernel, sends, keeps, bool(late))
        out = local_call(kernel, shapes, "sum" + str(step), *state, *late)
        late = []
        state = [out[1], over(out[0], axes[0]), out[3], over(out[2], axes[1])]
    table = iterations(*state)

    seats = (expert_size, KV_ROWS // dp_size)
    weight = weight_rows[0]
    full = lambda place: ((place, 0), (place, HEAD_P))

    def apply(picks, spread, tables, *outs):
        if picks[0][0] == 0:
            rows, places = [rows_zero], [(0, 1 if own_core else 0) for _, own_core in picks]
        else:
            rows = [rows_own, rows_other]
            places = [(0 if own_core else 1, every.index(r)) for r, own_core in picks]
        return apply_rows(picks, spread, places, seats, me, counts, tables, rows, weight, *outs)

    tables = {0: table}
    for position in range(bits - 1, -1, -1) if bits > 2 else ():
        for known in list(tables):
            tables[known | 1 << position] = over(tables[known], owner_axes[position])
    if bits == 2:
        tables[2], tables[1] = over(table, owner_axes[1]), over(table, owner_axes[0])
    pair = [table, over(table, core_axis)]
    outs = apply(((0, True), (0, False)), (full(0), full(1)), pair)
    if bits == 2:
        tables[1], tables[2], outs = lax.optimization_barrier((tables[1], tables[2], outs))
        tail = [over(tables[1][:HEAD_P], owner_axes[1]), over(tables[2][HEAD_P:], owner_axes[0])]
        near = [tables[1], tables[2]]
        near += [over(x, core_axis) for x in near]
        outs = apply(((1, True), (2, True), (1, False), (2, False)), tuple(full(k) for k in range(4)), near, *outs)
        tail, outs = lax.optimization_barrier((tail, outs))
        tail += [over(x, core_axis) for x in tail]
        spread = (((0, 0), (1, 0)), ((2, 0), (3, 0)))
        outs = apply(((3, True), (3, False)), spread, tail, *outs)
    else:
        for relative in range(1, 1 << bits):
            pair = [tables[relative], over(tables[relative], core_axis)]
            outs = apply(((relative, True), (relative, False)), (full(0), full(1)), pair, *outs)
    return (outs[0][None], outs[1][None])


def solution(mesh):
    return jax.shard_map(
        functools.partial(local, mesh.shape["dp"], mesh.shape["expert"]),
        mesh=mesh,
        in_specs=(
            P("dp", None, "expert", None),
            P("dp", None, "expert", None),
            P("dp", None, "expert", None),
            P("dp", None, "expert"),
            P("dp", "expert", None, None),
        ),
        out_specs=(P("dp", None, "expert", None), P("dp", None, "expert", None)),
        check_vma=False,
    )
```

```python
import functools
import math

import jax
import jax.numpy as jnp
from jax import lax
from jax.experimental import pallas as pl
from jax.experimental.pallas import tpu as pltpu
from jax.sharding import PartitionSpec as P

KV_RANK = 512
NOPE = 128
VDIM = 128
NS_ITERS = 5
KV_ROWS = 16384

momentum_coef = 0.95
learn_rate = 0.02
decay_rate = 0.1
clip_limit = 100.0
coef_first = 3.4445
coef_second = -4.775
coef_third = 2.0315

f32 = jnp.float32
bf16 = jnp.bfloat16
i16 = jnp.int16
i32 = jnp.int32

LANES = 128
BLOCKS = KV_RANK // LANES
HALVES = (
    ((0, 1, True), (0, 1, False), (0, 2, False), (1, 2, False)),
    ((2, 3, True), (0, 3, False), (1, 3, False), (2, 3, False)),
)
AUX = 8
HALF = AUX + 4 * LANES
AUX_CODE = 16
HALF_CODE = AUX_CODE + 4 * LANES
AUX_P = 32
HEAD_P = AUX_P + 4 * LANES
ROWS_P = AUX_P + 8 * LANES
UNIT = 32000.0
CHUNKS = 2


SHORT = pl.CostEstimate(flops=1000, bytes_accessed=1000, transcendentals=0)


def params(mebibytes=40):
    return pltpu.CompilerParams(vmem_limit_bytes=mebibytes * 1024 * 1024)


def pinned(x):
    return pltpu.with_memory_space_constraint(x, pltpu.HBM)


def square_iotas():
    row = lax.broadcasted_iota(i32, (LANES, LANES), 0)
    col = lax.broadcasted_iota(i32, (LANES, LANES), 1)
    return row, col


def owner_bits(expert_size):
    return expert_size.bit_length() - 2


def place_of(expert_size):
    bits = owner_bits(expert_size)
    dp = lax.axis_index("dp").astype(i32)
    expert = lax.axis_index("expert").astype(i32)
    owner = ((dp >> 1) << (bits - 1)) | ((expert >> 1) & ((1 << (bits - 1)) - 1))
    return owner, expert & 1, dp * expert_size + expert


def layer_of(place, relative, own_core):
    core = place[1] if own_core else 1 - place[1]
    if isinstance(relative, tuple):
        relative = jnp.where(core == 0, relative[0], relative[1])
    return 2 * (place[0] ^ relative) + core


def gram_kernel(expert_size, picks, later, first, *refs):
    grad_ref, mom_ref = refs[:2]
    place = place_of(expert_size)
    if first:
        counts_ref, peaks_ref = refs[2:4]
        counts, peaks_buf, grad_buf, mom_buf, arrivals, own_arrivals, small_arrivals = refs[-7:]
        outs = refs[4:-7]
        facts_ref, outs = outs[0], outs[1:]
    else:
        facts_ref, grad_buf, mom_buf = refs[2:5]
        arrivals = refs[-1]
        outs = refs[5:-1]
    nes_ref, outs = outs[0], outs[1:]
    gram_refs, loads = outs[: 2 * len(picks)], outs[2 * len(picks) :]
    layers = [layer_of(place, *pick) for pick in picks]

    def copies_of(chosen, buffers, semaphores):
        return [
            pltpu.make_async_copy(source.at[layer], buffer.at[k], semaphores.at[n, k])
            for k, layer in enumerate(chosen)
            for n, (source, buffer) in enumerate(((grad_ref, buffers[0]), (mom_ref, buffers[1])))
        ]

    own_copies = copies_of(layers, (grad_buf, mom_buf), own_arrivals) if first else []
    small = []
    if first:
        small = [
            pltpu.make_async_copy(counts_ref, counts, small_arrivals.at[0]),
            pltpu.make_async_copy(peaks_ref, peaks_buf, small_arrivals.at[1]),
        ]
    late_copies = copies_of([layer_of(place, *pick) for pick in later], loads, arrivals) if later else []
    for copy in small + own_copies + late_copies:
        copy.start()
    row, col = square_iotas()
    line = lax.broadcasted_iota(i32, (AUX, LANES), 0)
    lane = lax.broadcasted_iota(i32, (AUX, LANES), 1)
    if first:
        for copy in small:
            copy.wait()
        every_peak = peaks_buf[...].astype(f32)
        every_peak = jnp.concatenate(
            [every_peak, jnp.zeros((every_peak.shape[0], LANES - every_peak.shape[1]), f32)], axis=1
        )
        for layer in range(every_peak.shape[0]):
            count = counts[layer].astype(f32)
            fact = jnp.where(line == 4, every_peak[layer : layer + 1], jnp.zeros((AUX, LANES), f32))
            fact = jnp.where((line == 6) | ((line == 5) & (lane == place[2])), count, fact)
            facts_ref[layer] = fact
    width = KV_RANK // 2
    dims = (((0,), (0,)), ((), ()))
    slot = lax.broadcasted_iota(i32, (grad_buf.shape[1], LANES), 0)

    def form_rows(k):
        for copy in own_copies[2 * k : 2 * k + 2]:
            copy.wait()
        live = slot < facts_ref[layers[k], 6:7, :].astype(i32)
        for i in range(BLOCKS):
            span = slice(i * LANES, (i + 1) * LANES)
            gradient = grad_buf[k, :, span].astype(f32)
            velocity = momentum_coef * mom_buf[k, :, span].astype(f32) + gradient
            nesterov = gradient + momentum_coef * velocity
            nes_ref[k, :, span] = jnp.where(live, nesterov, 0.0).astype(bf16)

    form_rows(0)
    for k, layer in enumerate(layers):
        if k + 1 < len(layers):
            form_rows(k + 1)
        rows = nes_ref[k]
        upper = lax.dot_general(rows[:, :width], rows, dims, preferred_element_type=f32)
        lower = lax.dot_general(rows[:, width:], rows[:, width:], dims, preferred_element_type=f32)

        def block(i, j):
            if i < 2:
                return upper[i * LANES : (i + 1) * LANES, j * LANES : (j + 1) * LANES]
            return lower[(i - 2) * LANES : (i - 1) * LANES, (j - 2) * LANES : (j - 1) * LANES]

        aux = jnp.where(line == 6, 0.0, facts_ref[layer])
        for i in range(BLOCKS):
            diagonal = jnp.sum(jnp.where(row == col, block(i, i), 0.0), axis=0, keepdims=True)
            aux = jnp.where(line == i, diagonal, aux)
        for which, entries in enumerate(HALVES):
            half = [aux]
            for i, j, triangle in entries:
                half.append(jnp.where(row <= col, block(i, i), block(j, j)) if triangle else block(i, j))
            store_half(gram_refs[2 * k + which], 0, half)
    for copy in late_copies:
        copy.wait()


def gram_parts(expert_size, picks, later, sources, facts=None, loaded=()):
    grad, mom, counts, peaks = sources
    layers, capacity, features = grad.shape
    first = facts is None
    number = len(picks)
    vmem = pl.BlockSpec(memory_space=pltpu.VMEM)
    hbm = pl.BlockSpec(memory_space=pltpu.HBM)
    rows = lambda n: jax.ShapeDtypeStruct((n, capacity, features), bf16)
    out_shapes = [jax.ShapeDtypeStruct((layers, AUX, LANES), f32)] if first else []
    out_shapes += [rows(number)] + [jax.ShapeDtypeStruct((1, HALF, LANES), f32)] * (2 * number)
    out_shapes += [rows(len(later))] * 2 if later else []
    args = [pinned(grad), pinned(mom)]
    args += [pinned(counts), pinned(peaks)] if first else [facts] + list(loaded)
    scratch = []
    if first:
        scratch += [pltpu.SMEM(counts.shape, i32), pltpu.VMEM(peaks.shape, bf16)]
        scratch += [pltpu.VMEM((number, capacity, features), bf16)] * 2
    scratch += [pltpu.SemaphoreType.DMA((2, max(len(later), 1)))]
    if first:
        scratch += [pltpu.SemaphoreType.DMA((2, number)), pltpu.SemaphoreType.DMA((2,))]
    out = pl.pallas_call(
        functools.partial(gram_kernel, expert_size, picks, later, first),
        in_specs=[hbm] * (4 if first else 2) + [vmem] * (0 if first else 3),
        out_specs=[vmem] * len(out_shapes),
        out_shape=out_shapes,
        scratch_shapes=scratch,
        compiler_params=params(),
        cost_estimate=SHORT,
        name="gram_parts",
    )(*args)
    if first:
        facts, out = out[0], out[1:]
    halves = [list(out[at : at + 2]) for at in range(1, 1 + 2 * number, 2)]
    return facts, out[0], halves, tuple(out[1 + 2 * number :])


def joined(first, second):
    line = lax.broadcasted_iota(i32, (AUX, LANES), 0)
    aux = jnp.where(line == 4, jnp.maximum(first[0], second[0]), first[0] + second[0])
    return [aux] + [x + y for x, y in zip(first[1:], second[1:])]


def load_half(ref, index, base=0):
    starts = [base + AUX + place * LANES for place in range(4)]
    return [ref[index, base : base + AUX, :]] + [ref[index, at : at + LANES, :] for at in starts]


def store_half(ref, index, half, base=0):
    ref[index, base : base + AUX, :] = half[0]
    for place in range(4):
        at = base + AUX + place * LANES
        ref[index, at : at + LANES, :] = half[1 + place]


def outer_scales(which, scale):
    row, col = square_iotas()
    across = [scale[g : g + 1] for g in range(BLOCKS)]
    down = {}

    def outer(i, j):
        if i not in down:
            down[i] = jnp.broadcast_to(across[i], (LANES, LANES)).T
        return down[i] * across[j]

    return [
        jnp.where(row <= col, outer(i, i), outer(j, j)) if triangle else outer(i, j)
        for i, j, triangle in HALVES[which]
    ]


def decoded(which, ref, index, base=0):
    line = lax.broadcasted_iota(i32, (AUX, LANES), 0)
    codes = ref[index, base : base + AUX_CODE, :].astype(i32).astype(f32)
    low, high = codes[0:AUX], codes[AUX:AUX_CODE]
    scale = jnp.where(line < 4, jnp.exp2(low) * jnp.sqrt(high * (1.0 / UNIT)), 0.0)
    aux = jnp.where(line < 4, scale * scale, jnp.where(line == 4, low * (1.0 / 64.0), low))
    half = [aux]
    for place, factor in enumerate(outer_scales(which, scale)):
        at = base + AUX_CODE + place * LANES
        half.append(ref[index, at : at + LANES, :].astype(i32).astype(f32) * (factor * (1.0 / UNIT)))
    return half


def encode(which, ref, index, half, base=0):
    line = lax.broadcasted_iota(i32, (AUX, LANES), 0)
    aux = half[0]
    diagonal = jnp.maximum(aux, 1e-30)
    power = jnp.ceil(0.5 * jnp.log2(diagonal))
    high = jnp.clip(jnp.floor(diagonal * jnp.exp2(-2.0 * power) * UNIT + 0.5), 1.0, 32767.0)
    low = jnp.where(line < 4, power, jnp.where(line == 4, jnp.floor(aux * 64.0 + 0.5), aux))
    high = jnp.where(line < 4, high, 0.0)
    ref[index, base : base + AUX_CODE, :] = jnp.concatenate([low, high], axis=0).astype(i32).astype(i16)
    inverse = jnp.where(line < 4, jnp.exp2(-power) * lax.rsqrt(high * (1.0 / UNIT)), 0.0)
    for place, factor in enumerate(outer_scales(which, inverse)):
        at = base + AUX_CODE + place * LANES
        value = jnp.floor(half[1 + place] * (factor * UNIT) + 0.5)
        value = jnp.clip(value, -32767.0, 32767.0)
        ref[index, at : at + LANES, :] = value.astype(i32).astype(i16)


def local_call(kernel, out_shapes, name, *args):
    return pl.pallas_call(
        kernel,
        in_specs=[pl.BlockSpec(memory_space=pltpu.VMEM)] * len(args),
        out_specs=[pl.BlockSpec(memory_space=pltpu.VMEM)] * len(out_shapes),
        out_shape=list(out_shapes),
        compiler_params=params(),
        cost_estimate=SHORT,
        name=name,
    )(*args)


def send_kernel(number, *refs):
    for k in range(number):
        own, partner, message = refs[4 * k : 4 * k + 2], refs[4 * k + 2 : 4 * k + 4], refs[4 * number + k]
        for which in range(2):
            half = joined(load_half(own[which], 0), load_half(partner[which], 0))
            encode(which, message, 0, half, which * HALF_CODE)


def gather_kernel(*refs):
    messages, outs, stay = refs[4:-3], refs[-3:-1], refs[-1]
    for which in range(2):
        half = joined(load_half(refs[which], 0), load_half(refs[2 + which], 0))
        for arrived in messages:
            half = joined(half, decoded(which, arrived, 0, which * HALF_CODE))
        encode(which, outs[which], 0, half)
        store_half(stay, 0, half, which * HALF)


def sum_kernel(kept, arrived_a, arrived_b, *refs):
    outs, stay = refs[:2], refs[2]
    for which, arrived in enumerate((arrived_a, arrived_b)):
        half = joined(load_half(kept, 0, which * HALF), decoded(which, arrived, 0))
        encode(which, outs[which], 0, half)
        store_half(stay, 0, half, which * HALF)


def mm(x, y):
    return jnp.dot(x, y, preferred_element_type=f32)


def wide(*parts):
    return jnp.concatenate(parts, axis=1)


def tall(*parts):
    return jnp.concatenate(parts, axis=0)


def parts_of(x):
    high = x.astype(bf16)
    return high, (x - high.astype(f32)).astype(bf16)


def unpack_symmetric(which, blocks, diagonal, store):
    row, col = square_iotas()
    for (i, j, triangle), block in zip(HALVES[which], blocks):
        other = block.T
        if triangle:
            first = jnp.where(row < col, block, other)
            second = jnp.where(row > col, block, other)
            store(i, i, jnp.where(row == col, diagonal(i), first))
            store(j, j, jnp.where(row == col, diagonal(j), second))
        else:
            store(i, j, block)
            store(j, i, other)


def iterate_kernel(kept, arrived_a, arrived_b, out_ref, gram_ref):
    row, col = square_iotas()

    def store(i, j, block):
        gram_ref[i * LANES : (i + 1) * LANES, j * LANES : (j + 1) * LANES] = block

    aux = None
    for which, arrived in enumerate((arrived_a, arrived_b)):
        half = joined(load_half(kept, 0, which * HALF), decoded(which, arrived, 0))
        if aux is None:
            aux = half[0]
        unpack_symmetric(which, half[1:], lambda g: aux[g : g + 1], store)
    line = lax.broadcasted_iota(i32, (AUX, LANES), 0)
    squares = jnp.sum(jnp.where(line < 4, aux, 0.0), axis=0, keepdims=True)
    squares = jnp.sum(squares, axis=1, keepdims=True)
    inverse = 1.0 / (jnp.sqrt(squares) + 1e-07)
    gram = gram_ref[...] * inverse * inverse
    full_row = lax.broadcasted_iota(i32, (KV_RANK, KV_RANK), 0)
    full_col = lax.broadcasted_iota(i32, (KV_RANK, KV_RANK), 1)
    product = None
    for repeat in range(NS_ITERS):
        high, low = parts_of(gram)
        if repeat >= 2:
            square = mm(wide(high, high, low), tall(high, low, high))
        else:
            square = mm(high, high)
        mixing = (coef_second * gram + coef_third * square).astype(bf16)
        if product is None:
            product = jnp.where(full_row == full_col, coef_first, 0.0) + mixing.astype(f32)
        else:
            product_high, product_low = parts_of(product)
            product = coef_first * product + mm(wide(product_high, product_low), tall(mixing, mixing))
        if repeat < NS_ITERS - 1:
            half = coef_first * gram + mm(wide(high, low), tall(mixing, mixing))
            half_high, half_low = parts_of(half)
            gram = coef_first * half + mm(wide(mixing, mixing), tall(half_high, half_low))
    gram_ref[...] = product
    at = AUX_P
    for entries in HALVES:
        for i, j, triangle in entries:
            load = lambda i, j: gram_ref[i * LANES : (i + 1) * LANES, j * LANES : (j + 1) * LANES]
            if triangle:
                block = jnp.where(row <= col, load(i, i), load(j, j))
                block = 0.5 * (block + jnp.where(row <= col, load(i, i).T, load(j, j).T))
            else:
                block = 0.5 * (load(i, j) + load(j, i).T)
            out_ref[at : at + LANES, :] = block.astype(bf16)
            at += LANES

    def three(x):
        high = x.astype(bf16).astype(f32)
        middle = (x - high).astype(bf16).astype(f32)
        return high, middle, x - high - middle

    lines = [[], [], []]
    for i in range(BLOCKS):
        block = gram_ref[i * LANES : (i + 1) * LANES, i * LANES : (i + 1) * LANES]
        diagonal = jnp.sum(jnp.where(row == col, block, 0.0), axis=0, keepdims=True)
        for lines_of, part in zip(lines, three(diagonal)):
            lines_of.append(part)
    peaks = aux[4:5]
    tallies = aux[5:6]
    tally_high = tallies.astype(bf16).astype(f32)
    norm = three(jnp.broadcast_to(inverse, (1, LANES)))
    stacked = lines[0] + lines[1] + lines[2] + [peaks, tally_high, tallies - tally_high] + list(norm)
    place = lax.broadcasted_iota(i32, (AUX_P, LANES), 0)
    table = jnp.zeros((AUX_P, LANES), f32)
    for number, one in enumerate(stacked):
        table = jnp.where(place == number, one, table)
    out_ref[0:AUX_P, :] = table.astype(bf16)


def iterations(*args):
    return pl.pallas_call(
        iterate_kernel,
        in_specs=[pl.BlockSpec(memory_space=pltpu.VMEM)] * 3,
        out_specs=pl.BlockSpec(memory_space=pltpu.VMEM),
        out_shape=jax.ShapeDtypeStruct((ROWS_P, LANES), bf16),
        scratch_shapes=[pltpu.VMEM((KV_RANK, KV_RANK), f32)],
        compiler_params=params(),
        cost_estimate=SHORT,
        name="iterations",
    )(*args)


def apply_kernel(steps, spread, places, seats, number_of, *refs):
    tables = refs[: number_of[0]]
    rows_in = refs[number_of[0] : sum(number_of)]
    weight_ref = refs[sum(number_of)]
    update_out, weight_out, mat_ref, update_ref, new_ref, leaving = refs[-6:]
    groups, rows_block = seats
    here = place_of(groups)
    dp = lax.axis_index("dp").astype(i32)
    capacity = weight_ref.shape[1]
    head_rows = NOPE + VDIM
    rms_scale = 0.2 * math.sqrt(max(KV_ROWS, KV_RANK))
    lane = lax.broadcasted_iota(i32, (1, LANES), 1)
    head_shift = head_rows.bit_length() - 1
    assert head_rows == 1 << head_shift and capacity % (16 * CHUNKS) == 0
    rows_of_slots = -(-capacity // LANES)
    slot = lax.broadcasted_iota(i32, (rows_of_slots, LANES), 0) * LANES
    slot = slot + lax.broadcasted_iota(i32, (rows_of_slots, LANES), 1)
    copies = []
    for step, pick in enumerate(steps):
        layer = layer_of(here, *pick)
        (place_a, start_a), (place_b, start_b) = spread[step]
        aux = tables[place_a][start_a : start_a + AUX_P, :].astype(f32)
        diagonal = [aux[i : i + 1] + aux[4 + i : 5 + i] + aux[8 + i : 9 + i] for i in range(BLOCKS)]
        inverse = [1.0 / line for line in diagonal]
        norm = (aux[15:16] + aux[16:17] + aux[17:18]) * rms_scale
        factor = jnp.sqrt(jnp.minimum(1.0, clip_limit / aux[12:13]))
        tallies = aux[13:14] + aux[14:15]

        def store(i, j, block):
            block = (block * inverse[j]).astype(bf16)
            mat_ref[step, i * LANES : (i + 1) * LANES, j * LANES : (j + 1) * LANES] = block

        for which, (place, start) in enumerate(((place_a, start_a + AUX_P), (place_b, start_b))):
            blocks = [
                tables[place][start + k * LANES : start + (k + 1) * LANES, :].astype(f32) for k in range(4)
            ]
            unpack_symmetric(which, blocks, lambda g: diagonal[g], store)
        lowest = dp * groups
        earlier = jnp.where((lane >= lowest) & (lane < here[2]), tallies, 0.0)
        base = jnp.sum(earlier, axis=1, keepdims=True).astype(i32) + dp * rows_block
        first_head = base >> head_shift
        row_index = base + slot
        head_of = row_index >> head_shift
        scale = jnp.ones(slot.shape, f32)
        for k in range((capacity - 1) // head_rows + 2):
            one = jnp.sum(jnp.where(lane == first_head + k, factor, 0.0), axis=1, keepdims=True)
            scale = jnp.where(head_of == first_head + k, one, scale)
        scale = jnp.where((row_index & (head_rows - 1)) < NOPE, scale, 1.0)
        count = jnp.sum(jnp.where(lane == here[2], tallies, 0.0), axis=1, keepdims=True).astype(i32)
        scale = jnp.where(slot < count, scale, 0.0)
        columns = [jnp.broadcast_to(scale[k : k + 1], (LANES, LANES)).T for k in range(slot.shape[0])]
        scale = jnp.concatenate(columns, axis=0)[:capacity]
        kept = scale * (1.0 - learn_rate * decay_rate)
        moved = scale * learn_rate
        source, index = places[step]
        if isinstance(index, tuple):
            core = here[1] if pick[1] else 1 - here[1]
            index = jnp.where(core == 0, index[0], index[1])
        for chunk in range(CHUNKS):
            size = capacity // CHUNKS
            among = slice(chunk * size, (chunk + 1) * size)
            product = mm(rows_in[source][index, among, :], mat_ref[step])
            for i in range(BLOCKS):
                span = slice(i * LANES, (i + 1) * LANES)
                update = product[:, span] * (diagonal[i] * norm)
                update_ref[step, among, span] = update.astype(bf16)
                weight = weight_ref[layer, among, span].astype(f32)
                new_ref[step, among, span] = (weight * kept[among] - update * moved[among]).astype(bf16)
            at = pl.ds(chunk * size, size)
            for number, (held, out) in enumerate(((update_ref, update_out), (new_ref, weight_out))):
                copy = pltpu.make_async_copy(
                    held.at[step, at], out.at[layer, at], leaving.at[number, step * CHUNKS + chunk]
                )
                copy.start()
                copies.append(copy)
    for copy in copies:
        copy.wait()


def apply_rows(steps, spread, places, seats, tables, rows, weight, *outs):
    number = len(steps)
    layers, capacity, features = weight.shape
    vmem = pl.BlockSpec(memory_space=pltpu.VMEM)
    hbm = pl.BlockSpec(memory_space=pltpu.HBM)
    args = list(tables) + list(rows) + [weight] + list(outs)
    shape = jax.ShapeDtypeStruct((layers, capacity, features), bf16)
    return pl.pallas_call(
        functools.partial(apply_kernel, steps, spread, places, seats, (len(tables), len(rows))),
        in_specs=[vmem] * (len(tables) + len(rows) + 1) + [hbm] * len(outs),
        out_specs=[hbm, hbm],
        out_shape=[shape, shape],
        scratch_shapes=[
            pltpu.VMEM((number, KV_RANK, KV_RANK), bf16),
            pltpu.VMEM((number, capacity, features), bf16),
            pltpu.VMEM((number, capacity, features), bf16),
            pltpu.SemaphoreType.DMA((2, number * CHUNKS)),
        ],
        input_output_aliases={len(args) - 2: 0, len(args) - 1: 1} if outs else {},
        compiler_params=params(),
        cost_estimate=SHORT,
        name="apply_rows",
    )(*args)


def local(dp_size, expert_size, grad_rows, momentum_rows, weight_rows, row_counts, logit_peaks):
    layers = grad_rows.shape[1]
    bits = owner_bits(expert_size)
    assert layers == expert_size == 2 << bits and bits >= 2
    assert dp_size == 4 and dp_size * expert_size <= LANES
    sources = (grad_rows[0], momentum_rows[0], row_counts.reshape(layers), logit_peaks[0, 0])

    def over(x, mask):
        everyone = range(dp_size * expert_size)
        return lax.ppermute(x, ("dp", "expert"), [(i, i ^ mask) for i in everyone])

    across_core = 1
    owner_masks = [2 << p for p in range(bits - 1)] + [2 * expert_size]
    copy_masks = [expert_size, expert_size // 2]

    def mask_of(relative):
        return sum(mask for p, mask in enumerate(owner_masks) if relative >> p & 1)

    def by_core(x, even, odd):
        everyone = range(dp_size * expert_size)
        return lax.ppermute(x, ("dp", "expert"), [(i, i ^ (odd if i & 1 else even)) for i in everyone])

    most = (1 << bits) - 1
    others = list(range(most - 1, 0, -1))
    turns = [
        [(most, False)],
        [(most, True)] + [(r, False) for r in others],
        [(r, True) for r in others],
        [(0, False), (0, True)],
    ]
    rows, partial, messages = {}, {}, []
    facts, loaded = None, ()
    message_shape = jax.ShapeDtypeStruct((1, 2 * HALF_CODE, LANES), i16)
    for number, turn in enumerate(turns):
        later = turns[number + 1] if number + 1 < len(turns) else []
        if messages and not later:
            loaded, messages[0] = lax.optimization_barrier((loaded, messages[0]))
        facts, made, grams, loaded = gram_parts(expert_size, turn, later, sources, facts, loaded)
        for index, (pick, gram) in enumerate(zip(turn, grams)):
            rows[pick] = (made, index)
            partial[pick] = gram if pick[1] else [over(half, across_core) for half in gram]
        ready = ([], [most], others, [])[number]
        if ready:
            sums = [half for r in ready for half in partial[r, True] + partial[r, False]]
            kernel = functools.partial(send_kernel, len(ready))
            made = local_call(kernel, [message_shape] * len(ready), "send", *sums)
            made, loaded = lax.optimization_barrier((made, loaded))
            messages += [over(message, mask_of(r)) for r, message in zip(ready, made)]
    codes = jax.ShapeDtypeStruct((1, HALF_CODE, LANES), i16)
    shapes = [codes, codes, jax.ShapeDtypeStruct((1, 2 * HALF, LANES), f32)]
    out = local_call(gather_kernel, shapes, "gather", *partial[0, True], *partial[0, False], *messages)
    state = [out[2], over(out[0], copy_masks[0]), over(out[1], copy_masks[1])]
    out = local_call(sum_kernel, shapes, "sum", *state)
    state = [out[2], over(out[0], copy_masks[1]), over(out[1], copy_masks[0])]
    table = iterations(*state)

    seats = (expert_size, KV_ROWS // dp_size)
    weight = weight_rows[0]
    full = lambda place: ((place, 0), (place, HEAD_P))

    def apply(picks, tables, *outs):
        arrays, places = [], []
        for relative, own_core in picks:
            found = [rows[r, own_core] for r in (relative if isinstance(relative, tuple) else (relative,))]
            if not any(array is found[0][0] for array in arrays):
                arrays.append(found[0][0])
            (source,) = [k for k, array in enumerate(arrays) if array is found[0][0]]
            assert all(made is arrays[source] for made, _ in found)
            indices = tuple(index for _, index in found)
            places.append((source, indices if len(indices) > 1 else indices[0]))
        spread = tuple(full(k) for k in range(len(tables)))
        return apply_rows(tuple(picks), spread, places, seats, tables, arrays, weight, *outs)

    if bits == 2:
        first = by_core(table, owner_masks[1], owner_masks[0])
        second = by_core(table, owner_masks[0], owner_masks[1])
        table, first, second = lax.optimization_barrier((table, first, second))
        last = by_core(second, owner_masks[1], owner_masks[0])
        known, relatives = [table, first, second], [0, (2, 1), (1, 2)]
        outs = apply([(r, True) for r in relatives], known)
        outs = apply([(r, False) for r in relatives], [over(x, across_core) for x in known], *outs)
        last, outs = lax.optimization_barrier((last, outs))
        outs = apply(((3, True), (3, False)), [last, over(last, across_core)], *outs)
    else:
        outs = apply(((0, True), (0, False)), [table, over(table, across_core)])
        tables = {0: table}
        for position in range(bits - 1, -1, -1):
            for known in list(tables):
                tables[known | 1 << position] = over(tables[known], owner_masks[position])
        for relative in range(1, 1 << bits):
            pair = [tables[relative], over(tables[relative], across_core)]
            outs = apply(((relative, True), (relative, False)), pair, *outs)
    return (outs[0][None], outs[1][None])


def solution(mesh):
    return jax.shard_map(
        functools.partial(local, mesh.shape["dp"], mesh.shape["expert"]),
        mesh=mesh,
        in_specs=(
            P("dp", None, "expert", None),
            P("dp", None, "expert", None),
            P("dp", None, "expert", None),
            P("dp", None, "expert"),
            P("dp", "expert", None, None),
        ),
        out_specs=(P("dp", None, "expert", None), P("dp", None, "expert", None)),
        check_vma=False,
    )
```

```python
import functools
import math

import jax
import jax.numpy as jnp
from jax import lax
from jax.experimental import pallas as pl
from jax.experimental.pallas import tpu as pltpu
from jax.sharding import PartitionSpec as P

KV_RANK = 512
NOPE = 128
VDIM = 128
NS_ITERS = 5
KV_ROWS = 16384

momentum_coef = 0.95
learn_rate = 0.02
decay_rate = 0.1
clip_limit = 100.0
coef_first = 3.4445
coef_second = -4.775
coef_third = 2.0315

f32 = jnp.float32
bf16 = jnp.bfloat16
i16 = jnp.int16
i32 = jnp.int32

LANES = 128
BLOCKS = KV_RANK // LANES
HALVES = (
    ((0, 1, True), (0, 1, False), (0, 2, False), (1, 2, False)),
    ((2, 3, True), (0, 3, False), (1, 3, False), (2, 3, False)),
)
AUX = 8
HALF = AUX + 4 * LANES
AUX_CODE = 16
HALF_CODE = AUX_CODE + 4 * LANES
AUX_P = 32
HEAD_P = AUX_P + 4 * LANES
ROWS_P = AUX_P + 8 * LANES
UNIT = 32000.0
CHUNKS = 2


SHORT = pl.CostEstimate(flops=1000, bytes_accessed=1000, transcendentals=0)


def params(mebibytes=40):
    return pltpu.CompilerParams(vmem_limit_bytes=mebibytes * 1024 * 1024)


def pinned(x):
    return pltpu.with_memory_space_constraint(x, pltpu.HBM)


def square_iotas():
    row = lax.broadcasted_iota(i32, (LANES, LANES), 0)
    col = lax.broadcasted_iota(i32, (LANES, LANES), 1)
    return row, col


def owner_bits(expert_size):
    return expert_size.bit_length() - 2


def place_of(expert_size):
    bits = owner_bits(expert_size)
    dp = lax.axis_index("dp").astype(i32)
    expert = lax.axis_index("expert").astype(i32)
    owner = ((dp >> 1) << (bits - 1)) | ((expert >> 1) & ((1 << (bits - 1)) - 1))
    return owner, expert & 1, dp * expert_size + expert


def layer_of(place, relative, own_core):
    core = place[1] if own_core else 1 - place[1]
    if isinstance(relative, tuple):
        relative = jnp.where(core == 0, relative[0], relative[1])
    return 2 * (place[0] ^ relative) + core


def gram_kernel(expert_size, picks, later, first, loaded, *refs):
    refs = list(refs)
    take = lambda n: [refs.pop(0) for _ in range(n)]
    grad_ref, mom_ref = take(2)
    if first:
        counts_ref, peaks_ref = take(2)
    else:
        (facts_ref,) = take(1)
    given = take(2 if loaded else 0)
    if first:
        (facts_ref,) = take(1)
    (nes_ref,) = take(1)
    gram_refs = take(2 * len(picks))
    loads = take(2 if later else 0)
    if first:
        counts, peaks_buf, small_arrivals = take(3)
    late_arrivals, own_arrivals, own_grad, own_mom = take(4)
    place = place_of(expert_size)
    layers = [layer_of(place, *pick) for pick in picks]

    def copies_of(chosen, buffers, semaphores):
        return [
            pltpu.make_async_copy(source.at[layer], buffer.at[k], semaphores.at[n, k])
            for k, layer in enumerate(chosen)
            for n, (source, buffer) in enumerate(((grad_ref, buffers[0]), (mom_ref, buffers[1])))
        ]

    own_copies = copies_of(layers[loaded:], (own_grad, own_mom), own_arrivals)
    small = []
    if first:
        small = [
            pltpu.make_async_copy(counts_ref, counts, small_arrivals.at[0]),
            pltpu.make_async_copy(peaks_ref, peaks_buf, small_arrivals.at[1]),
        ]
    late_copies = copies_of([layer_of(place, *pick) for pick in later], loads, late_arrivals) if later else []
    for copy in small + own_copies + late_copies:
        copy.start()
    row, col = square_iotas()
    line = lax.broadcasted_iota(i32, (AUX, LANES), 0)
    lane = lax.broadcasted_iota(i32, (AUX, LANES), 1)
    if first:
        for copy in small:
            copy.wait()
        every_peak = peaks_buf[...].astype(f32)
        every_peak = jnp.concatenate(
            [every_peak, jnp.zeros((every_peak.shape[0], LANES - every_peak.shape[1]), f32)], axis=1
        )
        for layer in range(every_peak.shape[0]):
            count = counts[layer].astype(f32)
            fact = jnp.where(line == 4, every_peak[layer : layer + 1], jnp.zeros((AUX, LANES), f32))
            fact = jnp.where((line == 6) | ((line == 5) & (lane == place[2])), count, fact)
            facts_ref[layer] = fact
    width = KV_RANK // 2
    dims = (((0,), (0,)), ((), ()))
    slot = lax.broadcasted_iota(i32, (nes_ref.shape[1], LANES), 0)

    def form_rows(k):
        (grad_buf, mom_buf), at = (given, k) if k < loaded else ((own_grad, own_mom), k - loaded)
        if k >= loaded:
            for copy in own_copies[2 * at : 2 * at + 2]:
                copy.wait()
        live = slot < facts_ref[layers[k], 6:7, :].astype(i32)
        for i in range(BLOCKS):
            span = slice(i * LANES, (i + 1) * LANES)
            gradient = grad_buf[at, :, span].astype(f32)
            velocity = momentum_coef * mom_buf[at, :, span].astype(f32) + gradient
            nesterov = gradient + momentum_coef * velocity
            nes_ref[k, :, span] = jnp.where(live, nesterov, 0.0).astype(bf16)

    form_rows(0)
    for k, layer in enumerate(layers):
        if k + 1 < len(layers):
            form_rows(k + 1)
        rows = nes_ref[k]
        upper = lax.dot_general(rows[:, :width], rows, dims, preferred_element_type=f32)
        lower = lax.dot_general(rows[:, width:], rows[:, width:], dims, preferred_element_type=f32)

        def block(i, j):
            if i < 2:
                return upper[i * LANES : (i + 1) * LANES, j * LANES : (j + 1) * LANES]
            return lower[(i - 2) * LANES : (i - 1) * LANES, (j - 2) * LANES : (j - 1) * LANES]

        aux = jnp.where(line == 6, 0.0, facts_ref[layer])
        for i in range(BLOCKS):
            diagonal = jnp.sum(jnp.where(row == col, block(i, i), 0.0), axis=0, keepdims=True)
            aux = jnp.where(line == i, diagonal, aux)
        for which, entries in enumerate(HALVES):
            half = [aux]
            for i, j, triangle in entries:
                half.append(jnp.where(row <= col, block(i, i), block(j, j)) if triangle else block(i, j))
            store_half(gram_refs[2 * k + which], 0, half)
    for copy in late_copies:
        copy.wait()


def gram_parts(expert_size, picks, later, sources, facts=None, loaded=()):
    grad, mom, counts, peaks = sources
    layers, capacity, features = grad.shape
    first = facts is None
    number = len(picks)
    vmem = pl.BlockSpec(memory_space=pltpu.VMEM)
    hbm = pl.BlockSpec(memory_space=pltpu.HBM)
    rows = lambda n: jax.ShapeDtypeStruct((n, capacity, features), bf16)
    out_shapes = [jax.ShapeDtypeStruct((layers, AUX, LANES), f32)] if first else []
    out_shapes += [rows(number)] + [jax.ShapeDtypeStruct((1, HALF, LANES), f32)] * (2 * number)
    out_shapes += [rows(len(later))] * 2 if later else []
    args = [pinned(grad), pinned(mom)]
    args += [pinned(counts), pinned(peaks)] if first else [facts] + list(loaded)
    known = loaded[0].shape[0] if loaded else 0
    own = max(number - known, 1)
    scratch = []
    if first:
        scratch += [pltpu.SMEM(counts.shape, i32), pltpu.VMEM(peaks.shape, bf16), pltpu.SemaphoreType.DMA((2,))]
    scratch += [pltpu.SemaphoreType.DMA((2, max(len(later), 1))), pltpu.SemaphoreType.DMA((2, own))]
    scratch += [pltpu.VMEM((own, capacity, features), bf16)] * 2
    out = pl.pallas_call(
        functools.partial(gram_kernel, expert_size, picks, later, first, known),
        in_specs=[hbm] * (4 if first else 2) + [vmem] * (0 if first else 1) + [vmem] * len(loaded),
        out_specs=[vmem] * len(out_shapes),
        out_shape=out_shapes,
        scratch_shapes=scratch,
        compiler_params=params(),
        cost_estimate=SHORT,
        name="gram_parts",
    )(*args)
    if first:
        facts, out = out[0], out[1:]
    halves = [list(out[at : at + 2]) for at in range(1, 1 + 2 * number, 2)]
    return facts, out[0], halves, tuple(out[1 + 2 * number :])


def joined(first, second):
    line = lax.broadcasted_iota(i32, (AUX, LANES), 0)
    aux = jnp.where(line == 4, jnp.maximum(first[0], second[0]), first[0] + second[0])
    return [aux] + [x + y for x, y in zip(first[1:], second[1:])]


def load_half(ref, index, base=0):
    starts = [base + AUX + place * LANES for place in range(4)]
    return [ref[index, base : base + AUX, :]] + [ref[index, at : at + LANES, :] for at in starts]


def store_half(ref, index, half, base=0):
    ref[index, base : base + AUX, :] = half[0]
    for place in range(4):
        at = base + AUX + place * LANES
        ref[index, at : at + LANES, :] = half[1 + place]


def outer_scales(which, scale):
    row, col = square_iotas()
    across = [scale[g : g + 1] for g in range(BLOCKS)]
    down = {}

    def outer(i, j):
        if i not in down:
            down[i] = jnp.broadcast_to(across[i], (LANES, LANES)).T
        return down[i] * across[j]

    return [
        jnp.where(row <= col, outer(i, i), outer(j, j)) if triangle else outer(i, j)
        for i, j, triangle in HALVES[which]
    ]


def decoded(which, ref, index, base=0):
    line = lax.broadcasted_iota(i32, (AUX, LANES), 0)
    codes = ref[index, base : base + AUX_CODE, :].astype(i32).astype(f32)
    low, high = codes[0:AUX], codes[AUX:AUX_CODE]
    scale = jnp.where(line < 4, jnp.exp2(low) * jnp.sqrt(high * (1.0 / UNIT)), 0.0)
    aux = jnp.where(line < 4, scale * scale, jnp.where(line == 4, low * (1.0 / 64.0), low))
    half = [aux]
    for place, factor in enumerate(outer_scales(which, scale)):
        at = base + AUX_CODE + place * LANES
        half.append(ref[index, at : at + LANES, :].astype(i32).astype(f32) * (factor * (1.0 / UNIT)))
    return half


def encode(which, ref, index, half, base=0):
    line = lax.broadcasted_iota(i32, (AUX, LANES), 0)
    aux = half[0]
    diagonal = jnp.maximum(aux, 1e-30)
    power = jnp.ceil(0.5 * jnp.log2(diagonal))
    high = jnp.clip(jnp.floor(diagonal * jnp.exp2(-2.0 * power) * UNIT + 0.5), 1.0, 32767.0)
    low = jnp.where(line < 4, power, jnp.where(line == 4, jnp.floor(aux * 64.0 + 0.5), aux))
    high = jnp.where(line < 4, high, 0.0)
    ref[index, base : base + AUX_CODE, :] = jnp.concatenate([low, high], axis=0).astype(i32).astype(i16)
    inverse = jnp.where(line < 4, jnp.exp2(-power) * lax.rsqrt(high * (1.0 / UNIT)), 0.0)
    for place, factor in enumerate(outer_scales(which, inverse)):
        at = base + AUX_CODE + place * LANES
        value = jnp.floor(half[1 + place] * (factor * UNIT) + 0.5)
        value = jnp.clip(value, -32767.0, 32767.0)
        ref[index, at : at + LANES, :] = value.astype(i32).astype(i16)


def local_call(kernel, out_shapes, name, *args):
    return pl.pallas_call(
        kernel,
        in_specs=[pl.BlockSpec(memory_space=pltpu.VMEM)] * len(args),
        out_specs=[pl.BlockSpec(memory_space=pltpu.VMEM)] * len(out_shapes),
        out_shape=list(out_shapes),
        compiler_params=params(),
        cost_estimate=SHORT,
        name=name,
    )(*args)


def send_kernel(number, *refs):
    for k in range(number):
        own, partner, message = refs[4 * k : 4 * k + 2], refs[4 * k + 2 : 4 * k + 4], refs[4 * number + k]
        for which in range(2):
            half = joined(load_half(own[which], 0), load_half(partner[which], 0))
            encode(which, message, 0, half, which * HALF_CODE)


def gather_kernel(*refs):
    messages, outs, stay = refs[4:-3], refs[-3:-1], refs[-1]
    for which in range(2):
        half = joined(load_half(refs[which], 0), load_half(refs[2 + which], 0))
        for arrived in messages:
            half = joined(half, decoded(which, arrived, 0, which * HALF_CODE))
        encode(which, outs[which], 0, half)
        store_half(stay, 0, half, which * HALF)


def sum_kernel(kept, arrived_a, arrived_b, *refs):
    outs, stay = refs[:2], refs[2]
    for which, arrived in enumerate((arrived_a, arrived_b)):
        half = joined(load_half(kept, 0, which * HALF), decoded(which, arrived, 0))
        encode(which, outs[which], 0, half)
        store_half(stay, 0, half, which * HALF)


def mm(x, y):
    return jnp.dot(x, y, preferred_element_type=f32)


def wide(*parts):
    return jnp.concatenate(parts, axis=1)


def tall(*parts):
    return jnp.concatenate(parts, axis=0)


def parts_of(x):
    high = x.astype(bf16)
    return high, (x - high.astype(f32)).astype(bf16)


def unpack_symmetric(which, blocks, diagonal, store):
    row, col = square_iotas()
    for (i, j, triangle), block in zip(HALVES[which], blocks):
        other = block.T
        if triangle:
            first = jnp.where(row < col, block, other)
            second = jnp.where(row > col, block, other)
            store(i, i, jnp.where(row == col, diagonal(i), first))
            store(j, j, jnp.where(row == col, diagonal(j), second))
        else:
            store(i, j, block)
            store(j, i, other)


def iterate_kernel(kept, arrived_a, arrived_b, out_ref, gram_ref):
    row, col = square_iotas()

    def store(i, j, block):
        gram_ref[i * LANES : (i + 1) * LANES, j * LANES : (j + 1) * LANES] = block

    aux = None
    for which, arrived in enumerate((arrived_a, arrived_b)):
        half = joined(load_half(kept, 0, which * HALF), decoded(which, arrived, 0))
        if aux is None:
            aux = half[0]
        unpack_symmetric(which, half[1:], lambda g: aux[g : g + 1], store)
    line = lax.broadcasted_iota(i32, (AUX, LANES), 0)
    squares = jnp.sum(jnp.where(line < 4, aux, 0.0), axis=0, keepdims=True)
    squares = jnp.sum(squares, axis=1, keepdims=True)
    inverse = 1.0 / (jnp.sqrt(squares) + 1e-07)
    gram = gram_ref[...] * inverse * inverse
    full_row = lax.broadcasted_iota(i32, (KV_RANK, KV_RANK), 0)
    full_col = lax.broadcasted_iota(i32, (KV_RANK, KV_RANK), 1)
    on_diagonal = full_row == full_col
    product = None
    for repeat in range(NS_ITERS):
        high, low = parts_of(gram)
        if repeat >= 2:
            square = mm(wide(high, high, low), tall(high, low, high))
        else:
            square = mm(high, high)
        mixing = (coef_second * gram + coef_third * square).astype(bf16)
        if product is None:
            product = jnp.where(on_diagonal, coef_first, 0.0) + mixing.astype(f32)
        else:
            diagonal = jnp.sum(jnp.where(on_diagonal, product, 0.0), axis=0, keepdims=True)
            rest = jnp.where(on_diagonal, 0.0, product).astype(bf16)
            product = coef_first * product + (mm(mixing, rest) + mixing.astype(f32) * diagonal)
        if repeat < NS_ITERS - 1:
            half = coef_first * gram + mm(wide(high, low), tall(mixing, mixing))
            half_high, half_low = parts_of(half)
            gram = coef_first * half + mm(wide(mixing, mixing), tall(half_high, half_low))
    gram_ref[...] = product
    at = AUX_P
    for entries in HALVES:
        for i, j, triangle in entries:
            load = lambda i, j: gram_ref[i * LANES : (i + 1) * LANES, j * LANES : (j + 1) * LANES]
            if triangle:
                block = jnp.where(row <= col, load(i, i), load(j, j))
                block = 0.5 * (block + jnp.where(row <= col, load(i, i).T, load(j, j).T))
            else:
                block = 0.5 * (load(i, j) + load(j, i).T)
            out_ref[at : at + LANES, :] = block.astype(bf16)
            at += LANES

    def three(x):
        high = x.astype(bf16).astype(f32)
        middle = (x - high).astype(bf16).astype(f32)
        return high, middle, x - high - middle

    lines = [[], [], []]
    for i in range(BLOCKS):
        block = gram_ref[i * LANES : (i + 1) * LANES, i * LANES : (i + 1) * LANES]
        diagonal = jnp.sum(jnp.where(row == col, block, 0.0), axis=0, keepdims=True)
        for lines_of, part in zip(lines, three(diagonal)):
            lines_of.append(part)
    peaks = aux[4:5]
    tallies = aux[5:6]
    tally_high = tallies.astype(bf16).astype(f32)
    norm = three(jnp.broadcast_to(inverse, (1, LANES)))
    stacked = lines[0] + lines[1] + lines[2] + [peaks, tally_high, tallies - tally_high] + list(norm)
    place = lax.broadcasted_iota(i32, (AUX_P, LANES), 0)
    table = jnp.zeros((AUX_P, LANES), f32)
    for number, one in enumerate(stacked):
        table = jnp.where(place == number, one, table)
    out_ref[0:AUX_P, :] = table.astype(bf16)


def iterations(*args):
    return pl.pallas_call(
        iterate_kernel,
        in_specs=[pl.BlockSpec(memory_space=pltpu.VMEM)] * 3,
        out_specs=pl.BlockSpec(memory_space=pltpu.VMEM),
        out_shape=jax.ShapeDtypeStruct((ROWS_P, LANES), bf16),
        scratch_shapes=[pltpu.VMEM((KV_RANK, KV_RANK), f32)],
        compiler_params=params(),
        cost_estimate=SHORT,
        name="iterations",
    )(*args)


def apply_kernel(steps, spread, places, seats, number_of, *refs):
    tables = refs[: number_of[0]]
    rows_in = refs[number_of[0] : sum(number_of)]
    weight_ref = refs[sum(number_of)]
    update_out, weight_out, mat_ref, update_ref, new_ref, leaving = refs[-6:]
    groups, rows_block = seats
    here = place_of(groups)
    dp = lax.axis_index("dp").astype(i32)
    capacity = weight_ref.shape[1]
    head_rows = NOPE + VDIM
    rms_scale = 0.2 * math.sqrt(max(KV_ROWS, KV_RANK))
    lane = lax.broadcasted_iota(i32, (1, LANES), 1)
    head_shift = head_rows.bit_length() - 1
    assert head_rows == 1 << head_shift and capacity % (16 * CHUNKS) == 0
    rows_of_slots = -(-capacity // LANES)
    slot = lax.broadcasted_iota(i32, (rows_of_slots, LANES), 0) * LANES
    slot = slot + lax.broadcasted_iota(i32, (rows_of_slots, LANES), 1)
    copies = []
    for step, pick in enumerate(steps):
        layer = layer_of(here, *pick)
        (place_a, start_a), (place_b, start_b) = spread[step]
        aux = tables[place_a][start_a : start_a + AUX_P, :].astype(f32)
        diagonal = [aux[i : i + 1] + aux[4 + i : 5 + i] + aux[8 + i : 9 + i] for i in range(BLOCKS)]
        inverse = [1.0 / line for line in diagonal]
        norm = (aux[15:16] + aux[16:17] + aux[17:18]) * rms_scale
        factor = jnp.sqrt(jnp.minimum(1.0, clip_limit / aux[12:13]))
        tallies = aux[13:14] + aux[14:15]

        def store(i, j, block):
            block = (block * inverse[j]).astype(bf16)
            mat_ref[step, i * LANES : (i + 1) * LANES, j * LANES : (j + 1) * LANES] = block

        for which, (place, start) in enumerate(((place_a, start_a + AUX_P), (place_b, start_b))):
            blocks = [
                tables[place][start + k * LANES : start + (k + 1) * LANES, :].astype(f32) for k in range(4)
            ]
            unpack_symmetric(which, blocks, lambda g: diagonal[g], store)
        lowest = dp * groups
        earlier = jnp.where((lane >= lowest) & (lane < here[2]), tallies, 0.0)
        base = jnp.sum(earlier, axis=1, keepdims=True).astype(i32) + dp * rows_block
        first_head = base >> head_shift
        row_index = base + slot
        head_of = row_index >> head_shift
        scale = jnp.ones(slot.shape, f32)
        for k in range((capacity - 1) // head_rows + 2):
            one = jnp.sum(jnp.where(lane == first_head + k, factor, 0.0), axis=1, keepdims=True)
            scale = jnp.where(head_of == first_head + k, one, scale)
        scale = jnp.where((row_index & (head_rows - 1)) < NOPE, scale, 1.0)
        count = jnp.sum(jnp.where(lane == here[2], tallies, 0.0), axis=1, keepdims=True).astype(i32)
        scale = jnp.where(slot < count, scale, 0.0)
        columns = [jnp.broadcast_to(scale[k : k + 1], (LANES, LANES)).T for k in range(slot.shape[0])]
        scale = jnp.concatenate(columns, axis=0)[:capacity]
        kept = scale * (1.0 - learn_rate * decay_rate)
        moved = scale * learn_rate
        source, index = places[step]
        if isinstance(index, tuple):
            core = here[1] if pick[1] else 1 - here[1]
            index = jnp.where(core == 0, index[0], index[1])
        for chunk in range(CHUNKS):
            size = capacity // CHUNKS
            among = slice(chunk * size, (chunk + 1) * size)
            product = mm(rows_in[source][index, among, :], mat_ref[step])
            for i in range(BLOCKS):
                span = slice(i * LANES, (i + 1) * LANES)
                update = product[:, span] * (diagonal[i] * norm)
                update_ref[step, among, span] = update.astype(bf16)
                weight = weight_ref[layer, among, span].astype(f32)
                new_ref[step, among, span] = (weight * kept[among] - update * moved[among]).astype(bf16)
            at = pl.ds(chunk * size, size)
            for number, (held, out) in enumerate(((update_ref, update_out), (new_ref, weight_out))):
                copy = pltpu.make_async_copy(
                    held.at[step, at], out.at[layer, at], leaving.at[number, step * CHUNKS + chunk]
                )
                copy.start()
                copies.append(copy)
    for copy in copies:
        copy.wait()


def apply_rows(steps, spread, places, seats, tables, rows, weight, *outs):
    number = len(steps)
    layers, capacity, features = weight.shape
    vmem = pl.BlockSpec(memory_space=pltpu.VMEM)
    hbm = pl.BlockSpec(memory_space=pltpu.HBM)
    args = list(tables) + list(rows) + [weight] + list(outs)
    shape = jax.ShapeDtypeStruct((layers, capacity, features), bf16)
    return pl.pallas_call(
        functools.partial(apply_kernel, steps, spread, places, seats, (len(tables), len(rows))),
        in_specs=[vmem] * (len(tables) + len(rows) + 1) + [hbm] * len(outs),
        out_specs=[hbm, hbm],
        out_shape=[shape, shape],
        scratch_shapes=[
            pltpu.VMEM((number, KV_RANK, KV_RANK), bf16),
            pltpu.VMEM((number, capacity, features), bf16),
            pltpu.VMEM((number, capacity, features), bf16),
            pltpu.SemaphoreType.DMA((2, number * CHUNKS)),
        ],
        input_output_aliases={len(args) - 2: 0, len(args) - 1: 1} if outs else {},
        compiler_params=params(),
        cost_estimate=SHORT,
        name="apply_rows",
    )(*args)


def local(dp_size, expert_size, grad_rows, momentum_rows, weight_rows, row_counts, logit_peaks):
    layers = grad_rows.shape[1]
    bits = owner_bits(expert_size)
    assert layers == expert_size == 2 << bits and bits >= 2
    assert dp_size == 4 and dp_size * expert_size <= LANES
    sources = (grad_rows[0], momentum_rows[0], row_counts.reshape(layers), logit_peaks[0, 0])

    def over(x, mask):
        everyone = range(dp_size * expert_size)
        return lax.ppermute(x, ("dp", "expert"), [(i, i ^ mask) for i in everyone])

    across_core = 1
    owner_masks = [2 << p for p in range(bits - 1)] + [2 * expert_size]
    copy_masks = [expert_size, expert_size // 2]

    def mask_of(relative):
        return sum(mask for p, mask in enumerate(owner_masks) if relative >> p & 1)

    def by_core(x, even, odd):
        everyone = range(dp_size * expert_size)
        return lax.ppermute(x, ("dp", "expert"), [(i, i ^ (odd if i & 1 else even)) for i in everyone])

    most = (1 << bits) - 1
    others = list(range(most - 1, 0, -1))
    turns = [
        [(most, False)],
        [(most, True)] + [(r, False) for r in others],
        [(r, True) for r in others],
        [(0, False), (0, True)],
    ]
    rows, partial, messages = {}, {}, []
    facts, loaded = None, ()
    message_shape = jax.ShapeDtypeStruct((1, 2 * HALF_CODE, LANES), i16)
    for number, turn in enumerate(turns):
        later = turns[number + 1][:2] if number + 1 < len(turns) else []
        if messages and not later:
            loaded, messages[0] = lax.optimization_barrier((loaded, messages[0]))
        facts, made, grams, loaded = gram_parts(expert_size, turn, later, sources, facts, loaded)
        for index, (pick, gram) in enumerate(zip(turn, grams)):
            rows[pick] = (made, index)
            partial[pick] = gram if pick[1] else [over(half, across_core) for half in gram]
        ready = ([], [most], others, [])[number]
        if ready:
            sums = [half for r in ready for half in partial[r, True] + partial[r, False]]
            kernel = functools.partial(send_kernel, len(ready))
            made = local_call(kernel, [message_shape] * len(ready), "send", *sums)
            made, loaded = lax.optimization_barrier((made, loaded))
            messages += [over(message, mask_of(r)) for r, message in zip(ready, made)]
    codes = jax.ShapeDtypeStruct((1, HALF_CODE, LANES), i16)
    shapes = [codes, codes, jax.ShapeDtypeStruct((1, 2 * HALF, LANES), f32)]
    out = local_call(gather_kernel, shapes, "gather", *partial[0, True], *partial[0, False], *messages)
    state = [out[2], over(out[0], copy_masks[0]), over(out[1], copy_masks[1])]
    out = local_call(sum_kernel, shapes, "sum", *state)
    state = [out[2], over(out[0], copy_masks[1]), over(out[1], copy_masks[0])]
    table = iterations(*state)

    seats = (expert_size, KV_ROWS // dp_size)
    weight = weight_rows[0]
    full = lambda place: ((place, 0), (place, HEAD_P))

    def apply(picks, tables, *outs):
        arrays, places = [], []
        for relative, own_core in picks:
            found = [rows[r, own_core] for r in (relative if isinstance(relative, tuple) else (relative,))]
            if not any(array is found[0][0] for array in arrays):
                arrays.append(found[0][0])
            (source,) = [k for k, array in enumerate(arrays) if array is found[0][0]]
            assert all(made is arrays[source] for made, _ in found)
            indices = tuple(index for _, index in found)
            places.append((source, indices if len(indices) > 1 else indices[0]))
        spread = tuple(full(k) for k in range(len(tables)))
        return apply_rows(tuple(picks), spread, places, seats, tables, arrays, weight, *outs)

    if bits == 2:
        first = by_core(table, owner_masks[1], owner_masks[0])
        second = by_core(table, owner_masks[0], owner_masks[1])
        outs = apply([(0, True)], [table])
        table, first, second, outs = lax.optimization_barrier((table, first, second, outs))
        last = by_core(second, owner_masks[1], owner_masks[0])
        near = [(2, 1), (1, 2)]
        outs = apply([(r, True) for r in near], [first, second], *outs)
        crossed = [over(x, across_core) for x in (table, first, second)]
        outs = apply([(r, False) for r in [0] + near], crossed, *outs)
        last, outs = lax.optimization_barrier((last, outs))
        outs = apply([(3, True)], [last], *outs)
        outs = apply([(3, False)], [over(last, across_core)], *outs)
    else:
        outs = apply(((0, True), (0, False)), [table, over(table, across_core)])
        tables = {0: table}
        for position in range(bits - 1, -1, -1):
            for known in list(tables):
                tables[known | 1 << position] = over(tables[known], owner_masks[position])
        for relative in range(1, 1 << bits):
            pair = [tables[relative], over(tables[relative], across_core)]
            outs = apply(((relative, True), (relative, False)), pair, *outs)
    return (outs[0][None], outs[1][None])


def solution(mesh):
    return jax.shard_map(
        functools.partial(local, mesh.shape["dp"], mesh.shape["expert"]),
        mesh=mesh,
        in_specs=(
            P("dp", None, "expert", None),
            P("dp", None, "expert", None),
            P("dp", None, "expert", None),
            P("dp", None, "expert"),
            P("dp", "expert", None, None),
        ),
        out_specs=(P("dp", None, "expert", None), P("dp", None, "expert", None)),
        check_vma=False,
    )
```

```python
import functools
import math

import jax
import jax.numpy as jnp
from jax import lax
from jax.experimental import pallas as pl
from jax.experimental.pallas import tpu as pltpu
from jax.sharding import PartitionSpec as P

KV_RANK = 512
NOPE = 128
VDIM = 128
NS_ITERS = 5
KV_ROWS = 16384

momentum_coef = 0.95
learn_rate = 0.02
decay_rate = 0.1
clip_limit = 100.0
coef_first = 3.4445
coef_second = -4.775
coef_third = 2.0315

f32 = jnp.float32
bf16 = jnp.bfloat16
i16 = jnp.int16
i32 = jnp.int32

LANES = 128
BLOCKS = KV_RANK // LANES
HALVES = (
    ((0, 1, True), (0, 1, False), (0, 2, False), (1, 2, False)),
    ((2, 3, True), (0, 3, False), (1, 3, False), (2, 3, False)),
)
AUX = 8
HALF = AUX + 4 * LANES
AUX_CODE = 16
HALF_CODE = AUX_CODE + 4 * LANES
AUX_P = 32
HEAD_P = AUX_P + 4 * LANES
ROWS_P = AUX_P + 8 * LANES
UNIT = 32000.0


def chunks_of(capacity):
    return 4 if capacity % 64 == 0 else 2 if capacity % 32 == 0 else 1


SHORT = pl.CostEstimate(flops=1000, bytes_accessed=1000, transcendentals=0)


def params(mebibytes=40):
    return pltpu.CompilerParams(vmem_limit_bytes=mebibytes * 1024 * 1024)


def pinned(x):
    return pltpu.with_memory_space_constraint(x, pltpu.HBM)


def square_iotas():
    row = lax.broadcasted_iota(i32, (LANES, LANES), 0)
    col = lax.broadcasted_iota(i32, (LANES, LANES), 1)
    return row, col


def owner_bits(expert_size):
    return expert_size.bit_length() - 2


def place_of(expert_size):
    bits = owner_bits(expert_size)
    dp = lax.axis_index("dp").astype(i32)
    expert = lax.axis_index("expert").astype(i32)
    owner = ((dp >> 1) << (bits - 1)) | ((expert >> 1) & ((1 << (bits - 1)) - 1))
    return owner, expert & 1, dp * expert_size + expert


def layer_of(place, relative, own_core):
    core = place[1] if own_core else 1 - place[1]
    if isinstance(relative, tuple):
        relative = jnp.where(core == 0, relative[0], relative[1])
    return 2 * (place[0] ^ relative) + core


def gram_kernel(expert_size, picks, later, first, loaded, *refs):
    refs = list(refs)
    take = lambda n: [refs.pop(0) for _ in range(n)]
    grad_ref, mom_ref = take(2)
    if first:
        counts_ref, peaks_ref = take(2)
    else:
        (facts_ref,) = take(1)
    given = take(2 if loaded else 0)
    if first:
        (facts_ref,) = take(1)
    (nes_ref,) = take(1)
    gram_refs = take(2 * len(picks))
    loads = take(2 if later else 0)
    if first:
        counts, peaks_buf, small_arrivals = take(3)
    late_arrivals, own_arrivals, own_grad, own_mom = take(4)
    place = place_of(expert_size)
    layers = [layer_of(place, *pick) for pick in picks]

    def copies_of(chosen, buffers, semaphores):
        return [
            pltpu.make_async_copy(source.at[layer], buffer.at[k], semaphores.at[n, k])
            for k, layer in enumerate(chosen)
            for n, (source, buffer) in enumerate(((grad_ref, buffers[0]), (mom_ref, buffers[1])))
        ]

    own_copies = copies_of(layers[loaded:], (own_grad, own_mom), own_arrivals)
    small = []
    if first:
        small = [
            pltpu.make_async_copy(counts_ref, counts, small_arrivals.at[0]),
            pltpu.make_async_copy(peaks_ref, peaks_buf, small_arrivals.at[1]),
        ]
    late_copies = copies_of([layer_of(place, *pick) for pick in later], loads, late_arrivals) if later else []
    for copy in small + own_copies + late_copies:
        copy.start()
    row, col = square_iotas()
    line = lax.broadcasted_iota(i32, (AUX, LANES), 0)
    lane = lax.broadcasted_iota(i32, (AUX, LANES), 1)
    if first:
        for copy in small:
            copy.wait()
        every_peak = peaks_buf[...].astype(f32)
        every_peak = jnp.concatenate(
            [every_peak, jnp.zeros((every_peak.shape[0], LANES - every_peak.shape[1]), f32)], axis=1
        )
        for layer in range(every_peak.shape[0]):
            count = counts[layer].astype(f32)
            fact = jnp.where(line == 4, every_peak[layer : layer + 1], jnp.zeros((AUX, LANES), f32))
            fact = jnp.where((line == 6) | ((line == 5) & (lane == place[2])), count, fact)
            facts_ref[layer] = fact
    width = KV_RANK // 2
    dims = (((0,), (0,)), ((), ()))
    slot = lax.broadcasted_iota(i32, (nes_ref.shape[1], LANES), 0)

    def form_rows(k):
        (grad_buf, mom_buf), at = (given, k) if k < loaded else ((own_grad, own_mom), k - loaded)
        if k >= loaded:
            for copy in own_copies[2 * at : 2 * at + 2]:
                copy.wait()
        live = slot < facts_ref[layers[k], 6:7, :].astype(i32)
        for i in range(BLOCKS):
            span = slice(i * LANES, (i + 1) * LANES)
            gradient = grad_buf[at, :, span].astype(f32)
            velocity = momentum_coef * mom_buf[at, :, span].astype(f32) + gradient
            nesterov = gradient + momentum_coef * velocity
            nes_ref[k, :, span] = jnp.where(live, nesterov, 0.0).astype(bf16)

    form_rows(0)
    for k, layer in enumerate(layers):
        if k + 1 < len(layers):
            form_rows(k + 1)
        rows = nes_ref[k]
        upper = lax.dot_general(rows[:, :width], rows, dims, preferred_element_type=f32)
        lower = lax.dot_general(rows[:, width:], rows[:, width:], dims, preferred_element_type=f32)

        def block(i, j):
            if i < 2:
                return upper[i * LANES : (i + 1) * LANES, j * LANES : (j + 1) * LANES]
            return lower[(i - 2) * LANES : (i - 1) * LANES, (j - 2) * LANES : (j - 1) * LANES]

        aux = jnp.where(line == 6, 0.0, facts_ref[layer])
        for i in range(BLOCKS):
            diagonal = jnp.sum(jnp.where(row == col, block(i, i), 0.0), axis=0, keepdims=True)
            aux = jnp.where(line == i, diagonal, aux)
        for which, entries in enumerate(HALVES):
            half = [aux]
            for i, j, triangle in entries:
                half.append(jnp.where(row <= col, block(i, i), block(j, j)) if triangle else block(i, j))
            store_half(gram_refs[2 * k + which], 0, half)
    for copy in late_copies:
        copy.wait()


def gram_parts(expert_size, picks, later, sources, facts=None, loaded=()):
    grad, mom, counts, peaks = sources
    layers, capacity, features = grad.shape
    first = facts is None
    number = len(picks)
    vmem = pl.BlockSpec(memory_space=pltpu.VMEM)
    hbm = pl.BlockSpec(memory_space=pltpu.HBM)
    rows = lambda n: jax.ShapeDtypeStruct((n, capacity, features), bf16)
    out_shapes = [jax.ShapeDtypeStruct((layers, AUX, LANES), f32)] if first else []
    out_shapes += [rows(number)] + [jax.ShapeDtypeStruct((1, HALF, LANES), f32)] * (2 * number)
    out_shapes += [rows(len(later))] * 2 if later else []
    args = [pinned(grad), pinned(mom)]
    args += [pinned(counts), pinned(peaks)] if first else [facts] + list(loaded)
    known = loaded[0].shape[0] if loaded else 0
    own = max(number - known, 1)
    scratch = []
    if first:
        scratch += [pltpu.SMEM(counts.shape, i32), pltpu.VMEM(peaks.shape, bf16), pltpu.SemaphoreType.DMA((2,))]
    scratch += [pltpu.SemaphoreType.DMA((2, max(len(later), 1))), pltpu.SemaphoreType.DMA((2, own))]
    scratch += [pltpu.VMEM((own, capacity, features), bf16)] * 2
    out = pl.pallas_call(
        functools.partial(gram_kernel, expert_size, picks, later, first, known),
        in_specs=[hbm] * (4 if first else 2) + [vmem] * (0 if first else 1) + [vmem] * len(loaded),
        out_specs=[vmem] * len(out_shapes),
        out_shape=out_shapes,
        scratch_shapes=scratch,
        compiler_params=params(),
        cost_estimate=SHORT,
        name="gram_parts",
    )(*args)
    if first:
        facts, out = out[0], out[1:]
    halves = [list(out[at : at + 2]) for at in range(1, 1 + 2 * number, 2)]
    return facts, out[0], halves, tuple(out[1 + 2 * number :])


def joined(first, second):
    line = lax.broadcasted_iota(i32, (AUX, LANES), 0)
    aux = jnp.where(line == 4, jnp.maximum(first[0], second[0]), first[0] + second[0])
    return [aux] + [x + y for x, y in zip(first[1:], second[1:])]


def load_half(ref, index, base=0):
    starts = [base + AUX + place * LANES for place in range(4)]
    return [ref[index, base : base + AUX, :]] + [ref[index, at : at + LANES, :] for at in starts]


def store_half(ref, index, half, base=0):
    ref[index, base : base + AUX, :] = half[0]
    for place in range(4):
        at = base + AUX + place * LANES
        ref[index, at : at + LANES, :] = half[1 + place]


def outer_scales(which, scale):
    row, col = square_iotas()
    across = [scale[g : g + 1] for g in range(BLOCKS)]
    down = {}

    def outer(i, j):
        if i not in down:
            down[i] = jnp.broadcast_to(across[i], (LANES, LANES)).T
        return down[i] * across[j]

    return [
        jnp.where(row <= col, outer(i, i), outer(j, j)) if triangle else outer(i, j)
        for i, j, triangle in HALVES[which]
    ]


def decoded(which, ref, index, base=0):
    line = lax.broadcasted_iota(i32, (AUX, LANES), 0)
    codes = ref[index, base : base + AUX_CODE, :].astype(i32).astype(f32)
    low, high = codes[0:AUX], codes[AUX:AUX_CODE]
    scale = jnp.where(line < 4, jnp.exp2(low) * jnp.sqrt(high * (1.0 / UNIT)), 0.0)
    aux = jnp.where(line < 4, scale * scale, jnp.where(line == 4, low * (1.0 / 64.0), low))
    half = [aux]
    for place, factor in enumerate(outer_scales(which, scale)):
        at = base + AUX_CODE + place * LANES
        half.append(ref[index, at : at + LANES, :].astype(i32).astype(f32) * (factor * (1.0 / UNIT)))
    return half


def encode(which, ref, index, half, base=0):
    line = lax.broadcasted_iota(i32, (AUX, LANES), 0)
    aux = half[0]
    diagonal = jnp.maximum(aux, 1e-30)
    power = jnp.ceil(0.5 * jnp.log2(diagonal))
    high = jnp.clip(jnp.floor(diagonal * jnp.exp2(-2.0 * power) * UNIT + 0.5), 1.0, 32767.0)
    low = jnp.where(line < 4, power, jnp.where(line == 4, jnp.floor(aux * 64.0 + 0.5), aux))
    high = jnp.where(line < 4, high, 0.0)
    ref[index, base : base + AUX_CODE, :] = jnp.concatenate([low, high], axis=0).astype(i32).astype(i16)
    inverse = jnp.where(line < 4, jnp.exp2(-power) * lax.rsqrt(high * (1.0 / UNIT)), 0.0)
    for place, factor in enumerate(outer_scales(which, inverse)):
        at = base + AUX_CODE + place * LANES
        value = jnp.floor(half[1 + place] * (factor * UNIT) + 0.5)
        value = jnp.clip(value, -32767.0, 32767.0)
        ref[index, at : at + LANES, :] = value.astype(i32).astype(i16)


def local_call(kernel, out_shapes, name, *args):
    return pl.pallas_call(
        kernel,
        in_specs=[pl.BlockSpec(memory_space=pltpu.VMEM)] * len(args),
        out_specs=[pl.BlockSpec(memory_space=pltpu.VMEM)] * len(out_shapes),
        out_shape=list(out_shapes),
        compiler_params=params(),
        cost_estimate=SHORT,
        name=name,
    )(*args)


def send_kernel(number, *refs):
    for k in range(number):
        own, partner, message = refs[4 * k : 4 * k + 2], refs[4 * k + 2 : 4 * k + 4], refs[4 * number + k]
        for which in range(2):
            half = joined(load_half(own[which], 0), load_half(partner[which], 0))
            encode(which, message, 0, half, which * HALF_CODE)


def gather_kernel(*refs):
    messages, outs, stay = refs[4:-3], refs[-3:-1], refs[-1]
    for which in range(2):
        half = joined(load_half(refs[which], 0), load_half(refs[2 + which], 0))
        for arrived in messages:
            half = joined(half, decoded(which, arrived, 0, which * HALF_CODE))
        encode(which, outs[which], 0, half)
        store_half(stay, 0, half, which * HALF)


def sum_kernel(kept, arrived_a, arrived_b, *refs):
    outs, stay = refs[:2], refs[2]
    for which, arrived in enumerate((arrived_a, arrived_b)):
        half = joined(load_half(kept, 0, which * HALF), decoded(which, arrived, 0))
        encode(which, outs[which], 0, half)
        store_half(stay, 0, half, which * HALF)


def mm(x, y):
    return jnp.dot(x, y, preferred_element_type=f32)


def unpack_symmetric(which, blocks, diagonal, store):
    row, col = square_iotas()
    for (i, j, triangle), block in zip(HALVES[which], blocks):
        other = block.T
        if triangle:
            first = jnp.where(row < col, block, other)
            second = jnp.where(row > col, block, other)
            store(i, i, jnp.where(row == col, diagonal(i), first))
            store(j, j, jnp.where(row == col, diagonal(j), second))
        else:
            store(i, j, block)
            store(j, i, other)


def iterate_kernel(kept, arrived_a, arrived_b, out_ref, gram_ref):
    row, col = square_iotas()

    def store(i, j, block):
        gram_ref[i * LANES : (i + 1) * LANES, j * LANES : (j + 1) * LANES] = block

    aux = None
    for which, arrived in enumerate((arrived_a, arrived_b)):
        half = joined(load_half(kept, 0, which * HALF), decoded(which, arrived, 0))
        if aux is None:
            aux = half[0]
        unpack_symmetric(which, half[1:], lambda g: aux[g : g + 1], store)
    line = lax.broadcasted_iota(i32, (AUX, LANES), 0)
    squares = jnp.sum(jnp.where(line < 4, aux, 0.0), axis=0, keepdims=True)
    squares = jnp.sum(squares, axis=1, keepdims=True)
    inverse = 1.0 / (jnp.sqrt(squares) + 1e-07)
    gram = gram_ref[...] * inverse * inverse
    full_row = lax.broadcasted_iota(i32, (KV_RANK, KV_RANK), 0)
    full_col = lax.broadcasted_iota(i32, (KV_RANK, KV_RANK), 1)
    on_diagonal = full_row == full_col
    def diagonal_of(x):
        return jnp.sum(jnp.where(on_diagonal, x, 0.0), axis=0, keepdims=True)

    def rest_of(x):
        return jnp.where(on_diagonal, 0.0, x).astype(bf16)

    product = None
    for repeat in range(NS_ITERS):
        diagonal = diagonal_of(gram)
        columns = [diagonal[:, i * LANES : (i + 1) * LANES] for i in range(BLOCKS)]
        down = jnp.concatenate([jnp.broadcast_to(one, (LANES, LANES)).T for one in columns], axis=0)
        down = jnp.concatenate([down] * BLOCKS, axis=1)
        rest = rest_of(gram)
        square = mm(rest, rest) + jnp.where(on_diagonal, diagonal * diagonal, gram * (down + diagonal))
        mixing = (coef_second * gram + coef_third * square).astype(bf16)
        mixing_wide = mixing.astype(f32)
        if product is None:
            product = jnp.where(on_diagonal, coef_first, 0.0) + mixing_wide
        else:
            moved = mm(mixing, rest_of(product)) + mixing_wide * diagonal_of(product)
            product = coef_first * product + moved
        if repeat < NS_ITERS - 1:
            half = coef_first * gram + (mm(rest, mixing) + mixing_wide * down)
            gram = coef_first * half + (mm(mixing, rest_of(half)) + mixing_wide * diagonal_of(half))
    gram_ref[...] = product
    at = AUX_P
    for entries in HALVES:
        for i, j, triangle in entries:
            load = lambda i, j: gram_ref[i * LANES : (i + 1) * LANES, j * LANES : (j + 1) * LANES]
            if triangle:
                block = jnp.where(row <= col, load(i, i), load(j, j))
                block = 0.5 * (block + jnp.where(row <= col, load(i, i).T, load(j, j).T))
            else:
                block = 0.5 * (load(i, j) + load(j, i).T)
            out_ref[at : at + LANES, :] = block.astype(bf16)
            at += LANES

    def three(x):
        high = x.astype(bf16).astype(f32)
        middle = (x - high).astype(bf16).astype(f32)
        return high, middle, x - high - middle

    lines = [[], [], []]
    for i in range(BLOCKS):
        block = gram_ref[i * LANES : (i + 1) * LANES, i * LANES : (i + 1) * LANES]
        diagonal = jnp.sum(jnp.where(row == col, block, 0.0), axis=0, keepdims=True)
        for lines_of, part in zip(lines, three(diagonal)):
            lines_of.append(part)
    peaks = aux[4:5]
    tallies = aux[5:6]
    tally_high = tallies.astype(bf16).astype(f32)
    norm = three(jnp.broadcast_to(inverse, (1, LANES)))
    stacked = lines[0] + lines[1] + lines[2] + [peaks, tally_high, tallies - tally_high] + list(norm)
    place = lax.broadcasted_iota(i32, (AUX_P, LANES), 0)
    table = jnp.zeros((AUX_P, LANES), f32)
    for number, one in enumerate(stacked):
        table = jnp.where(place == number, one, table)
    out_ref[0:AUX_P, :] = table.astype(bf16)


def iterations(*args):
    return pl.pallas_call(
        iterate_kernel,
        in_specs=[pl.BlockSpec(memory_space=pltpu.VMEM)] * 3,
        out_specs=pl.BlockSpec(memory_space=pltpu.VMEM),
        out_shape=jax.ShapeDtypeStruct((ROWS_P, LANES), bf16),
        scratch_shapes=[pltpu.VMEM((KV_RANK, KV_RANK), f32)],
        compiler_params=params(),
        cost_estimate=SHORT,
        name="iterations",
    )(*args)


def apply_kernel(steps, spread, places, seats, number_of, *refs):
    tables = refs[: number_of[0]]
    rows_in = refs[number_of[0] : sum(number_of)]
    weight_ref = refs[sum(number_of)]
    update_out, weight_out, mat_ref, update_ref, new_ref, leaving = refs[-6:]
    groups, rows_block = seats
    here = place_of(groups)
    dp = lax.axis_index("dp").astype(i32)
    capacity = weight_ref.shape[1]
    head_rows = NOPE + VDIM
    rms_scale = 0.2 * math.sqrt(max(KV_ROWS, KV_RANK))
    lane = lax.broadcasted_iota(i32, (1, LANES), 1)
    head_shift = head_rows.bit_length() - 1
    chunks = chunks_of(capacity)
    assert head_rows == 1 << head_shift and capacity % (16 * chunks) == 0
    rows_of_slots = -(-capacity // LANES)
    slot = lax.broadcasted_iota(i32, (rows_of_slots, LANES), 0) * LANES
    slot = slot + lax.broadcasted_iota(i32, (rows_of_slots, LANES), 1)
    copies = []
    for step, pick in enumerate(steps):
        layer = layer_of(here, *pick)
        (place_a, start_a), (place_b, start_b) = spread[step]
        aux = tables[place_a][start_a : start_a + AUX_P, :].astype(f32)
        diagonal = [aux[i : i + 1] + aux[4 + i : 5 + i] + aux[8 + i : 9 + i] for i in range(BLOCKS)]
        inverse = [1.0 / line for line in diagonal]
        norm = (aux[15:16] + aux[16:17] + aux[17:18]) * rms_scale
        factor = jnp.sqrt(jnp.minimum(1.0, clip_limit / aux[12:13]))
        tallies = aux[13:14] + aux[14:15]

        def store(i, j, block):
            block = (block * inverse[j]).astype(bf16)
            mat_ref[step, i * LANES : (i + 1) * LANES, j * LANES : (j + 1) * LANES] = block

        for which, (place, start) in enumerate(((place_a, start_a + AUX_P), (place_b, start_b))):
            blocks = [
                tables[place][start + k * LANES : start + (k + 1) * LANES, :].astype(f32) for k in range(4)
            ]
            unpack_symmetric(which, blocks, lambda g: diagonal[g], store)
        lowest = dp * groups
        earlier = jnp.where((lane >= lowest) & (lane < here[2]), tallies, 0.0)
        base = jnp.sum(earlier, axis=1, keepdims=True).astype(i32) + dp * rows_block
        first_head = base >> head_shift
        row_index = base + slot
        head_of = row_index >> head_shift
        scale = jnp.ones(slot.shape, f32)
        for k in range((capacity - 1) // head_rows + 2):
            one = jnp.sum(jnp.where(lane == first_head + k, factor, 0.0), axis=1, keepdims=True)
            scale = jnp.where(head_of == first_head + k, one, scale)
        scale = jnp.where((row_index & (head_rows - 1)) < NOPE, scale, 1.0)
        count = jnp.sum(jnp.where(lane == here[2], tallies, 0.0), axis=1, keepdims=True).astype(i32)
        scale = jnp.where(slot < count, scale, 0.0)
        columns = [jnp.broadcast_to(scale[k : k + 1], (LANES, LANES)).T for k in range(slot.shape[0])]
        scale = jnp.concatenate(columns, axis=0)[:capacity]
        kept = scale * (1.0 - learn_rate * decay_rate)
        moved = scale * learn_rate
        source, index = places[step]
        if isinstance(index, tuple):
            core = here[1] if pick[1] else 1 - here[1]
            index = jnp.where(core == 0, index[0], index[1])
        for chunk in range(chunks):
            size = capacity // chunks
            among = slice(chunk * size, (chunk + 1) * size)
            product = mm(rows_in[source][index, among, :], mat_ref[step])
            for i in range(BLOCKS):
                span = slice(i * LANES, (i + 1) * LANES)
                update = product[:, span] * (diagonal[i] * norm)
                update_ref[step, among, span] = update.astype(bf16)
                weight = weight_ref[layer, among, span].astype(f32)
                new_ref[step, among, span] = (weight * kept[among] - update * moved[among]).astype(bf16)
            at = pl.ds(chunk * size, size)
            for number, (held, out) in enumerate(((update_ref, update_out), (new_ref, weight_out))):
                copy = pltpu.make_async_copy(
                    held.at[step, at], out.at[layer, at], leaving.at[number, step * chunks + chunk]
                )
                copy.start()
                copies.append(copy)
    for copy in copies:
        copy.wait()


def apply_rows(steps, spread, places, seats, tables, rows, weight, *outs):
    number = len(steps)
    layers, capacity, features = weight.shape
    vmem = pl.BlockSpec(memory_space=pltpu.VMEM)
    hbm = pl.BlockSpec(memory_space=pltpu.HBM)
    args = list(tables) + list(rows) + [weight] + list(outs)
    shape = jax.ShapeDtypeStruct((layers, capacity, features), bf16)
    return pl.pallas_call(
        functools.partial(apply_kernel, steps, spread, places, seats, (len(tables), len(rows))),
        in_specs=[vmem] * (len(tables) + len(rows) + 1) + [hbm] * len(outs),
        out_specs=[hbm, hbm],
        out_shape=[shape, shape],
        scratch_shapes=[
            pltpu.VMEM((number, KV_RANK, KV_RANK), bf16),
            pltpu.VMEM((number, capacity, features), bf16),
            pltpu.VMEM((number, capacity, features), bf16),
            pltpu.SemaphoreType.DMA((2, number * chunks_of(capacity))),
        ],
        input_output_aliases={len(args) - 2: 0, len(args) - 1: 1} if outs else {},
        compiler_params=params(),
        cost_estimate=SHORT,
        name="apply_rows",
    )(*args)


def local(dp_size, expert_size, grad_rows, momentum_rows, weight_rows, row_counts, logit_peaks):
    layers = grad_rows.shape[1]
    bits = owner_bits(expert_size)
    assert layers == expert_size == 2 << bits and bits >= 2
    assert dp_size == 4 and dp_size * expert_size <= LANES
    sources = (grad_rows[0], momentum_rows[0], row_counts.reshape(layers), logit_peaks[0, 0])

    def over(x, mask):
        everyone = range(dp_size * expert_size)
        return lax.ppermute(x, ("dp", "expert"), [(i, i ^ mask) for i in everyone])

    across_core = 1
    owner_masks = [2 << p for p in range(bits - 1)] + [2 * expert_size]
    copy_masks = [expert_size, expert_size // 2]

    def mask_of(relative):
        return sum(mask for p, mask in enumerate(owner_masks) if relative >> p & 1)

    def by_core(x, even, odd):
        everyone = range(dp_size * expert_size)
        return lax.ppermute(x, ("dp", "expert"), [(i, i ^ (odd if i & 1 else even)) for i in everyone])

    most = (1 << bits) - 1
    others = list(range(most - 1, 0, -1))
    turns = [
        [(most, False)],
        [(most, True)] + [(r, False) for r in others],
        [(r, True) for r in others],
        [(0, False), (0, True)],
    ]
    rows, partial, messages = {}, {}, []
    facts, loaded = None, ()
    message_shape = jax.ShapeDtypeStruct((1, 2 * HALF_CODE, LANES), i16)
    for number, turn in enumerate(turns):
        later = turns[number + 1][:2] if number + 1 < len(turns) else []
        if messages and not later:
            loaded, messages[0] = lax.optimization_barrier((loaded, messages[0]))
        facts, made, grams, loaded = gram_parts(expert_size, turn, later, sources, facts, loaded)
        for index, (pick, gram) in enumerate(zip(turn, grams)):
            rows[pick] = (made, index)
            partial[pick] = gram if pick[1] else [over(half, across_core) for half in gram]
        ready = ([], [most], others, [])[number]
        if ready:
            sums = [half for r in ready for half in partial[r, True] + partial[r, False]]
            kernel = functools.partial(send_kernel, len(ready))
            made = local_call(kernel, [message_shape] * len(ready), "send", *sums)
            made, loaded = lax.optimization_barrier((made, loaded))
            messages += [over(message, mask_of(r)) for r, message in zip(ready, made)]
    codes = jax.ShapeDtypeStruct((1, HALF_CODE, LANES), i16)
    shapes = [codes, codes, jax.ShapeDtypeStruct((1, 2 * HALF, LANES), f32)]
    out = local_call(gather_kernel, shapes, "gather", *partial[0, True], *partial[0, False], *messages)
    state = [out[2], over(out[0], copy_masks[0]), over(out[1], copy_masks[1])]
    out = local_call(sum_kernel, shapes, "sum", *state)
    state = [out[2], over(out[0], copy_masks[1]), over(out[1], copy_masks[0])]
    table = iterations(*state)

    seats = (expert_size, KV_ROWS // dp_size)
    weight = weight_rows[0]
    full = lambda place: ((place, 0), (place, HEAD_P))

    def apply(picks, tables, *outs):
        arrays, places = [], []
        for relative, own_core in picks:
            found = [rows[r, own_core] for r in (relative if isinstance(relative, tuple) else (relative,))]
            if not any(array is found[0][0] for array in arrays):
                arrays.append(found[0][0])
            (source,) = [k for k, array in enumerate(arrays) if array is found[0][0]]
            assert all(made is arrays[source] for made, _ in found)
            indices = tuple(index for _, index in found)
            places.append((source, indices if len(indices) > 1 else indices[0]))
        spread = tuple(full(k) for k in range(len(tables)))
        return apply_rows(tuple(picks), spread, places, seats, tables, arrays, weight, *outs)

    if bits == 2:
        first = by_core(table, owner_masks[1], owner_masks[0])
        second = by_core(table, owner_masks[0], owner_masks[1])
        outs = apply([(0, True)], [table])
        table, first, second, outs = lax.optimization_barrier((table, first, second, outs))
        last = by_core(second, owner_masks[1], owner_masks[0])
        near = [(2, 1), (1, 2)]
        outs = apply([(r, True) for r in near], [first, second], *outs)
        crossed = [over(x, across_core) for x in (table, first, second)]
        outs = apply([(r, False) for r in [0] + near], crossed, *outs)
        last, outs = lax.optimization_barrier((last, outs))
        outs = apply([(3, True)], [last], *outs)
        outs = apply([(3, False)], [over(last, across_core)], *outs)
    else:
        outs = apply(((0, True), (0, False)), [table, over(table, across_core)])
        tables = {0: table}
        for position in range(bits - 1, -1, -1):
            for known in list(tables):
                tables[known | 1 << position] = over(tables[known], owner_masks[position])
        for relative in range(1, 1 << bits):
            pair = [tables[relative], over(tables[relative], across_core)]
            outs = apply(((relative, True), (relative, False)), pair, *outs)
    return (outs[0][None], outs[1][None])


def solution(mesh):
    return jax.shard_map(
        functools.partial(local, mesh.shape["dp"], mesh.shape["expert"]),
        mesh=mesh,
        in_specs=(
            P("dp", None, "expert", None),
            P("dp", None, "expert", None),
            P("dp", None, "expert", None),
            P("dp", None, "expert"),
            P("dp", "expert", None, None),
        ),
        out_specs=(P("dp", None, "expert", None), P("dp", None, "expert", None)),
        check_vma=False,
    )
```

```python
import functools
import math

import jax
import jax.numpy as jnp
from jax import lax
from jax.experimental import pallas as pl
from jax.experimental.pallas import tpu as pltpu
from jax.sharding import PartitionSpec as P

KV_RANK = 512
NOPE = 128
VDIM = 128
NS_ITERS = 5
KV_ROWS = 16384

momentum_coef = 0.95
learn_rate = 0.02
decay_rate = 0.1
clip_limit = 100.0
coef_first = 3.4445
coef_second = -4.775
coef_third = 2.0315

f32 = jnp.float32
bf16 = jnp.bfloat16
i16 = jnp.int16
i32 = jnp.int32

LANES = 128
BLOCKS = KV_RANK // LANES
HALVES = (
    ((0, 1, True), (0, 1, False), (0, 2, False), (1, 2, False)),
    ((2, 3, True), (0, 3, False), (1, 3, False), (2, 3, False)),
)
AUX = 8
HALF = AUX + 4 * LANES
AUX_CODE = 16
HALF_CODE = AUX_CODE + 4 * LANES
AUX_P = 32
HEAD_P = AUX_P + 4 * LANES
ROWS_P = AUX_P + 8 * LANES
UNIT = 32000.0


def chunks_of(capacity):
    return 4 if capacity % 64 == 0 else 2 if capacity % 32 == 0 else 1


SHORT = pl.CostEstimate(flops=1000, bytes_accessed=1000, transcendentals=0)


def params(mebibytes=40):
    return pltpu.CompilerParams(vmem_limit_bytes=mebibytes * 1024 * 1024)


def pinned(x):
    return pltpu.with_memory_space_constraint(x, pltpu.HBM)


def square_iotas():
    row = lax.broadcasted_iota(i32, (LANES, LANES), 0)
    col = lax.broadcasted_iota(i32, (LANES, LANES), 1)
    return row, col


def owner_bits(expert_size):
    return expert_size.bit_length() - 2


def place_of(expert_size):
    bits = owner_bits(expert_size)
    dp = lax.axis_index("dp").astype(i32)
    expert = lax.axis_index("expert").astype(i32)
    owner = ((dp >> 1) << (bits - 1)) | ((expert >> 1) & ((1 << (bits - 1)) - 1))
    return owner, expert & 1, dp * expert_size + expert


def layer_of(place, relative, own_core):
    core = place[1] if own_core else 1 - place[1]
    if isinstance(relative, tuple):
        relative = jnp.where(core == 0, relative[0], relative[1])
    return 2 * (place[0] ^ relative) + core


def gram_kernel(expert_size, picks, later, first, where, *refs):
    refs = list(refs)
    take = lambda n: [refs.pop(0) for _ in range(n)]
    grad_ref, mom_ref = take(2)
    if first:
        counts_ref, peaks_ref = take(2)
    else:
        (facts_ref,) = take(1)
    given = [take(2) for _ in range(1 + max([spot[0] for spot in where if spot] + [-1]))]
    if first:
        (facts_ref,) = take(1)
    (nes_ref,) = take(1)
    gram_refs = take(2 * len(picks))
    loads = take(2 if later else 0)
    if first:
        counts, peaks_buf, small_arrivals = take(3)
    late_arrivals, own_arrivals, own_grad, own_mom = take(4)
    place = place_of(expert_size)
    layers = [layer_of(place, *pick) for pick in picks]

    def copies_of(chosen, buffers, semaphores):
        return [
            pltpu.make_async_copy(source.at[layer], buffer.at[k], semaphores.at[n, k])
            for k, layer in enumerate(chosen)
            for n, (source, buffer) in enumerate(((grad_ref, buffers[0]), (mom_ref, buffers[1])))
        ]

    own = [k for k, spot in enumerate(where) if not spot]
    own_copies = copies_of([layers[k] for k in own], (own_grad, own_mom), own_arrivals)
    small = []
    if first:
        small = [
            pltpu.make_async_copy(counts_ref, counts, small_arrivals.at[0]),
            pltpu.make_async_copy(peaks_ref, peaks_buf, small_arrivals.at[1]),
        ]
    late_copies = copies_of([layer_of(place, *pick) for pick in later], loads, late_arrivals) if later else []
    for copy in small + own_copies + late_copies:
        copy.start()
    row, col = square_iotas()
    line = lax.broadcasted_iota(i32, (AUX, LANES), 0)
    lane = lax.broadcasted_iota(i32, (AUX, LANES), 1)
    if first:
        for copy in small:
            copy.wait()
        every_peak = peaks_buf[...].astype(f32)
        every_peak = jnp.concatenate(
            [every_peak, jnp.zeros((every_peak.shape[0], LANES - every_peak.shape[1]), f32)], axis=1
        )
        for layer in range(every_peak.shape[0]):
            count = counts[layer].astype(f32)
            fact = jnp.where(line == 4, every_peak[layer : layer + 1], jnp.zeros((AUX, LANES), f32))
            fact = jnp.where((line == 6) | ((line == 5) & (lane == place[2])), count, fact)
            facts_ref[layer] = fact
    width = KV_RANK // 2
    dims = (((0,), (0,)), ((), ()))
    slot = lax.broadcasted_iota(i32, (nes_ref.shape[1], LANES), 0)

    def form_rows(k):
        if where[k]:
            (grad_buf, mom_buf), at = given[where[k][0]], where[k][1]
        else:
            (grad_buf, mom_buf), at = (own_grad, own_mom), own.index(k)
            for copy in own_copies[2 * at : 2 * at + 2]:
                copy.wait()
        live = slot < facts_ref[layers[k], 6:7, :].astype(i32)
        for i in range(BLOCKS):
            span = slice(i * LANES, (i + 1) * LANES)
            gradient = grad_buf[at, :, span].astype(f32)
            velocity = momentum_coef * mom_buf[at, :, span].astype(f32) + gradient
            nesterov = gradient + momentum_coef * velocity
            nes_ref[k, :, span] = jnp.where(live, nesterov, 0.0).astype(bf16)

    form_rows(0)
    for k, layer in enumerate(layers):
        if k + 1 < len(layers):
            form_rows(k + 1)
        rows = nes_ref[k]
        upper = lax.dot_general(rows[:, :width], rows, dims, preferred_element_type=f32)
        lower = lax.dot_general(rows[:, width:], rows[:, width:], dims, preferred_element_type=f32)

        def block(i, j):
            if i < 2:
                return upper[i * LANES : (i + 1) * LANES, j * LANES : (j + 1) * LANES]
            return lower[(i - 2) * LANES : (i - 1) * LANES, (j - 2) * LANES : (j - 1) * LANES]

        aux = jnp.where(line == 6, 0.0, facts_ref[layer])
        for i in range(BLOCKS):
            diagonal = jnp.sum(jnp.where(row == col, block(i, i), 0.0), axis=0, keepdims=True)
            aux = jnp.where(line == i, diagonal, aux)
        for which, entries in enumerate(HALVES):
            half = [aux]
            for i, j, triangle in entries:
                half.append(jnp.where(row <= col, block(i, i), block(j, j)) if triangle else block(i, j))
            store_half(gram_refs[2 * k + which], 0, half)
    for copy in late_copies:
        copy.wait()


def gram_parts(expert_size, picks, later, sources, facts, loaded):
    pairs, where = [], []
    for pick in picks:
        spot = None
        if pick in loaded:
            grad_rows, mom_rows, index = loaded[pick]
            if not any(pair[0] is grad_rows for pair in pairs):
                pairs.append((grad_rows, mom_rows))
            spot = [k for k, pair in enumerate(pairs) if pair[0] is grad_rows][0], index
        where.append(spot)
    grad, mom, counts, peaks = sources
    layers, capacity, features = grad.shape
    first = facts is None
    number = len(picks)
    vmem = pl.BlockSpec(memory_space=pltpu.VMEM)
    hbm = pl.BlockSpec(memory_space=pltpu.HBM)
    rows = lambda n: jax.ShapeDtypeStruct((n, capacity, features), bf16)
    out_shapes = [jax.ShapeDtypeStruct((layers, AUX, LANES), f32)] if first else []
    out_shapes += [rows(number)] + [jax.ShapeDtypeStruct((1, HALF, LANES), f32)] * (2 * number)
    out_shapes += [rows(len(later))] * 2 if later else []
    args = [pinned(grad), pinned(mom)]
    args += [pinned(counts), pinned(peaks)] if first else [facts]
    args += [array for pair in pairs for array in pair]
    own = max(where.count(None), 1)
    scratch = []
    if first:
        scratch += [pltpu.SMEM(counts.shape, i32), pltpu.VMEM(peaks.shape, bf16), pltpu.SemaphoreType.DMA((2,))]
    scratch += [pltpu.SemaphoreType.DMA((2, max(len(later), 1))), pltpu.SemaphoreType.DMA((2, own))]
    scratch += [pltpu.VMEM((own, capacity, features), bf16)] * 2
    out = pl.pallas_call(
        functools.partial(gram_kernel, expert_size, picks, later, first, where),
        in_specs=[hbm] * (4 if first else 2) + [vmem] * (0 if first else 1) + [vmem] * (2 * len(pairs)),
        out_specs=[vmem] * len(out_shapes),
        out_shape=out_shapes,
        scratch_shapes=scratch,
        compiler_params=params(),
        cost_estimate=SHORT,
        name="gram_parts",
    )(*args)
    if first:
        facts, out = out[0], out[1:]
    halves = [list(out[at : at + 2]) for at in range(1, 1 + 2 * number, 2)]
    loads = out[1 + 2 * number :]
    loaded = loaded | {pick: (loads[0], loads[1], k) for k, pick in enumerate(later)}
    return facts, out[0], halves, loaded


def joined(first, second):
    line = lax.broadcasted_iota(i32, (AUX, LANES), 0)
    aux = jnp.where(line == 4, jnp.maximum(first[0], second[0]), first[0] + second[0])
    return [aux] + [x + y for x, y in zip(first[1:], second[1:])]


def load_half(ref, index, base=0):
    starts = [base + AUX + place * LANES for place in range(4)]
    return [ref[index, base : base + AUX, :]] + [ref[index, at : at + LANES, :] for at in starts]


def store_half(ref, index, half, base=0):
    ref[index, base : base + AUX, :] = half[0]
    for place in range(4):
        at = base + AUX + place * LANES
        ref[index, at : at + LANES, :] = half[1 + place]


def outer_scales(which, scale):
    row, col = square_iotas()
    across = [scale[g : g + 1] for g in range(BLOCKS)]
    down = {}

    def outer(i, j):
        if i not in down:
            down[i] = jnp.broadcast_to(across[i], (LANES, LANES)).T
        return down[i] * across[j]

    return [
        jnp.where(row <= col, outer(i, i), outer(j, j)) if triangle else outer(i, j)
        for i, j, triangle in HALVES[which]
    ]


def decoded(which, ref, index, base=0):
    line = lax.broadcasted_iota(i32, (AUX, LANES), 0)
    codes = ref[index, base : base + AUX_CODE, :].astype(i32).astype(f32)
    low, high = codes[0:AUX], codes[AUX:AUX_CODE]
    scale = jnp.where(line < 4, jnp.exp2(low) * jnp.sqrt(high * (1.0 / UNIT)), 0.0)
    aux = jnp.where(line < 4, scale * scale, jnp.where(line == 4, low * (1.0 / 64.0), low))
    half = [aux]
    for place, factor in enumerate(outer_scales(which, scale)):
        at = base + AUX_CODE + place * LANES
        half.append(ref[index, at : at + LANES, :].astype(i32).astype(f32) * (factor * (1.0 / UNIT)))
    return half


def encode(which, ref, index, half, base=0):
    line = lax.broadcasted_iota(i32, (AUX, LANES), 0)
    aux = half[0]
    diagonal = jnp.maximum(aux, 1e-30)
    power = jnp.ceil(0.5 * jnp.log2(diagonal))
    high = jnp.clip(jnp.floor(diagonal * jnp.exp2(-2.0 * power) * UNIT + 0.5), 1.0, 32767.0)
    low = jnp.where(line < 4, power, jnp.where(line == 4, jnp.floor(aux * 64.0 + 0.5), aux))
    high = jnp.where(line < 4, high, 0.0)
    ref[index, base : base + AUX_CODE, :] = jnp.concatenate([low, high], axis=0).astype(i32).astype(i16)
    inverse = jnp.where(line < 4, jnp.exp2(-power) * lax.rsqrt(high * (1.0 / UNIT)), 0.0)
    for place, factor in enumerate(outer_scales(which, inverse)):
        at = base + AUX_CODE + place * LANES
        value = jnp.floor(half[1 + place] * (factor * UNIT) + 0.5)
        value = jnp.clip(value, -32767.0, 32767.0)
        ref[index, at : at + LANES, :] = value.astype(i32).astype(i16)


def local_call(kernel, out_shapes, name, *args):
    return pl.pallas_call(
        kernel,
        in_specs=[pl.BlockSpec(memory_space=pltpu.VMEM)] * len(args),
        out_specs=[pl.BlockSpec(memory_space=pltpu.VMEM)] * len(out_shapes),
        out_shape=list(out_shapes),
        compiler_params=params(),
        cost_estimate=SHORT,
        name=name,
    )(*args)


def send_kernel(number, *refs):
    for k in range(number):
        own, partner, message = refs[4 * k : 4 * k + 2], refs[4 * k + 2 : 4 * k + 4], refs[4 * number + k]
        for which in range(2):
            half = joined(load_half(own[which], 0), load_half(partner[which], 0))
            encode(which, message, 0, half, which * HALF_CODE)


def gather_kernel(*refs):
    messages, outs, stay = refs[4:-3], refs[-3:-1], refs[-1]
    for which in range(2):
        half = joined(load_half(refs[which], 0), load_half(refs[2 + which], 0))
        for arrived in messages:
            half = joined(half, decoded(which, arrived, 0, which * HALF_CODE))
        encode(which, outs[which], 0, half)
        store_half(stay, 0, half, which * HALF)


def sum_kernel(kept, arrived_a, arrived_b, *refs):
    outs, stay = refs[:2], refs[2]
    for which, arrived in enumerate((arrived_a, arrived_b)):
        half = joined(load_half(kept, 0, which * HALF), decoded(which, arrived, 0))
        encode(which, outs[which], 0, half)
        store_half(stay, 0, half, which * HALF)


def mm(x, y):
    return jnp.dot(x, y, preferred_element_type=f32)


def unpack_symmetric(which, blocks, diagonal, store):
    row, col = square_iotas()
    for (i, j, triangle), block in zip(HALVES[which], blocks):
        other = block.T
        if triangle:
            first = jnp.where(row < col, block, other)
            second = jnp.where(row > col, block, other)
            store(i, i, jnp.where(row == col, diagonal(i), first))
            store(j, j, jnp.where(row == col, diagonal(j), second))
        else:
            store(i, j, block)
            store(j, i, other)


def iterate_kernel(kept, arrived_a, arrived_b, out_ref, gram_ref):
    row, col = square_iotas()

    def store(i, j, block):
        gram_ref[i * LANES : (i + 1) * LANES, j * LANES : (j + 1) * LANES] = block

    aux = None
    for which, arrived in enumerate((arrived_a, arrived_b)):
        half = joined(load_half(kept, 0, which * HALF), decoded(which, arrived, 0))
        if aux is None:
            aux = half[0]
        unpack_symmetric(which, half[1:], lambda g: aux[g : g + 1], store)
    line = lax.broadcasted_iota(i32, (AUX, LANES), 0)
    squares = jnp.sum(jnp.where(line < 4, aux, 0.0), axis=0, keepdims=True)
    squares = jnp.sum(squares, axis=1, keepdims=True)
    inverse = 1.0 / (jnp.sqrt(squares) + 1e-07)
    gram = gram_ref[...] * inverse * inverse
    full_row = lax.broadcasted_iota(i32, (KV_RANK, KV_RANK), 0)
    full_col = lax.broadcasted_iota(i32, (KV_RANK, KV_RANK), 1)
    on_diagonal = full_row == full_col
    def diagonal_of(x):
        return jnp.sum(jnp.where(on_diagonal, x, 0.0), axis=0, keepdims=True)

    def rest_of(x):
        return jnp.where(on_diagonal, 0.0, x).astype(bf16)

    product = None
    for repeat in range(NS_ITERS):
        diagonal = diagonal_of(gram)
        columns = [diagonal[:, i * LANES : (i + 1) * LANES] for i in range(BLOCKS)]
        down = jnp.concatenate([jnp.broadcast_to(one, (LANES, LANES)).T for one in columns], axis=0)
        down = jnp.concatenate([down] * BLOCKS, axis=1)
        rest = rest_of(gram)
        square = mm(rest, rest) + jnp.where(on_diagonal, diagonal * diagonal, gram * (down + diagonal))
        mixing = (coef_second * gram + coef_third * square).astype(bf16)
        mixing_wide = mixing.astype(f32)
        if product is None:
            product = jnp.where(on_diagonal, coef_first, 0.0) + mixing_wide
        else:
            moved = mm(mixing, rest_of(product)) + mixing_wide * diagonal_of(product)
            product = coef_first * product + moved
        if repeat < NS_ITERS - 1:
            half = coef_first * gram + (mm(rest, mixing) + mixing_wide * down)
            gram = coef_first * half + (mm(mixing, rest_of(half)) + mixing_wide * diagonal_of(half))
    gram_ref[...] = product
    at = AUX_P
    for entries in HALVES:
        for i, j, triangle in entries:
            load = lambda i, j: gram_ref[i * LANES : (i + 1) * LANES, j * LANES : (j + 1) * LANES]
            if triangle:
                block = jnp.where(row <= col, load(i, i), load(j, j))
                block = 0.5 * (block + jnp.where(row <= col, load(i, i).T, load(j, j).T))
            else:
                block = 0.5 * (load(i, j) + load(j, i).T)
            out_ref[at : at + LANES, :] = block.astype(bf16)
            at += LANES

    def three(x):
        high = x.astype(bf16).astype(f32)
        middle = (x - high).astype(bf16).astype(f32)
        return high, middle, x - high - middle

    lines = [[], [], []]
    for i in range(BLOCKS):
        block = gram_ref[i * LANES : (i + 1) * LANES, i * LANES : (i + 1) * LANES]
        diagonal = jnp.sum(jnp.where(row == col, block, 0.0), axis=0, keepdims=True)
        for lines_of, part in zip(lines, three(diagonal)):
            lines_of.append(part)
    peaks = aux[4:5]
    tallies = aux[5:6]
    tally_high = tallies.astype(bf16).astype(f32)
    norm = three(jnp.broadcast_to(inverse, (1, LANES)))
    stacked = lines[0] + lines[1] + lines[2] + [peaks, tally_high, tallies - tally_high] + list(norm)
    place = lax.broadcasted_iota(i32, (AUX_P, LANES), 0)
    table = jnp.zeros((AUX_P, LANES), f32)
    for number, one in enumerate(stacked):
        table = jnp.where(place == number, one, table)
    out_ref[0:AUX_P, :] = table.astype(bf16)


def iterations(*args):
    return pl.pallas_call(
        iterate_kernel,
        in_specs=[pl.BlockSpec(memory_space=pltpu.VMEM)] * 3,
        out_specs=pl.BlockSpec(memory_space=pltpu.VMEM),
        out_shape=jax.ShapeDtypeStruct((ROWS_P, LANES), bf16),
        scratch_shapes=[pltpu.VMEM((KV_RANK, KV_RANK), f32)],
        compiler_params=params(),
        cost_estimate=SHORT,
        name="iterations",
    )(*args)


def apply_kernel(steps, spread, places, seats, number_of, *refs):
    tables = refs[: number_of[0]]
    rows_in = refs[number_of[0] : sum(number_of)]
    weight_ref = refs[sum(number_of)]
    update_out, weight_out, mat_ref, update_ref, new_ref, leaving = refs[-6:]
    groups, rows_block = seats
    here = place_of(groups)
    dp = lax.axis_index("dp").astype(i32)
    capacity = weight_ref.shape[1]
    head_rows = NOPE + VDIM
    rms_scale = 0.2 * math.sqrt(max(KV_ROWS, KV_RANK))
    lane = lax.broadcasted_iota(i32, (1, LANES), 1)
    head_shift = head_rows.bit_length() - 1
    chunks = chunks_of(capacity)
    assert head_rows == 1 << head_shift and capacity % (16 * chunks) == 0
    rows_of_slots = -(-capacity // LANES)
    slot = lax.broadcasted_iota(i32, (rows_of_slots, LANES), 0) * LANES
    slot = slot + lax.broadcasted_iota(i32, (rows_of_slots, LANES), 1)
    copies = []
    for step, pick in enumerate(steps):
        layer = layer_of(here, *pick)
        (place_a, start_a), (place_b, start_b) = spread[step]
        aux = tables[place_a][start_a : start_a + AUX_P, :].astype(f32)
        diagonal = [aux[i : i + 1] + aux[4 + i : 5 + i] + aux[8 + i : 9 + i] for i in range(BLOCKS)]
        inverse = [1.0 / line for line in diagonal]
        norm = (aux[15:16] + aux[16:17] + aux[17:18]) * rms_scale
        factor = jnp.sqrt(jnp.minimum(1.0, clip_limit / aux[12:13]))
        tallies = aux[13:14] + aux[14:15]

        def store(i, j, block):
            block = (block * inverse[j]).astype(bf16)
            mat_ref[step, i * LANES : (i + 1) * LANES, j * LANES : (j + 1) * LANES] = block

        for which, (place, start) in enumerate(((place_a, start_a + AUX_P), (place_b, start_b))):
            blocks = [
                tables[place][start + k * LANES : start + (k + 1) * LANES, :].astype(f32) for k in range(4)
            ]
            unpack_symmetric(which, blocks, lambda g: diagonal[g], store)
        lowest = dp * groups
        earlier = jnp.where((lane >= lowest) & (lane < here[2]), tallies, 0.0)
        base = jnp.sum(earlier, axis=1, keepdims=True).astype(i32) + dp * rows_block
        first_head = base >> head_shift
        row_index = base + slot
        head_of = row_index >> head_shift
        scale = jnp.ones(slot.shape, f32)
        for k in range((capacity - 1) // head_rows + 2):
            one = jnp.sum(jnp.where(lane == first_head + k, factor, 0.0), axis=1, keepdims=True)
            scale = jnp.where(head_of == first_head + k, one, scale)
        scale = jnp.where((row_index & (head_rows - 1)) < NOPE, scale, 1.0)
        count = jnp.sum(jnp.where(lane == here[2], tallies, 0.0), axis=1, keepdims=True).astype(i32)
        scale = jnp.where(slot < count, scale, 0.0)
        columns = [jnp.broadcast_to(scale[k : k + 1], (LANES, LANES)).T for k in range(slot.shape[0])]
        scale = jnp.concatenate(columns, axis=0)[:capacity]
        kept = scale * (1.0 - learn_rate * decay_rate)
        moved = scale * learn_rate
        source, index = places[step]
        if isinstance(index, tuple):
            core = here[1] if pick[1] else 1 - here[1]
            index = jnp.where(core == 0, index[0], index[1])
        for chunk in range(chunks):
            size = capacity // chunks
            among = slice(chunk * size, (chunk + 1) * size)
            product = mm(rows_in[source][index, among, :], mat_ref[step])
            for i in range(BLOCKS):
                span = slice(i * LANES, (i + 1) * LANES)
                update = product[:, span] * (diagonal[i] * norm)
                update_ref[step, among, span] = update.astype(bf16)
                weight = weight_ref[layer, among, span].astype(f32)
                new_ref[step, among, span] = (weight * kept[among] - update * moved[among]).astype(bf16)
            at = pl.ds(chunk * size, size)
            for number, (held, out) in enumerate(((update_ref, update_out), (new_ref, weight_out))):
                copy = pltpu.make_async_copy(
                    held.at[step, at], out.at[layer, at], leaving.at[number, step * chunks + chunk]
                )
                copy.start()
                copies.append(copy)
    for copy in copies:
        copy.wait()


def apply_rows(steps, spread, places, seats, tables, rows, weight, *outs):
    number = len(steps)
    layers, capacity, features = weight.shape
    vmem = pl.BlockSpec(memory_space=pltpu.VMEM)
    hbm = pl.BlockSpec(memory_space=pltpu.HBM)
    args = list(tables) + list(rows) + [weight] + list(outs)
    shape = jax.ShapeDtypeStruct((layers, capacity, features), bf16)
    return pl.pallas_call(
        functools.partial(apply_kernel, steps, spread, places, seats, (len(tables), len(rows))),
        in_specs=[vmem] * (len(tables) + len(rows) + 1) + [hbm] * len(outs),
        out_specs=[hbm, hbm],
        out_shape=[shape, shape],
        scratch_shapes=[
            pltpu.VMEM((number, KV_RANK, KV_RANK), bf16),
            pltpu.VMEM((number, capacity, features), bf16),
            pltpu.VMEM((number, capacity, features), bf16),
            pltpu.SemaphoreType.DMA((2, number * chunks_of(capacity))),
        ],
        input_output_aliases={len(args) - 2: 0, len(args) - 1: 1} if outs else {},
        compiler_params=params(),
        cost_estimate=SHORT,
        name="apply_rows",
    )(*args)


def local(dp_size, expert_size, grad_rows, momentum_rows, weight_rows, row_counts, logit_peaks):
    layers = grad_rows.shape[1]
    bits = owner_bits(expert_size)
    assert layers == expert_size == 2 << bits and bits >= 2
    assert dp_size == 4 and dp_size * expert_size <= LANES
    sources = (grad_rows[0], momentum_rows[0], row_counts.reshape(layers), logit_peaks[0, 0])

    def over(x, mask):
        everyone = range(dp_size * expert_size)
        return lax.ppermute(x, ("dp", "expert"), [(i, i ^ mask) for i in everyone])

    across_core = 1
    owner_masks = [2 << p for p in range(bits - 1)] + [2 * expert_size]
    copy_masks = [expert_size, expert_size // 2]

    def mask_of(relative):
        return sum(mask for p, mask in enumerate(owner_masks) if relative >> p & 1)

    def by_core(x, even, odd):
        everyone = range(dp_size * expert_size)
        return lax.ppermute(x, ("dp", "expert"), [(i, i ^ (odd if i & 1 else even)) for i in everyone])

    most = (1 << bits) - 1
    others = list(range(most - 1, 0, -1))
    turns = [
        [(most, False)],
        [(most, True)],
        [(r, False) for r in others],
        [(r, True) for r in others],
        [(0, False), (0, True)],
    ]
    ahead = [turns[1] + turns[2][:1], turns[2][1:2], turns[3][:2], turns[4], []]
    rows, partial, messages = {}, {}, []
    facts, loaded = None, {}
    message_shape = jax.ShapeDtypeStruct((1, 2 * HALF_CODE, LANES), i16)

    def after(loaded, arrays):
        kept = []
        for first_array, second_array, _ in loaded.values():
            if not any(first_array is pair[0] for pair in kept):
                kept.append((first_array, second_array))
        held, arrays = lax.optimization_barrier((kept, arrays))
        number_of = lambda array: [k for k, pair in enumerate(kept) if pair[0] is array][0]
        return {pick: (*held[number_of(g)], index) for pick, (g, _, index) in loaded.items()}, arrays

    for number, turn in enumerate(turns):
        facts, made, grams, loaded = gram_parts(expert_size, turn, ahead[number], sources, facts, loaded)
        for index, (pick, gram) in enumerate(zip(turn, grams)):
            rows[pick] = (made, index)
            partial[pick] = gram if pick[1] else [over(half, across_core) for half in gram]
        ready = ([], [most], [], others, [])[number]
        if ready:
            sums = [half for r in ready for half in partial[r, True] + partial[r, False]]
            if messages:
                sums, messages[0] = lax.optimization_barrier((sums, messages[0]))
            kernel = functools.partial(send_kernel, len(ready))
            made = local_call(kernel, [message_shape] * len(ready), "send", *sums)
            loaded, made = after(loaded, made)
            messages += [over(message, mask_of(r)) for r, message in zip(ready, made)]
    codes = jax.ShapeDtypeStruct((1, HALF_CODE, LANES), i16)
    shapes = [codes, codes, jax.ShapeDtypeStruct((1, 2 * HALF, LANES), f32)]
    out = local_call(gather_kernel, shapes, "gather", *partial[0, True], *partial[0, False], *messages)
    state = [out[2], over(out[0], copy_masks[0]), over(out[1], copy_masks[1])]
    out = local_call(sum_kernel, shapes, "sum", *state)
    state = [out[2], over(out[0], copy_masks[1]), over(out[1], copy_masks[0])]
    table = iterations(*state)

    seats = (expert_size, KV_ROWS // dp_size)
    weight = weight_rows[0]
    full = lambda place: ((place, 0), (place, HEAD_P))

    def apply(picks, tables, *outs):
        arrays, places = [], []
        for relative, own_core in picks:
            found = [rows[r, own_core] for r in (relative if isinstance(relative, tuple) else (relative,))]
            if not any(array is found[0][0] for array in arrays):
                arrays.append(found[0][0])
            (source,) = [k for k, array in enumerate(arrays) if array is found[0][0]]
            assert all(made is arrays[source] for made, _ in found)
            indices = tuple(index for _, index in found)
            places.append((source, indices if len(indices) > 1 else indices[0]))
        spread = tuple(full(k) for k in range(len(tables)))
        return apply_rows(tuple(picks), spread, places, seats, tables, arrays, weight, *outs)

    if bits == 2:
        first = by_core(table, owner_masks[1], owner_masks[0])
        second = by_core(table, owner_masks[0], owner_masks[1])
        outs = apply([(0, True)], [table])
        table, first, second, outs = lax.optimization_barrier((table, first, second, outs))
        last = by_core(second, owner_masks[1], owner_masks[0])
        near = [(2, 1), (1, 2)]
        outs = apply([(r, True) for r in near], [first, second], *outs)
        crossed = [over(x, across_core) for x in (table, first, second)]
        outs = apply([(r, False) for r in [0] + near], crossed, *outs)
        last, outs = lax.optimization_barrier((last, outs))
        outs = apply([(3, True)], [last], *outs)
        outs = apply([(3, False)], [over(last, across_core)], *outs)
    else:
        outs = apply(((0, True), (0, False)), [table, over(table, across_core)])
        tables = {0: table}
        for position in range(bits - 1, -1, -1):
            for known in list(tables):
                tables[known | 1 << position] = over(tables[known], owner_masks[position])
        for relative in range(1, 1 << bits):
            pair = [tables[relative], over(tables[relative], across_core)]
            outs = apply(((relative, True), (relative, False)), pair, *outs)
    return (outs[0][None], outs[1][None])


def solution(mesh):
    return jax.shard_map(
        functools.partial(local, mesh.shape["dp"], mesh.shape["expert"]),
        mesh=mesh,
        in_specs=(
            P("dp", None, "expert", None),
            P("dp", None, "expert", None),
            P("dp", None, "expert", None),
            P("dp", None, "expert"),
            P("dp", "expert", None, None),
        ),
        out_specs=(P("dp", None, "expert", None), P("dp", None, "expert", None)),
        check_vma=False,
    )
```
